32 devices in a mesh: dp: 4 (over y, x), ctx: 8 (over z, core).
Axes of the slice: x: 2, y: 2, z: 4, core: 2. Of those that a mesh axis runs over, the one named last changes fastest.
Arguments:
- q_rows: bfloat16 [4, 2048, 8192], P('dp', 'ctx'), may hold values from -16 to 16
- k_rows: bfloat16 [4, 2048, 1024], P('dp', 'ctx'), may hold values from -16 to 16
- value_slot_rows: bfloat16 [4, 2048, 1024], P('dp', 'ctx'), may hold values from -6 to 6
- counts: int32 [4, 8], P('dp', 'ctx'), may hold values from 0 to 256, as said below
- doc_ids: int32 [4, 1024], P('dp', 'ctx'), may hold values from 0 to 2, never falling along the last dimension, each value on 1 to 512 neighbouring positions
Outputs:
- attended: bfloat16 [4, 1024, 8192], P('dp', 'ctx')
The draws below stay inside these ranges and needn't reach their ends.
Inputs may be any that keep to these rules, and one draw needn't show every extreme that they name: In every column c and for every replica r, the sum of counts of replicas 0 to r exceeds (r + 1) * 128 by 0 to 128, and by 0 for the last replica. In every column some replica's count is 256 and the next replica's is 0. `doc_ids`: along each window the ids never fall; each id covers 1 to 512 positions, one exactly that many.
All inputs are finite; a program needn't handle non-finite values.
Results may differ from the reference program's by a relative error of at most 0.0038.
Values may be sent and summed in bfloat16 or wider, within the bound.
No kernel may reach another device: no remote copies, remote signals or barrier semaphores. Data moves between devices by JAX's collectives and lax.ppermute only.
A program may use at most 64 MiB of HBM per device.

```python
import math
import jax
import jax.numpy as jnp
import numpy as np
from jax import lax

QUERY_HEADS = 64
KEY_VALUE_HEADS = 8
HEAD_SIZE = 128
QUOTA = 128
DOCS = 3
SLOT_LIMIT = 256
WINDOW_SPAN = 1024
N_DP = 4
N_CTX = 8


def count_table(key):
    key = jax.random.fold_in(key, 11)
    first, latter_part = jax.random.split(key)
    extra = jax.random.randint(first, (N_DP, N_CTX), 0, QUOTA + 1)
    chosen = jax.random.randint(latter_part, (1, N_CTX), 1, N_DP - 1)
    places = jnp.arange(N_DP, dtype=jnp.int32)[:, None]
    extra = jnp.where(places == chosen - 1, 0, extra)
    extra = jnp.where(places == chosen, QUOTA, extra)
    extra = jnp.where(places == chosen + 1, 0, extra)
    extra = jnp.where(places == N_DP - 1, 0, extra)
    earlier = jnp.concatenate([jnp.zeros((1, N_CTX), jnp.int32), extra[:-1]], axis=0)
    return (QUOTA + extra - earlier).astype(jnp.int32)


def draw_counts(key, part):
    return count_table(key)


def draw_q_rows(key, part):
    key = jax.random.fold_in(key, 5)
    tensor_dims = (N_DP, N_CTX, SLOT_LIMIT, KEY_VALUE_HEADS, QUERY_HEADS // KEY_VALUE_HEADS, HEAD_SIZE)
    value_tensor = jnp.clip(jax.random.normal(key, tensor_dims), -6.0, 6.0)
    return value_tensor.reshape(N_DP, N_CTX * SLOT_LIMIT, QUERY_HEADS * HEAD_SIZE).astype(jnp.bfloat16)


def draw_k_rows(key, part):
    key = jax.random.fold_in(key, 7)
    tensor_dims = (N_DP, N_CTX, SLOT_LIMIT, KEY_VALUE_HEADS, HEAD_SIZE)
    value_tensor = jnp.clip(jax.random.normal(key, tensor_dims), -6.0, 6.0)
    return value_tensor.reshape(N_DP, N_CTX * SLOT_LIMIT, KEY_VALUE_HEADS * HEAD_SIZE).astype(jnp.bfloat16)


def block_levels(rng, extent, shards, smallest, high):
    gain = 1.0
    for dim, shards_of in shards:
        draws = jax.random.uniform(jax.random.fold_in(jax.random.fold_in(rng, 6), dim), (shards_of,), jnp.float32, smallest / len(shards), high / len(shards))
        gain = gain * jnp.repeat(jnp.exp(draws), extent[dim] // shards_of).reshape((-1,) + (1,) * (len(extent) - 1 - dim))
    return gain


def profile(number_of, total, limit, slope):
    portions = [(1 << 20) // math.isqrt(grade ** slope) + 1 for grade in range(2, number_of + 1)]
    rest, given = total - limit - (number_of - 1), [1] * (number_of - 1)
    while rest > 0:
        movable = [i for i in range(number_of - 1) if given[i] < limit]
        pool, remaining = sum([portions[i] for i in movable]), rest
        for i in movable:
            addition = min(limit - given[i], max(1, remaining * portions[i] // pool), rest)
            given[i] = given[i] + addition
            rest = rest - addition
    return np.array([limit] + given)


def uneven(own_key, amount, total, most, skew):
    if amount == 2:
        one = jax.random.randint(own_key, (), max(1, total - most), min(most, total - 1) + 1)
        return jnp.stack([one, total - one])
    lengths = jnp.asarray(profile(amount, total, most, skew), jnp.int32)
    twos = (amount - 1) // 2
    giver, taker = lengths[1:1 + 2 * twos:2], lengths[2:2 + 2 * twos:2]
    margin = jnp.minimum(giver - 1, most - taker)
    moved = jax.random.randint(jax.random.fold_in(own_key, 1), (twos,), 0, 1 << 20) % (margin + 1)
    lengths = lengths.at[1:1 + 2 * twos:2].set(giver - moved).at[2:2 + 2 * twos:2].set(taker + moved)
    return lengths[jax.random.permutation(jax.random.fold_in(own_key, 2), amount)]


def noise(rng, extent, scale, limit, cuts=(), held_as=jnp.bfloat16):
    factor_of = block_levels(rng, extent, cuts, -0.22, 0.18) if cuts else 1.0
    array = jax.random.normal(rng, extent, jnp.float32) * scale * factor_of
    return jnp.minimum(jnp.maximum(array, -limit), limit).astype(held_as)


def setup_inputs(seed: int = 0) -> dict:
    keys = jax.random.split(jax.random.key(seed), 6)
    q_rows = draw_q_rows(jax.random.fold_in(keys[5], 71), 0)
    k_rows = draw_k_rows(jax.random.fold_in(keys[5], 71), 0)
    value_slot_rows = noise(keys[2], (N_DP, N_CTX * SLOT_LIMIT, KEY_VALUE_HEADS * HEAD_SIZE), 1.0, 6.0, ((0, 4), (1, 8)))
    counts = draw_counts(jax.random.fold_in(keys[5], 71), 0)
    doc_ids = jax.vmap(lambda own: jnp.searchsorted(jnp.cumsum(uneven(own, DOCS, WINDOW_SPAN, WINDOW_SPAN // 2, 2)), jnp.arange(WINDOW_SPAN), side="right"))(jax.random.split(keys[4], N_DP)).reshape((N_DP, WINDOW_SPAN)).astype(jnp.int32)
    return {"q_rows": q_rows, "k_rows": k_rows, "value_slot_rows": value_slot_rows, "counts": counts, "doc_ids": doc_ids}


def balance(source_rows, counts):
    inclusive = jnp.cumsum(counts, axis=0).astype(jnp.int32)
    starting = (inclusive - counts).astype(jnp.int32)
    targets = jnp.arange(N_DP * QUOTA, dtype=jnp.int32)
    owners = lax.optimization_barrier(jnp.sum((inclusive[None, :, :] <= targets[:, None, None]).astype(jnp.int32), axis=1)).astype(jnp.int32)
    columns = jnp.arange(N_CTX, dtype=jnp.int32)[None, :]
    offsets = (targets[:, None] - starting[owners, columns]).astype(jnp.int32)
    picked = source_rows[owners, columns * SLOT_LIMIT + offsets]
    width = source_rows.shape[2]
    picked = picked.reshape(N_DP, QUOTA, N_CTX, width).transpose(0, 2, 1, 3)
    return picked.reshape(N_DP, N_CTX * QUOTA, width)

def attend(query_tensor, key_tensor, value_tensor, doc_row):
    query_per_key_head = QUERY_HEADS // KEY_VALUE_HEADS
    score_scale = 1.0 / math.sqrt(HEAD_SIZE)
    query_head_split = query_tensor.astype(jnp.float32).reshape(WINDOW_SPAN, KEY_VALUE_HEADS, query_per_key_head, HEAD_SIZE).transpose(1, 2, 0, 3)
    key_head_split = key_tensor.astype(jnp.float32).reshape(WINDOW_SPAN, KEY_VALUE_HEADS, HEAD_SIZE).transpose(1, 0, 2)
    value_head_split = value_tensor.astype(jnp.float32).reshape(WINDOW_SPAN, KEY_VALUE_HEADS, HEAD_SIZE).transpose(1, 0, 2)
    places = jnp.arange(WINDOW_SPAN, dtype=jnp.int32)
    allowed = (places[None, :] <= places[:, None]) & (doc_row[None, :] == doc_row[:, None])

    def per_group(operands):
        q_group = operands[0]
        k_group = operands[1]
        v_group = operands[2]
        scores = jnp.einsum('gpd,td->gpt', q_group, k_group) * score_scale
        scores = jnp.where(allowed[None], scores, -jnp.inf)
        largest = lax.optimization_barrier(jnp.max(scores, axis=-1, keepdims=True))
        weights = jnp.exp(scores - largest)
        totals = lax.optimization_barrier(jnp.sum(weights, axis=-1, keepdims=True))
        rounded = lax.optimization_barrier(weights.astype(jnp.bfloat16)).astype(jnp.float32)
        mixed = jnp.einsum('gpt,td->gpd', rounded, v_group) / totals
        return mixed.astype(jnp.bfloat16)
    heads_out = lax.map(per_group, (query_head_split, key_head_split, value_head_split))
    return heads_out.transpose(2, 0, 1, 3).reshape(WINDOW_SPAN, QUERY_HEADS * HEAD_SIZE)

def reference(q_rows, k_rows, value_slot_rows, counts, doc_ids):
    balanced_q = balance(q_rows, counts)
    levelled_key_rows = balance(k_rows, counts)
    levelled_value_rows = balance(value_slot_rows, counts)

    def per_window(operands):
        return attend(operands[0], operands[1], operands[2], operands[3])
    return lax.map(per_window, (balanced_q, levelled_key_rows, levelled_value_rows, doc_ids))
```

```python
import functools
import math

import jax
import jax.numpy as jnp
from jax import lax
from jax.experimental import pallas as pl
from jax.experimental.pallas import tpu as pltpu
from jax.sharding import PartitionSpec as P

QUERY_HEADS = 64
KEY_VALUE_HEADS = 8
HEAD_SIZE = 128
GROUP = QUERY_HEADS // KEY_VALUE_HEADS
GROUP_WIDTH = GROUP * HEAD_SIZE
KV_WIDTH = KEY_VALUE_HEADS * HEAD_SIZE
MASKED = -1e30
CHUNKS = (2, 2, 2, 1, 1)


def shifted(x, axis, steps):
    n = lax.axis_size(axis)
    return lax.ppermute(x, axis, [(i, i + steps) for i in range(n - steps)])


def swapped_cores(x):
    n = lax.axis_size("ctx")
    return lax.ppermute(x, "ctx", [(i, i ^ 1) for i in range(n)])


def everyones(x, axis):
    n = lax.axis_size(axis)
    spread = jnp.broadcast_to(x[None], (n,) + x.shape)
    return lax.all_to_all(spread, axis, split_axis=0, concat_axis=0)


def placing(scal_ref, quota):
    s, s_before = scal_ref[0], scal_ref[1]
    row = lax.broadcasted_iota(jnp.int32, (quota, 2 * quota), 0)
    col = lax.broadcasted_iota(jnp.int32, (quota, 2 * quota), 1)
    turned = row - s_before
    turned = jnp.where(turned < 0, turned + quota, turned)
    source = jnp.where(row < s, turned, row - s + quota)
    return jnp.where(col == source, 1.0, 0.0).astype(jnp.bfloat16)


def place_rows(hot, arrived, local):
    both = jnp.concatenate([arrived, local], axis=0)
    return jnp.dot(hot, both, preferred_element_type=jnp.float32).astype(jnp.bfloat16)


def settle_kernel(scal_ref, arrived_ref, k_ref, v_ref, out_ref):
    quota = out_ref.shape[0]
    hot = placing(scal_ref, quota)
    out_ref[:, :KV_WIDTH] = place_rows(hot, arrived_ref[:, :KV_WIDTH], k_ref[0])
    out_ref[:, KV_WIDTH:] = place_rows(hot, arrived_ref[:, KV_WIDTH:], v_ref[0])


def settle_kv(scal, arrived, k_rows, v_rows):
    quota = arrived.shape[0]
    half = pl.BlockSpec((1, quota, KV_WIDTH), lambda i: (0, 0, 0))
    whole = pl.BlockSpec((quota, 2 * KV_WIDTH), lambda i: (0, 0))
    return pl.pallas_call(
        settle_kernel,
        grid=(1,),
        in_specs=[pl.BlockSpec(memory_space=pltpu.SMEM), whole, half, half],
        out_specs=whole,
        out_shape=jax.ShapeDtypeStruct(arrived.shape, jnp.bfloat16),
        name="settle_kv",
    )(scal, arrived, k_rows, v_rows)


def attend_kernel(blocks, has_out, scal_ref, bias_ref, arrived_ref, local_ref, *refs):
    k_refs, v_refs = refs[:blocks], refs[blocks : 2 * blocks]
    out_ref = refs[-1]
    quota = arrived_ref.shape[0]
    hot = placing(scal_ref, quota)
    q = place_rows(hot, arrived_ref[...], local_ref[0])
    keys = jnp.concatenate([r[...] for r in k_refs], axis=0)
    values = jnp.concatenate([r[...] for r in v_refs], axis=0)
    unit = math.log2(math.e) / math.sqrt(HEAD_SIZE)
    for head in range(GROUP):
        cols = slice(head * HEAD_SIZE, (head + 1) * HEAD_SIZE)
        scores = lax.dot_general(
            q[:, cols], keys, (((1,), (1,)), ((), ())), preferred_element_type=jnp.float32
        )
        scores = scores * unit + bias_ref[...]
        weights = jnp.exp2(scores - jnp.max(scores, axis=1, keepdims=True))
        totals = jnp.sum(weights, axis=1, keepdims=True)
        mixed = jnp.dot(weights.astype(jnp.bfloat16), values, preferred_element_type=jnp.float32)
        out_ref[0, :, cols] = (mixed / totals).astype(jnp.bfloat16)


def attend(scal, bias, arrived, q_rows, kv_blocks, first, count, out):
    quota = arrived.shape[0]
    blocks = len(kv_blocks)
    k_spec = pl.BlockSpec((quota, HEAD_SIZE), lambda g: (0, first + g))
    v_spec = pl.BlockSpec((quota, HEAD_SIZE), lambda g: (0, KEY_VALUE_HEADS + first + g))
    in_specs = [
        pl.BlockSpec(memory_space=pltpu.SMEM),
        pl.BlockSpec(bias.shape, lambda g: (0, 0)),
        pl.BlockSpec((quota, GROUP_WIDTH), lambda g: (0, g)),
        pl.BlockSpec((1, quota, GROUP_WIDTH), lambda g: (0, 0, first + g)),
    ]
    in_specs += [k_spec] * blocks + [v_spec] * blocks
    operands = [scal, bias, arrived, q_rows, *kv_blocks, *kv_blocks]
    aliases = {}
    if out is not None:
        in_specs.append(pl.BlockSpec(memory_space=pl.ANY))
        aliases = {len(operands): 0}
        operands.append(out)
    pairs = count * GROUP * quota * quota * blocks
    return pl.pallas_call(
        functools.partial(attend_kernel, blocks, out is not None),
        grid=(count,),
        in_specs=in_specs,
        out_specs=pl.BlockSpec((1, quota, GROUP_WIDTH), lambda g: (0, 0, first + g)),
        out_shape=jax.ShapeDtypeStruct((1, quota, QUERY_HEADS * HEAD_SIZE), jnp.bfloat16),
        input_output_aliases=aliases,
        cost_estimate=pl.CostEstimate(
            flops=4 * pairs * HEAD_SIZE,
            bytes_accessed=count * quota * (3 * GROUP_WIDTH + 2 * blocks * HEAD_SIZE) * 2,
            transcendentals=pairs,
        ),
        compiler_params=pltpu.CompilerParams(vmem_limit_bytes=32 * 1024 * 1024),
        name="attend_heads",
    )(*operands)


def circular_tail(rows, own_count, quota):
    later = (quota + jnp.arange(quota, dtype=jnp.int32) < own_count)[:, None]
    return jnp.where(later, rows[quota:], rows[:quota])


def body(q_rows, k_rows, value_slot_rows, counts, doc_ids):
    quota = doc_ids.shape[1]
    n_ctx = lax.axis_size("ctx")
    rounds = n_ctx // 4
    replica, rank = lax.axis_index("dp"), lax.axis_index("ctx")
    core = rank % 2
    own_count = counts[0, 0]

    kv_tail = jnp.concatenate(
        [
            circular_tail(k_rows[0], own_count, quota),
            circular_tail(value_slot_rows[0], own_count, quota),
        ],
        axis=1,
    )
    arrived_kv = shifted(kv_tail, "dp", 1)

    all_counts = everyones(counts[0], "dp")[:, 0]
    window_docs = everyones(doc_ids[0], "ctx").reshape(-1)

    places = jnp.arange(lax.axis_size("dp"), dtype=jnp.int32)
    before = jnp.sum(jnp.where(places < replica, all_counts, 0))
    before_last = jnp.sum(jnp.where(places < replica - 1, all_counts, 0))
    shift_in = before - replica * quota
    shift_before = jnp.where(replica > 0, before_last - (replica - 1) * quota, 0)
    scal = jnp.stack([shift_in, shift_before]).astype(jnp.int32)

    ranks = [rank]
    for back in range(1, rounds + 1):
        ranks.append(rank - 2 * back)
        if back < rounds:
            ranks.append(rank - 2 * back + jnp.where(core == 0, 1, -1))
    ranks.append(jnp.where(core == 0, rank - 2 * rounds + 1, rank - 1))
    key_places = (
        jnp.stack(ranks)[:, None] * quota + jnp.arange(quota, dtype=jnp.int32)[None, :]
    ).reshape(1, -1)
    own_places = rank * quota + jnp.arange(quota, dtype=jnp.int32)[:, None]
    doc_start = jnp.sum(
        (window_docs[None, :] < doc_ids[0][:, None]).astype(jnp.int32), axis=1, keepdims=True
    )
    allowed = (key_places <= own_places) & (key_places >= doc_start)
    bias = jnp.where(allowed, 0.0, MASKED).astype(jnp.float32)

    own = settle_kv(scal, arrived_kv, k_rows, value_slot_rows)

    arrived_q = []
    first = 0
    for size in CHUNKS:
        cols = slice(first * GROUP_WIDTH, (first + size) * GROUP_WIDTH)
        tail = circular_tail(q_rows[0, :, cols], own_count, quota)
        arrived_q.append(shifted(tail, "dp", 1))
        first += size

    kv_blocks = [own]
    carried = own
    for back in range(1, rounds + 1):
        carried = shifted(carried, "ctx", 2)
        kv_blocks.append(carried)
        if back < rounds:
            kv_blocks.append(swapped_cores(carried))
    kv_blocks.append(swapped_cores(jnp.where(core == 0, own, carried)))

    out = None
    first = 0
    for size, arrived in zip(CHUNKS, arrived_q):
        out = attend(scal, bias, arrived, q_rows, kv_blocks, first, size, out)
        first += size
    return out


def solution(mesh):
    return jax.shard_map(
        body,
        mesh=mesh,
        in_specs=(
            P("dp", "ctx", None),
            P("dp", "ctx", None),
            P("dp", "ctx", None),
            P("dp", "ctx"),
            P("dp", "ctx"),
        ),
        out_specs=P("dp", "ctx", None),
        check_vma=False,
    )
```

```python
import functools
import math

import jax
import jax.numpy as jnp
from jax import lax
from jax.experimental import pallas as pl
from jax.experimental.pallas import tpu as pltpu
from jax.sharding import PartitionSpec as P

QUERY_HEADS = 64
KEY_VALUE_HEADS = 8
HEAD_SIZE = 128
GROUP = QUERY_HEADS // KEY_VALUE_HEADS
GROUP_WIDTH = GROUP * HEAD_SIZE
KV_WIDTH = KEY_VALUE_HEADS * HEAD_SIZE
MASKED = -1e30
CHUNKS = (1, 3, 2, 2)
PARTS = 2


def shifted(x, axis, steps):
    n = lax.axis_size(axis)
    return lax.ppermute(x, axis, [(i, i + steps) for i in range(n - steps)])


def swapped_cores(x):
    n = lax.axis_size("ctx")
    return lax.ppermute(x, "ctx", [(i, i ^ 1) for i in range(n)])


def everyones(x, axis):
    n = lax.axis_size(axis)
    spread = jnp.broadcast_to(x[None], (n,) + x.shape)
    return lax.all_to_all(spread, axis, split_axis=0, concat_axis=0)


def placing(scal_ref, quota):
    s, s_before = scal_ref[0], scal_ref[1]
    row = lax.broadcasted_iota(jnp.int32, (quota, 2 * quota), 0)
    col = lax.broadcasted_iota(jnp.int32, (quota, 2 * quota), 1)
    turned = row - s_before
    turned = jnp.where(turned < 0, turned + quota, turned)
    source = jnp.where(row < s, turned, row - s + quota)
    return jnp.where(col == source, 1.0, 0.0).astype(jnp.bfloat16)


def place_rows(hot, arrived, local):
    both = jnp.concatenate([arrived, local], axis=0)
    return jnp.dot(hot, both, preferred_element_type=jnp.float32).astype(jnp.bfloat16)


def settle_kernel(scal_ref, arrived_ref, k_ref, v_ref, out_ref):
    quota = out_ref.shape[0]
    hot = placing(scal_ref, quota)
    out_ref[:, :KV_WIDTH] = place_rows(hot, arrived_ref[:, :KV_WIDTH], k_ref[0])
    out_ref[:, KV_WIDTH:] = place_rows(hot, arrived_ref[:, KV_WIDTH:], v_ref[0])


def settle_kv(scal, arrived, k_rows, v_rows):
    quota = arrived.shape[0]
    half = pl.BlockSpec((1, quota, KV_WIDTH), lambda i: (0, 0, 0))
    whole = pl.BlockSpec((quota, 2 * KV_WIDTH), lambda i: (0, 0))
    return pl.pallas_call(
        settle_kernel,
        grid=(1,),
        in_specs=[pl.BlockSpec(memory_space=pltpu.SMEM), whole, half, half],
        out_specs=whole,
        out_shape=jax.ShapeDtypeStruct(arrived.shape, jnp.bfloat16),
        name="settle_kv",
    )(scal, arrived, k_rows, v_rows)


def attend_kernel(blocks, scal_ref, bias_ref, arrived_ref, local_ref, *refs):
    k_refs, v_refs = refs[:blocks], refs[blocks : 2 * blocks]
    out_ref = refs[-1]
    quota = arrived_ref.shape[0]
    hot = placing(scal_ref, quota)
    q = place_rows(hot, arrived_ref[...], local_ref[0])
    keys = jnp.concatenate([r[...] for r in k_refs], axis=0)
    values = jnp.concatenate([r[...] for r in v_refs], axis=0)
    values = jnp.concatenate([values, jnp.ones_like(values)], axis=1)
    unit = math.log2(math.e) / math.sqrt(HEAD_SIZE)
    heads = GROUP // PARTS

    def scored(part):
        stacked = jnp.concatenate(
            [
                q[:, h * HEAD_SIZE : (h + 1) * HEAD_SIZE]
                for h in range(part * heads, (part + 1) * heads)
            ],
            axis=0,
        )
        return lax.dot_general(
            stacked, keys, (((1,), (1,)), ((), ())), preferred_element_type=jnp.float32
        )

    def finished(part, scores):
        scores = scores.reshape(heads, quota, -1) * unit + bias_ref[...][None]
        weights = jnp.exp2(scores - jnp.max(scores, axis=2, keepdims=True))
        weights = weights.astype(jnp.bfloat16).reshape(heads * quota, -1)
        mixed = jnp.dot(weights, values, preferred_element_type=jnp.float32)
        mixed = (mixed[:, :HEAD_SIZE] / mixed[:, HEAD_SIZE:]).astype(jnp.bfloat16)
        for h in range(heads):
            at = (part * heads + h) * HEAD_SIZE
            out_ref[0, :, at : at + HEAD_SIZE] = mixed[h * quota : (h + 1) * quota]

    scores = scored(0)
    for part in range(PARTS):
        later = scored(part + 1) if part + 1 < PARTS else None
        finished(part, scores)
        scores = later


def attend(scal, bias, arrived, q_rows, kv_blocks, first, count, out):
    quota = arrived.shape[0]
    blocks = len(kv_blocks)
    k_spec = pl.BlockSpec((quota, HEAD_SIZE), lambda g: (0, first + g))
    v_spec = pl.BlockSpec((quota, HEAD_SIZE), lambda g: (0, KEY_VALUE_HEADS + first + g))
    in_specs = [
        pl.BlockSpec(memory_space=pltpu.SMEM),
        pl.BlockSpec(bias.shape, lambda g: (0, 0)),
        pl.BlockSpec((quota, GROUP_WIDTH), lambda g: (0, g)),
        pl.BlockSpec((1, quota, GROUP_WIDTH), lambda g: (0, 0, first + g)),
    ]
    in_specs += [k_spec] * blocks + [v_spec] * blocks
    operands = [scal, bias, arrived, q_rows, *kv_blocks, *kv_blocks]
    aliases = {}
    if out is not None:
        in_specs.append(pl.BlockSpec(memory_space=pl.ANY))
        aliases = {len(operands): 0}
        operands.append(out)
    pairs = count * GROUP * quota * quota * blocks
    return pl.pallas_call(
        functools.partial(attend_kernel, blocks),
        grid=(count,),
        in_specs=in_specs,
        out_specs=pl.BlockSpec((1, quota, GROUP_WIDTH), lambda g: (0, 0, first + g)),
        out_shape=jax.ShapeDtypeStruct((1, quota, QUERY_HEADS * HEAD_SIZE), jnp.bfloat16),
        input_output_aliases=aliases,
        cost_estimate=pl.CostEstimate(
            flops=4 * pairs * HEAD_SIZE,
            bytes_accessed=count * quota * (3 * GROUP_WIDTH + 2 * blocks * HEAD_SIZE) * 2,
            transcendentals=pairs,
        ),
        compiler_params=pltpu.CompilerParams(vmem_limit_bytes=32 * 1024 * 1024),
        name="attend_heads",
    )(*operands)


def circular_tail(rows, later):
    quota = later.shape[0]
    return jnp.where(later[:, None], rows[quota:], rows[:quota])


def body(q_rows, k_rows, value_slot_rows, counts, doc_ids):
    quota = doc_ids.shape[1]
    n_ctx = lax.axis_size("ctx")
    rounds = n_ctx // 4
    replica, rank = lax.axis_index("dp"), lax.axis_index("ctx")
    core = rank % 2
    own_count = counts[0, 0]

    all_counts = everyones(counts[0], "dp")[:, 0]
    later = quota + jnp.arange(quota, dtype=jnp.int32) < own_count
    kv_tail = jnp.concatenate(
        [
            circular_tail(k_rows[0], later),
            circular_tail(value_slot_rows[0], later),
        ],
        axis=1,
    )
    kv_tail, later = lax.optimization_barrier((kv_tail, later))
    arrived_kv = shifted(kv_tail, "dp", 1)
    q_tails = []
    first = 0
    for size in CHUNKS:
        cols = slice(first * GROUP_WIDTH, (first + size) * GROUP_WIDTH)
        q_tails.append(circular_tail(q_rows[0, :, cols], later))
        first += size
    arrived_q = [shifted(tail, "dp", 1) for tail in q_tails]

    window_docs = everyones(doc_ids[0], "ctx").reshape(-1)

    places = jnp.arange(lax.axis_size("dp"), dtype=jnp.int32)
    before = jnp.sum(jnp.where(places < replica, all_counts, 0))
    before_last = jnp.sum(jnp.where(places < replica - 1, all_counts, 0))
    shift_in = before - replica * quota
    shift_before = jnp.where(replica > 0, before_last - (replica - 1) * quota, 0)
    scal = jnp.stack([shift_in, shift_before]).astype(jnp.int32)

    ranks = [rank]
    for back in range(1, rounds + 1):
        ranks.append(rank - 2 * back)
        if back < rounds:
            ranks.append(rank - 2 * back + jnp.where(core == 0, 1, -1))
    ranks.append(jnp.where(core == 0, rank - 2 * rounds + 1, rank - 1))
    key_places = (
        jnp.stack(ranks)[:, None] * quota + jnp.arange(quota, dtype=jnp.int32)[None, :]
    ).reshape(1, -1)
    own_places = rank * quota + jnp.arange(quota, dtype=jnp.int32)[:, None]
    doc_start = jnp.sum(
        (window_docs[None, :] < doc_ids[0][:, None]).astype(jnp.int32), axis=1, keepdims=True
    )
    allowed = (key_places <= own_places) & (key_places >= doc_start)
    bias = jnp.where(allowed, 0.0, MASKED).astype(jnp.float32)

    own = settle_kv(scal, arrived_kv, k_rows, value_slot_rows)
    own, arrived_q[0] = lax.optimization_barrier((own, arrived_q[0]))

    kv_blocks = [own]
    carried = own
    for back in range(1, rounds + 1):
        carried = shifted(carried, "ctx", 2)
        kv_blocks.append(carried)
        if back < min(rounds + 1, len(CHUNKS)):
            carried, arrived_q[back] = lax.optimization_barrier((carried, arrived_q[back]))
        if back < rounds:
            kv_blocks.append(swapped_cores(carried))
    kv_blocks.append(swapped_cores(jnp.where(core == 0, own, carried)))

    out = None
    first = 0
    for size, arrived in zip(CHUNKS, arrived_q):
        out = attend(scal, bias, arrived, q_rows, kv_blocks, first, size, out)
        first += size
    return out


def solution(mesh):
    return jax.shard_map(
        body,
        mesh=mesh,
        in_specs=(
            P("dp", "ctx", None),
            P("dp", "ctx", None),
            P("dp", "ctx", None),
            P("dp", "ctx"),
            P("dp", "ctx"),
        ),
        out_specs=P("dp", "ctx", None),
        check_vma=False,
    )
```

```python
import functools
import math

import jax
import jax.numpy as jnp
from jax import lax
from jax.experimental import pallas as pl
from jax.experimental.pallas import tpu as pltpu
from jax.sharding import PartitionSpec as P

QUERY_HEADS = 64
KEY_VALUE_HEADS = 8
HEAD_SIZE = 128
GROUP = QUERY_HEADS // KEY_VALUE_HEADS
GROUP_WIDTH = GROUP * HEAD_SIZE
KV_WIDTH = KEY_VALUE_HEADS * HEAD_SIZE
NOTE = 2 * KV_WIDTH
MASKED = -1e30
CHUNKS = (3, 3, 2)
PARTS = 2

WHOLE = pl.BlockSpec(memory_space=pltpu.VMEM)
SCALARS = pl.BlockSpec(memory_space=pltpu.SMEM)


def shifted(x, axis, steps):
    n = lax.axis_size(axis)
    return lax.ppermute(x, axis, [(i, i + steps) for i in range(n - steps)])


def swapped_cores(x):
    n = lax.axis_size("ctx")
    return lax.ppermute(x, "ctx", [(i, i ^ 1) for i in range(n)])


def everyones(x, axis):
    n = lax.axis_size(axis)
    spread = jnp.broadcast_to(x[None], (n,) + x.shape)
    return lax.all_to_all(spread, axis, split_axis=0, concat_axis=0)


def shift_in_known(own_count, quota):
    n = lax.axis_size("dp")
    replica = lax.axis_index("dp")
    if n > 4:
        all_counts = everyones(own_count[None], "dp")[:, 0]
        places = jnp.arange(n, dtype=jnp.int32)
        before = jnp.sum(jnp.where(places < replica, all_counts, 0))
        return jnp.stack([before - replica * quota, jnp.int32(0)])
    shift = jnp.where(own_count == 0, quota, 0)
    shift = jnp.where(replica == n - 1, quota - own_count, shift)
    shift = jnp.where(replica == 0, 0, shift)
    return jnp.stack([shift, (replica == 1).astype(jnp.int32)])


def place_rows(hot, arrived, local):
    both = jnp.concatenate([arrived, local], axis=0)
    return jnp.dot(hot, both, preferred_element_type=jnp.float32).astype(jnp.bfloat16)


def settle_kernel(shift_ref, docs_ref, arrived_ref, k_ref, v_ref, out_ref, hot_ref):
    quota = out_ref.shape[0]
    count_before = arrived_ref[:, NOTE:].astype(jnp.float32).astype(jnp.int32)
    shift = jnp.where(shift_ref[1] == 1, count_before - quota, shift_ref[0])
    shift_before = shift - count_before + quota
    row = lax.broadcasted_iota(jnp.int32, (quota, quota), 0)
    col = lax.broadcasted_iota(jnp.int32, (quota, quota), 1)
    turned = row - shift_before
    turned = jnp.where(turned < 0, turned + quota, turned)
    hot_arrived = jnp.where((row < shift) & (col == turned), 1.0, 0.0)
    hot_local = jnp.where(col == row - shift, 1.0, 0.0)
    hot = jnp.concatenate([hot_arrived, hot_local], axis=1).astype(jnp.bfloat16)
    hot_ref[...] = hot
    out_ref[:, :KV_WIDTH] = place_rows(hot, arrived_ref[:, :KV_WIDTH], k_ref[0])
    out_ref[:, KV_WIDTH:NOTE] = place_rows(hot, arrived_ref[:, KV_WIDTH:NOTE], v_ref[0])
    docs = jnp.broadcast_to(docs_ref[...].astype(jnp.float32), (quota, quota))
    out_ref[:, NOTE:] = docs.astype(jnp.bfloat16)


def settle_kv(shift, docs, arrived, k_rows, v_rows):
    quota = arrived.shape[0]
    half = pl.BlockSpec((1, quota, KV_WIDTH), lambda i: (0, 0, 0))
    whole = pl.BlockSpec(arrived.shape, lambda i: (0, 0))
    return pl.pallas_call(
        settle_kernel,
        grid=(1,),
        in_specs=[SCALARS, pl.BlockSpec(docs.shape, lambda i: (0, 0)), whole, half, half],
        out_specs=[whole, pl.BlockSpec((quota, 2 * quota), lambda i: (0, 0))],
        out_shape=[
            jax.ShapeDtypeStruct(arrived.shape, jnp.bfloat16),
            jax.ShapeDtypeStruct((quota, 2 * quota), jnp.bfloat16),
        ],
        name="settle_kv",
    )(shift, docs, arrived, k_rows, v_rows)


def block_ranks(rank, core, rounds):
    ranks = [rank]
    for back in range(1, rounds + 1):
        ranks.append(rank - 2 * back)
        if back < rounds:
            ranks.append(rank - 2 * back + jnp.where(core == 0, 1, -1))
    ranks.append(jnp.where(core == 0, rank - 2 * rounds + 1, rank - 1))
    return ranks


def attend_kernel(blocks, first, count, rank_ref, hot_ref, arrived_ref, *refs):
    kv_refs, q_hbm = refs[:blocks], refs[blocks]
    out_hbm, local, result, bias, q_sem, out_sems = refs[-6:]
    quota = hot_ref.shape[0]
    width = count * GROUP_WIDTH
    start = first * GROUP_WIDTH
    fetch = pltpu.make_async_copy(q_hbm.at[0, 0:quota, start : start + width], local, q_sem)
    fetch.start()

    rank = rank_ref[0]
    row = lax.broadcasted_iota(jnp.int32, (quota, quota), 0)
    col = lax.broadcasted_iota(jnp.int32, (quota, quota), 1)
    own_docs = kv_refs[0][:, NOTE:].astype(jnp.float32)
    q_docs = jnp.sum(jnp.where(row == col, own_docs, 0.0), axis=1, keepdims=True)
    for b, block_rank in enumerate(block_ranks(rank, lax.rem(rank, 2), (blocks - 1) // 2)):
        allowed = kv_refs[b][:, NOTE:].astype(jnp.float32) == q_docs
        allowed &= (col <= row) if b == 0 else (block_rank >= 0)
        bias[:, b * quota : (b + 1) * quota] = jnp.where(allowed, 0.0, MASKED)

    unit = math.log2(math.e) / math.sqrt(HEAD_SIZE)
    heads = GROUP // PARTS
    hot = hot_ref[...]

    def operands(g):
        at = (first + g) * HEAD_SIZE
        keys = jnp.concatenate([r[:, at : at + HEAD_SIZE] for r in kv_refs], axis=0)
        at += KV_WIDTH
        values = jnp.concatenate([r[:, at : at + HEAD_SIZE] for r in kv_refs], axis=0)
        values = jnp.concatenate([values, jnp.ones_like(values)], axis=1)
        cols = slice(g * GROUP_WIDTH, (g + 1) * GROUP_WIDTH)
        q = place_rows(hot, arrived_ref[:, cols], local[:, cols])
        return q, keys, values

    def scored(q, keys, part):
        stacked = jnp.concatenate(
            [
                q[:, h * HEAD_SIZE : (h + 1) * HEAD_SIZE]
                for h in range(part * heads, (part + 1) * heads)
            ],
            axis=0,
        )
        return lax.dot_general(
            stacked, keys, (((1,), (1,)), ((), ())), preferred_element_type=jnp.float32
        )

    def finished(scores, values, g, part):
        scores = scores.reshape(heads, quota, -1) * unit + bias[...][None]
        weights = jnp.exp2(scores - jnp.max(scores, axis=2, keepdims=True))
        weights = weights.astype(jnp.bfloat16).reshape(heads * quota, -1)
        mixed = jnp.dot(weights, values, preferred_element_type=jnp.float32)
        mixed = (mixed[:, :HEAD_SIZE] / mixed[:, HEAD_SIZE:]).astype(jnp.bfloat16)
        for h in range(heads):
            at = g * GROUP_WIDTH + (part * heads + h) * HEAD_SIZE
            result[:, at : at + HEAD_SIZE] = mixed[h * quota : (h + 1) * quota]

    fetch.wait()
    stores = []
    q, keys, values = operands(0)
    scores = scored(q, keys, 0)
    for step in range(count * PARTS):
        g, part = divmod(step, PARTS)
        own_values, later = values, None
        if step + 1 < count * PARTS:
            if part == PARTS - 1:
                q, keys, values = operands(g + 1)
            later = scored(q, keys, (part + 1) % PARTS)
        finished(scores, own_values, g, part)
        scores = later
        if part == PARTS - 1:
            cols = slice(g * GROUP_WIDTH, (g + 1) * GROUP_WIDTH)
            at = (first + g) * GROUP_WIDTH
            store = pltpu.make_async_copy(
                result.at[:, cols], out_hbm.at[0, :, at : at + GROUP_WIDTH], out_sems.at[g]
            )
            store.start()
            stores.append(store)
    for store in stores:
        store.wait()


def attend(rank, hot, arrived, q_rows, kv_blocks, first, count, out):
    quota = arrived.shape[0]
    blocks = len(kv_blocks)
    width = count * GROUP_WIDTH
    anywhere = pl.BlockSpec(memory_space=pl.ANY)
    in_specs = [SCALARS, WHOLE, WHOLE] + [WHOLE] * blocks + [anywhere]
    operands = [rank, hot, arrived, *kv_blocks, q_rows]
    aliases = {}
    if out is not None:
        in_specs.append(anywhere)
        aliases = {len(operands): 0}
        operands.append(out)
    pairs = count * GROUP * quota * quota * blocks
    return pl.pallas_call(
        functools.partial(attend_kernel, blocks, first, count),
        in_specs=in_specs,
        out_specs=anywhere,
        out_shape=jax.ShapeDtypeStruct((1, quota, QUERY_HEADS * HEAD_SIZE), jnp.bfloat16),
        input_output_aliases=aliases,
        scratch_shapes=[
            pltpu.VMEM((quota, width), jnp.bfloat16),
            pltpu.VMEM((quota, width), jnp.bfloat16),
            pltpu.VMEM((quota, blocks * quota), jnp.float32),
            pltpu.SemaphoreType.DMA,
            pltpu.SemaphoreType.DMA((count,)),
        ],
        cost_estimate=pl.CostEstimate(
            flops=4 * pairs * HEAD_SIZE,
            bytes_accessed=count * quota * (3 * GROUP_WIDTH + 2 * blocks * HEAD_SIZE) * 2,
            transcendentals=pairs,
        ),
        compiler_params=pltpu.CompilerParams(vmem_limit_bytes=24 * 1024 * 1024),
        name="attend_heads",
    )(*operands)


def circular_tail(rows, later):
    quota = later.shape[0]
    return jnp.where(later[:, None], rows[quota:], rows[:quota])


def body(q_rows, k_rows, value_slot_rows, counts, doc_ids):
    quota = doc_ids.shape[1]
    rounds = lax.axis_size("ctx") // 4
    rank = lax.axis_index("ctx")
    own_count = counts[0, 0]

    later = quota + jnp.arange(quota, dtype=jnp.int32) < own_count
    kv_tail = jnp.concatenate(
        [
            circular_tail(k_rows[0], later),
            circular_tail(value_slot_rows[0], later),
            jnp.broadcast_to(own_count.astype(jnp.bfloat16), (quota, quota)),
        ],
        axis=1,
    )
    kv_tail, later = lax.optimization_barrier((kv_tail, later))
    arrived_kv = shifted(kv_tail, "dp", 1)
    arrived_q = []
    first = 0
    for size in CHUNKS:
        cols = slice(first * GROUP_WIDTH, (first + size) * GROUP_WIDTH)
        arrived_q.append(shifted(circular_tail(q_rows[0, :, cols], later), "dp", 1))
        first += size

    shift = shift_in_known(own_count, quota)
    own, hot = settle_kv(shift, doc_ids, arrived_kv, k_rows, value_slot_rows)

    kv_blocks = [own]
    carried = own
    for back in range(1, rounds + 1):
        carried = shifted(carried, "ctx", 2)
        kv_blocks.append(carried)
        if back <= min(rounds, len(CHUNKS) - 1):
            carried, arrived_q[back - 1] = lax.optimization_barrier((carried, arrived_q[back - 1]))
        if back < rounds:
            kv_blocks.append(swapped_cores(carried))
    kv_blocks.append(swapped_cores(jnp.where(rank % 2 == 0, own, carried)))

    out = None
    first = 0
    for size, arrived in zip(CHUNKS, arrived_q):
        out = attend(rank[None], hot, arrived, q_rows, kv_blocks, first, size, out)
        first += size
    return out


def solution(mesh):
    return jax.shard_map(
        body,
        mesh=mesh,
        in_specs=(
            P("dp", "ctx", None),
            P("dp", "ctx", None),
            P("dp", "ctx", None),
            P("dp", "ctx"),
            P("dp", "ctx"),
        ),
        out_specs=P("dp", "ctx", None),
        check_vma=False,
    )
```

```python
import functools
import math

import jax
import jax.numpy as jnp
from jax import lax
from jax.experimental import pallas as pl
from jax.experimental.pallas import tpu as pltpu
from jax.sharding import PartitionSpec as P

QUERY_HEADS = 64
KEY_VALUE_HEADS = 8
HEAD_SIZE = 128
GROUP = QUERY_HEADS // KEY_VALUE_HEADS
GROUP_WIDTH = GROUP * HEAD_SIZE
KV_WIDTH = KEY_VALUE_HEADS * HEAD_SIZE
NOTE = 2 * KV_WIDTH
MASKED = -1e30
CHUNKS = (2, 3, 3)
PARTS = 2

WHOLE = pl.BlockSpec(memory_space=pltpu.VMEM)
SCALARS = pl.BlockSpec(memory_space=pltpu.SMEM)


def shifted(x, axis, steps):
    n = lax.axis_size(axis)
    return lax.ppermute(x, axis, [(i, i + steps) for i in range(n - steps)])


def across_cores(x, sources=(0, 1)):
    n = lax.axis_size("ctx")
    return lax.ppermute(x, "ctx", [(i, i ^ 1) for i in range(n) if i % 2 in sources])


def everyones(x, axis):
    n = lax.axis_size(axis)
    spread = jnp.broadcast_to(x[None], (n,) + x.shape)
    return lax.all_to_all(spread, axis, split_axis=0, concat_axis=0)


def shift_in_known(own_count, quota):
    n = lax.axis_size("dp")
    replica = lax.axis_index("dp")
    if n > 4:
        all_counts = everyones(own_count[None], "dp")[:, 0]
        places = jnp.arange(n, dtype=jnp.int32)
        before = jnp.sum(jnp.where(places < replica, all_counts, 0))
        return jnp.stack([before - replica * quota, jnp.int32(0)])
    shift = jnp.where(own_count == 0, quota, 0)
    shift = jnp.where(replica == n - 1, quota - own_count, shift)
    shift = jnp.where(replica == 0, 0, shift)
    return jnp.stack([shift, (replica == 1).astype(jnp.int32)])


def place_rows(hot, arrived, local):
    both = jnp.concatenate([arrived, local], axis=0)
    return jnp.dot(hot, both, preferred_element_type=jnp.float32).astype(jnp.bfloat16)


def settle_kernel(shift_ref, docs_ref, arrived_ref, local_ref, out_ref, hot_ref):
    quota = out_ref.shape[0]
    count_before = arrived_ref[:, NOTE:].astype(jnp.float32).astype(jnp.int32)
    shift = jnp.where(shift_ref[1] == 1, count_before - quota, shift_ref[0])
    shift_before = shift - count_before + quota
    row = lax.broadcasted_iota(jnp.int32, (quota, quota), 0)
    col = lax.broadcasted_iota(jnp.int32, (quota, quota), 1)
    turned = row - shift_before
    turned = jnp.where(turned < 0, turned + quota, turned)
    hot_arrived = jnp.where((row < shift) & (col == turned), 1.0, 0.0)
    hot_local = jnp.where(col == row - shift, 1.0, 0.0)
    hot = jnp.concatenate([hot_arrived, hot_local], axis=1).astype(jnp.bfloat16)
    hot_ref[...] = hot
    out_ref[:, :NOTE] = place_rows(hot, arrived_ref[:, :NOTE], local_ref[...])
    docs = jnp.broadcast_to(docs_ref[...].astype(jnp.float32), (quota, quota))
    out_ref[:, NOTE:] = docs.astype(jnp.bfloat16)


def settle_kv(shift, docs, arrived, local):
    quota = arrived.shape[0]
    return pl.pallas_call(
        settle_kernel,
        in_specs=[SCALARS, WHOLE, WHOLE, WHOLE],
        out_specs=[WHOLE, WHOLE],
        out_shape=[
            jax.ShapeDtypeStruct(arrived.shape, jnp.bfloat16),
            jax.ShapeDtypeStruct((quota, 2 * quota), jnp.bfloat16),
        ],
        compiler_params=pltpu.CompilerParams(vmem_limit_bytes=24 * 1024 * 1024),
        name="settle_kv",
    )(shift, docs, arrived, local)


def block_ranks(rank, core, rounds):
    ranks = [rank]
    for back in range(1, rounds + 1):
        ranks.append(rank - 2 * back)
        if back < rounds:
            ranks.append(rank - 2 * back + jnp.where(core == 0, 1, -1))
    ranks.append(jnp.where(core == 0, rank - 2 * rounds + 1, rank - 1))
    return ranks


def attend_kernel(blocks, first, count, rank_ref, hot_ref, arrived_ref, *refs):
    kv_refs, far_ref, mate_ref, q_hbm = refs[: blocks - 1], *refs[blocks - 1 : blocks + 2]
    out_hbm, local, result, bias, rest, q_sem, out_sems = refs[-7:]
    quota = hot_ref.shape[0]
    width = count * GROUP_WIDTH
    start = first * GROUP_WIDTH
    fetch = pltpu.make_async_copy(q_hbm.at[0, 0:quota, start : start + width], local, q_sem)
    fetch.start()

    rank = rank_ref[0]
    core = lax.rem(rank, 2)
    parts = [(first + part) * HEAD_SIZE for part in (0, KEY_VALUE_HEADS)]
    spans = [slice(at, at + count * HEAD_SIZE) for at in parts] + [slice(NOTE, NOTE + quota)]

    @pl.when(core == 0)
    def _():
        for span in spans:
            rest[:, span] = far_ref[:, span]

    @pl.when(core == 1)
    def _():
        for span in spans:
            rest[:, span] = mate_ref[:, span]

    kv_refs = [*kv_refs, rest]
    row = lax.broadcasted_iota(jnp.int32, (quota, quota), 0)
    col = lax.broadcasted_iota(jnp.int32, (quota, quota), 1)
    own_docs = kv_refs[0][:, NOTE:].astype(jnp.float32)
    q_docs = jnp.sum(jnp.where(row == col, own_docs, 0.0), axis=1, keepdims=True)
    for b, block_rank in enumerate(block_ranks(rank, core, (blocks - 1) // 2)):
        allowed = kv_refs[b][:, NOTE:].astype(jnp.float32) == q_docs
        allowed &= (col <= row) if b == 0 else (block_rank >= 0)
        bias[:, b * quota : (b + 1) * quota] = jnp.where(allowed, 0.0, MASKED)

    unit = math.log2(math.e) / math.sqrt(HEAD_SIZE)
    heads = GROUP // PARTS
    hot = hot_ref[...]

    def operands(g):
        at = (first + g) * HEAD_SIZE
        keys = jnp.concatenate([r[:, at : at + HEAD_SIZE] for r in kv_refs], axis=0)
        at += KV_WIDTH
        values = jnp.concatenate([r[:, at : at + HEAD_SIZE] for r in kv_refs], axis=0)
        values = jnp.concatenate([values, jnp.ones_like(values)], axis=1)
        cols = slice(g * GROUP_WIDTH, (g + 1) * GROUP_WIDTH)
        q = place_rows(hot, arrived_ref[:, cols], local[:, cols])
        return q, keys, values

    def scored(q, keys, part):
        stacked = jnp.concatenate(
            [
                q[:, h * HEAD_SIZE : (h + 1) * HEAD_SIZE]
                for h in range(part * heads, (part + 1) * heads)
            ],
            axis=0,
        )
        return lax.dot_general(
            stacked, keys, (((1,), (1,)), ((), ())), preferred_element_type=jnp.float32
        )

    def finished(scores, values, g, part):
        scores = scores.reshape(heads, quota, -1) * unit + bias[...][None]
        weights = jnp.exp2(scores - jnp.max(scores, axis=2, keepdims=True))
        weights = weights.astype(jnp.bfloat16).reshape(heads * quota, -1)
        mixed = jnp.dot(weights, values, preferred_element_type=jnp.float32)
        mixed = (mixed[:, :HEAD_SIZE] / mixed[:, HEAD_SIZE:]).astype(jnp.bfloat16)
        for h in range(heads):
            at = g * GROUP_WIDTH + (part * heads + h) * HEAD_SIZE
            result[:, at : at + HEAD_SIZE] = mixed[h * quota : (h + 1) * quota]

    fetch.wait()
    stores = []
    q, keys, values = operands(0)
    scores = scored(q, keys, 0)
    for step in range(count * PARTS):
        g, part = divmod(step, PARTS)
        own_values, later = values, None
        if step + 1 < count * PARTS:
            if part == PARTS - 1:
                q, keys, values = operands(g + 1)
            later = scored(q, keys, (part + 1) % PARTS)
        finished(scores, own_values, g, part)
        scores = later
        if part == PARTS - 1:
            cols = slice(g * GROUP_WIDTH, (g + 1) * GROUP_WIDTH)
            at = (first + g) * GROUP_WIDTH
            store = pltpu.make_async_copy(
                result.at[:, cols], out_hbm.at[0, :, at : at + GROUP_WIDTH], out_sems.at[g]
            )
            store.start()
            stores.append(store)
    for store in stores:
        store.wait()


def attend(rank, hot, arrived, q_rows, kv_blocks, first, count, out):
    quota = arrived.shape[0]
    blocks = len(kv_blocks) - 1
    width = count * GROUP_WIDTH
    in_hbm = pl.BlockSpec(memory_space=pltpu.HBM)
    in_specs = [SCALARS, WHOLE, WHOLE] + [WHOLE] * len(kv_blocks) + [in_hbm]
    operands = [rank, hot, arrived, *kv_blocks, q_rows]
    aliases = {}
    if out is not None:
        in_specs.append(in_hbm)
        aliases = {len(operands): 0}
        operands.append(out)
    return pl.pallas_call(
        functools.partial(attend_kernel, blocks, first, count),
        in_specs=in_specs,
        out_specs=in_hbm,
        out_shape=jax.ShapeDtypeStruct((1, quota, QUERY_HEADS * HEAD_SIZE), jnp.bfloat16),
        input_output_aliases=aliases,
        scratch_shapes=[
            pltpu.VMEM((quota, width), jnp.bfloat16),
            pltpu.VMEM((quota, width), jnp.bfloat16),
            pltpu.VMEM((quota, blocks * quota), jnp.float32),
            pltpu.VMEM((quota, NOTE + quota), jnp.bfloat16),
            pltpu.SemaphoreType.DMA,
            pltpu.SemaphoreType.DMA((count,)),
        ],
        cost_estimate=pl.CostEstimate(flops=0, bytes_accessed=0, transcendentals=0),
        compiler_params=pltpu.CompilerParams(vmem_limit_bytes=24 * 1024 * 1024),
        name="attend_heads",
    )(*operands)


def circular_tail(rows, later):
    quota = later.shape[0]
    return jnp.where(later[:, None], rows[quota:], rows[:quota])


def body(q_rows, k_rows, value_slot_rows, counts, doc_ids):
    quota = doc_ids.shape[1]
    rounds = lax.axis_size("ctx") // 4
    rank = lax.axis_index("ctx")
    own_count = counts[0, 0]

    later = quota + jnp.arange(quota, dtype=jnp.int32) < own_count
    kv_tail = jnp.concatenate(
        [
            circular_tail(k_rows[0], later),
            circular_tail(value_slot_rows[0], later),
            jnp.broadcast_to(own_count.astype(jnp.bfloat16), (quota, quota)),
        ],
        axis=1,
    )
    local_kv = jnp.concatenate([k_rows[0, :quota], value_slot_rows[0, :quota]], axis=1)
    kv_tail, later = lax.optimization_barrier((kv_tail, later))
    local_kv, later = lax.optimization_barrier((local_kv, later))
    arrived_kv = shifted(kv_tail, "dp", 1)
    arrived_q = []
    first = 0
    for size in CHUNKS:
        cols = slice(first * GROUP_WIDTH, (first + size) * GROUP_WIDTH)
        arrived_q.append(shifted(circular_tail(q_rows[0, :, cols], later), "dp", 1))
        first += size

    shift = shift_in_known(own_count, quota)
    own, hot = settle_kv(shift, doc_ids, arrived_kv, local_kv)

    kv_blocks = [own]
    carried = own
    for back in range(1, rounds + 1):
        carried = shifted(carried, "ctx", 2)
        kv_blocks.append(carried)
        if back <= min(rounds, len(CHUNKS) - 1):
            carried, arrived_q[back - 1] = lax.optimization_barrier((carried, arrived_q[back - 1]))
        if back < rounds:
            kv_blocks.append(across_cores(carried))
    kv_blocks += [across_cores(carried, (1,)), across_cores(own, (0,))]

    out = None
    first = 0
    for size, arrived in zip(CHUNKS, arrived_q):
        out = attend(rank[None], hot, arrived, q_rows, kv_blocks, first, size, out)
        first += size
    return out


def solution(mesh):
    return jax.shard_map(
        body,
        mesh=mesh,
        in_specs=(
            P("dp", "ctx", None),
            P("dp", "ctx", None),
            P("dp", "ctx", None),
            P("dp", "ctx"),
            P("dp", "ctx"),
        ),
        out_specs=P("dp", "ctx", None),
        check_vma=False,
    )
```

```python
import functools
import math

import jax
import jax.numpy as jnp
from jax import lax
from jax.experimental import pallas as pl
from jax.experimental.pallas import tpu as pltpu
from jax.sharding import PartitionSpec as P

QUERY_HEADS = 64
KEY_VALUE_HEADS = 8
HEAD_SIZE = 128
GROUP = QUERY_HEADS // KEY_VALUE_HEADS
GROUP_WIDTH = GROUP * HEAD_SIZE
KV_WIDTH = KEY_VALUE_HEADS * HEAD_SIZE
NOTE = 2 * KV_WIDTH
MASKED = -1e30
CHUNKS = (2, 3, 3)
TILE = 32
VMEM_GRANT = 48 * 1024 * 1024

WHOLE = pl.BlockSpec(memory_space=pltpu.VMEM)
SCALARS = pl.BlockSpec(memory_space=pltpu.SMEM)


def shifted(x, axis, steps):
    n = lax.axis_size(axis)
    return lax.ppermute(x, axis, [(i, i + steps) for i in range(n - steps)])


def across_cores(x, sources=(0, 1)):
    n = lax.axis_size("ctx")
    return lax.ppermute(x, "ctx", [(i, i ^ 1) for i in range(n) if i % 2 in sources])


def everyones(x, axis):
    n = lax.axis_size(axis)
    spread = jnp.broadcast_to(x[None], (n,) + x.shape)
    return lax.all_to_all(spread, axis, split_axis=0, concat_axis=0)


def shift_in_known(own_count, quota):
    n = lax.axis_size("dp")
    replica = lax.axis_index("dp")
    if n > 4:
        all_counts = everyones(own_count[None], "dp")[:, 0]
        places = jnp.arange(n, dtype=jnp.int32)
        before = jnp.sum(jnp.where(places < replica, all_counts, 0))
        return jnp.stack([before - replica * quota, jnp.int32(0)])
    shift = jnp.where(own_count == 0, quota, 0)
    shift = jnp.where(replica == n - 1, quota - own_count, shift)
    shift = jnp.where(replica == 0, 0, shift)
    return jnp.stack([shift, (replica == 1).astype(jnp.int32)])


def place_rows(hot, arrived, local):
    both = jnp.concatenate([arrived, local], axis=0)
    return jnp.dot(hot, both, preferred_element_type=jnp.float32).astype(jnp.bfloat16)


def settle_kernel(shift_ref, docs_ref, arrived_ref, local_ref, out_ref, hot_ref):
    quota = out_ref.shape[0]
    count_before = arrived_ref[:, NOTE:].astype(jnp.float32).astype(jnp.int32)
    shift = jnp.where(shift_ref[1] == 1, count_before - quota, shift_ref[0])
    shift_before = shift - count_before + quota
    row = lax.broadcasted_iota(jnp.int32, (quota, quota), 0)
    col = lax.broadcasted_iota(jnp.int32, (quota, quota), 1)
    turned = row - shift_before
    turned = jnp.where(turned < 0, turned + quota, turned)
    hot_arrived = jnp.where((row < shift) & (col == turned), 1.0, 0.0)
    hot_local = jnp.where(col == row - shift, 1.0, 0.0)
    hot = jnp.concatenate([hot_arrived, hot_local], axis=1).astype(jnp.bfloat16)
    hot_ref[...] = hot
    out_ref[:, :NOTE] = place_rows(hot, arrived_ref[:, :NOTE], local_ref[...])
    docs = jnp.broadcast_to(docs_ref[...].astype(jnp.float32), (quota, quota))
    out_ref[:, NOTE:] = docs.astype(jnp.bfloat16)


def settle_kv(shift, docs, arrived, local):
    quota = arrived.shape[0]
    return pl.pallas_call(
        settle_kernel,
        in_specs=[SCALARS, WHOLE, WHOLE, WHOLE],
        out_specs=[WHOLE, WHOLE],
        out_shape=[
            jax.ShapeDtypeStruct(arrived.shape, jnp.bfloat16),
            jax.ShapeDtypeStruct((quota, 2 * quota), jnp.bfloat16),
        ],
        compiler_params=pltpu.CompilerParams(vmem_limit_bytes=VMEM_GRANT),
        name="settle_kv",
    )(shift, docs, arrived, local)


def block_ranks(rank, core, rounds):
    ranks = [rank]
    for back in range(1, rounds + 1):
        ranks.append(rank - 2 * back)
        if back < rounds:
            ranks.append(rank - 2 * back + jnp.where(core == 0, 1, -1))
    ranks.append(jnp.where(core == 0, rank - 2 * rounds + 1, rank - 1))
    return ranks


def attend_kernel(blocks, first, count, rank_ref, hot_ref, *refs):
    kv_refs, far_ref, mate_ref = refs[: blocks - 1], refs[blocks - 1], refs[blocks]
    arrived_hbm, local_hbm = refs[blocks + 1 : blocks + 3]
    out_hbm, arrived, local, result, bias, rest, q, keys, values, *refs = refs[-15:]
    scores, weights, (in_sems, out_sems) = refs[:2], refs[2:4], refs[4:]
    quota = hot_ref.shape[0]
    width = count * GROUP_WIDTH
    start = first * GROUP_WIDTH
    fetches = [
        pltpu.make_async_copy(arrived_hbm, arrived, in_sems.at[0]),
        pltpu.make_async_copy(
            local_hbm.at[0, 0:quota, start : start + width], local, in_sems.at[1]
        ),
    ]
    for fetch in fetches:
        fetch.start()

    rank = rank_ref[0]
    core = lax.rem(rank, 2)
    parts = [(first + part) * HEAD_SIZE for part in (0, KEY_VALUE_HEADS)]
    spans = [slice(at, at + count * HEAD_SIZE) for at in parts] + [slice(NOTE, NOTE + quota)]

    @pl.when(core == 0)
    def _():
        for span in spans:
            rest[:, span] = far_ref[:, span]

    @pl.when(core == 1)
    def _():
        for span in spans:
            rest[:, span] = mate_ref[:, span]

    kv_refs = [*kv_refs, rest]
    row = lax.broadcasted_iota(jnp.int32, (quota, quota), 0)
    col = lax.broadcasted_iota(jnp.int32, (quota, quota), 1)
    own_docs = kv_refs[0][:, NOTE:].astype(jnp.float32)
    q_docs = jnp.sum(jnp.where(row == col, own_docs, 0.0), axis=1, keepdims=True)
    for b, block_rank in enumerate(block_ranks(rank, core, (blocks - 1) // 2)):
        allowed = kv_refs[b][:, NOTE:].astype(jnp.float32) == q_docs
        allowed &= (col <= row) if b == 0 else (block_rank >= 0)
        bias[:, b * quota : (b + 1) * quota] = jnp.where(allowed, 0.0, MASKED)
    values[:, HEAD_SIZE:] = jnp.ones((blocks * quota, HEAD_SIZE), jnp.bfloat16)

    unit = math.log2(math.e) / math.sqrt(HEAD_SIZE)
    half = GROUP // 2

    def columns(at, g, width):
        return pl.ds(pl.multiple_of(at + g * width, width), width)

    def take_queries_and_keys(g):
        cols = columns(0, g, GROUP_WIDTH)
        placed = place_rows(hot_ref[...], arrived[:, cols], local[:, cols])
        for h in range(GROUP):
            q[h * quota : (h + 1) * quota] = placed[:, h * HEAD_SIZE : (h + 1) * HEAD_SIZE]
        for b, ref in enumerate(kv_refs):
            keys[b * quota : (b + 1) * quota] = ref[:, columns(parts[0], g, HEAD_SIZE)]

    def take_values(g):
        for b, ref in enumerate(kv_refs):
            values[b * quota : (b + 1) * quota, :HEAD_SIZE] = ref[:, columns(parts[1], g, HEAD_SIZE)]

    def score(part):
        rows = slice(part * half * quota, (part + 1) * half * quota)
        scores[part][...] = lax.dot_general(
            q[rows], keys[...], (((1,), (1,)), ((), ())), preferred_element_type=jnp.float32
        )

    def finish(part, g):
        for at in range(0, half * quota, TILE):
            rows = slice(at, at + TILE)
            bias_rows = slice(at % quota, at % quota + TILE)
            tile = scores[part][rows] * unit + bias[bias_rows]
            tile = jnp.exp2(tile - jnp.max(tile, axis=1, keepdims=True))
            weights[part][rows] = tile.astype(jnp.bfloat16)
        mixed = jnp.dot(weights[part][...], values[...], preferred_element_type=jnp.float32)
        mixed = (mixed[:, :HEAD_SIZE] / mixed[:, HEAD_SIZE:]).astype(jnp.bfloat16)
        for h in range(half):
            cols = pl.ds(
                pl.multiple_of(g * GROUP_WIDTH + (part * half + h) * HEAD_SIZE, HEAD_SIZE), HEAD_SIZE
            )
            result[:, cols] = mixed[h * quota : (h + 1) * quota]

    def store(g):
        return pltpu.make_async_copy(
            result.at[:, columns(0, g, GROUP_WIDTH)],
            out_hbm.at[0, :, columns(start, g, GROUP_WIDTH)],
            out_sems.at[g],
        )

    for fetch in fetches:
        fetch.wait()
    take_queries_and_keys(0)
    take_values(0)
    score(0)

    @pl.loop(0, count)
    def _(g):
        later = jnp.minimum(g + 1, count - 1)
        score(1)
        finish(0, g)
        take_queries_and_keys(later)
        score(0)
        finish(1, g)
        take_values(later)
        store(g).start()

    @pl.loop(0, count)
    def _(g):
        store(g).wait()


def attend(rank, hot, arrived, q_rows, kv_blocks, first, count, out):
    quota = arrived.shape[0]
    blocks = len(kv_blocks) - 1
    width = count * GROUP_WIDTH
    rows = GROUP // 2 * quota
    anywhere = pl.BlockSpec(memory_space=pl.ANY)
    in_specs = [SCALARS, WHOLE] + [WHOLE] * len(kv_blocks) + [anywhere] * 2
    operands = [rank, hot, *kv_blocks, arrived, q_rows]
    aliases = {}
    if out is not None:
        in_specs.append(anywhere)
        aliases = {len(operands): 0}
        operands.append(out)
    return pl.pallas_call(
        functools.partial(attend_kernel, blocks, first, count),
        in_specs=in_specs,
        out_specs=anywhere,
        out_shape=jax.ShapeDtypeStruct((1, quota, QUERY_HEADS * HEAD_SIZE), jnp.bfloat16),
        input_output_aliases=aliases,
        scratch_shapes=[
            pltpu.VMEM((quota, width), jnp.bfloat16),
            pltpu.VMEM((quota, width), jnp.bfloat16),
            pltpu.VMEM((quota, width), jnp.bfloat16),
            pltpu.VMEM((quota, blocks * quota), jnp.float32),
            pltpu.VMEM((quota, NOTE + quota), jnp.bfloat16),
            pltpu.VMEM((GROUP * quota, HEAD_SIZE), jnp.bfloat16),
            pltpu.VMEM((blocks * quota, HEAD_SIZE), jnp.bfloat16),
            pltpu.VMEM((blocks * quota, 2 * HEAD_SIZE), jnp.bfloat16),
            pltpu.VMEM((rows, blocks * quota), jnp.float32),
            pltpu.VMEM((rows, blocks * quota), jnp.float32),
            pltpu.VMEM((rows, blocks * quota), jnp.bfloat16),
            pltpu.VMEM((rows, blocks * quota), jnp.bfloat16),
            pltpu.SemaphoreType.DMA((2,)),
            pltpu.SemaphoreType.DMA((count,)),
        ],
        cost_estimate=pl.CostEstimate(flops=0, bytes_accessed=0, transcendentals=0),
        compiler_params=pltpu.CompilerParams(vmem_limit_bytes=VMEM_GRANT),
        name="attend_heads",
    )(*operands)


def circular_tail(rows, later):
    quota = later.shape[0]
    return jnp.where(later[:, None], rows[quota:], rows[:quota])


def body(q_rows, k_rows, value_slot_rows, counts, doc_ids):
    quota = doc_ids.shape[1]
    rounds = lax.axis_size("ctx") // 4
    rank = lax.axis_index("ctx")
    own_count = counts[0, 0]

    later = quota + jnp.arange(quota, dtype=jnp.int32) < own_count
    kv_tail = jnp.concatenate(
        [
            circular_tail(k_rows[0], later),
            circular_tail(value_slot_rows[0], later),
            jnp.broadcast_to(own_count.astype(jnp.bfloat16), (quota, quota)),
        ],
        axis=1,
    )
    local_kv = jnp.concatenate([k_rows[0, :quota], value_slot_rows[0, :quota]], axis=1)
    kv_tail, later = lax.optimization_barrier((kv_tail, later))
    local_kv, later = lax.optimization_barrier((local_kv, later))
    arrived_kv = shifted(kv_tail, "dp", 1)
    arrived_q = []
    first = 0
    for size in CHUNKS:
        cols = slice(first * GROUP_WIDTH, (first + size) * GROUP_WIDTH)
        arrived_q.append(shifted(circular_tail(q_rows[0, :, cols], later), "dp", 1))
        first += size

    shift = shift_in_known(own_count, quota)
    own, hot = settle_kv(shift, doc_ids, arrived_kv, local_kv)

    kv_blocks = [own]
    carried = own
    for back in range(1, rounds + 1):
        carried = shifted(carried, "ctx", 2)
        kv_blocks.append(carried)
        if back <= min(rounds, len(CHUNKS) - 1):
            carried, arrived_q[back - 1] = lax.optimization_barrier((carried, arrived_q[back - 1]))
        if back < rounds:
            kv_blocks.append(across_cores(carried))
    kv_blocks += [across_cores(carried, (1,)), across_cores(own, (0,))]

    out = None
    first = 0
    for size, arrived in zip(CHUNKS, arrived_q):
        out = attend(rank[None], hot, arrived, q_rows, kv_blocks, first, size, out)
        first += size
    return out


def solution(mesh):
    return jax.shard_map(
        body,
        mesh=mesh,
        in_specs=(
            P("dp", "ctx", None),
            P("dp", "ctx", None),
            P("dp", "ctx", None),
            P("dp", "ctx"),
            P("dp", "ctx"),
        ),
        out_specs=P("dp", "ctx", None),
        check_vma=False,
    )
```

```python
import functools
import math

import jax
import jax.numpy as jnp
from jax import lax
from jax.experimental import pallas as pl
from jax.experimental.pallas import tpu as pltpu
from jax.sharding import PartitionSpec as P

QUERY_HEADS = 64
KEY_VALUE_HEADS = 8
HEAD_SIZE = 128
GROUP = QUERY_HEADS // KEY_VALUE_HEADS
GROUP_WIDTH = GROUP * HEAD_SIZE
KV_WIDTH = KEY_VALUE_HEADS * HEAD_SIZE
NOTE = 2 * KV_WIDTH
MASKED = -1e30
CHUNKS = (2, 3, 3)
PARTS = 2
VMEM_GRANT = 48 * 1024 * 1024

WHOLE = pl.BlockSpec(memory_space=pltpu.VMEM)
ANYWHERE = pl.BlockSpec(memory_space=pl.ANY)
SCALARS = pl.BlockSpec(memory_space=pltpu.SMEM)


def shifted(x, axis, steps):
    n = lax.axis_size(axis)
    return lax.ppermute(x, axis, [(i, i + steps) for i in range(n - steps)])


def across_cores(x, sources=(0, 1)):
    n = lax.axis_size("ctx")
    return lax.ppermute(x, "ctx", [(i, i ^ 1) for i in range(n) if i % 2 in sources])


def everyones(x, axis):
    n = lax.axis_size(axis)
    spread = jnp.broadcast_to(x[None], (n,) + x.shape)
    return lax.all_to_all(spread, axis, split_axis=0, concat_axis=0)


def shift_in_known(own_count, quota):
    n = lax.axis_size("dp")
    replica = lax.axis_index("dp")
    if n > 4:
        all_counts = everyones(own_count[None], "dp")[:, 0]
        places = jnp.arange(n, dtype=jnp.int32)
        before = jnp.sum(jnp.where(places < replica, all_counts, 0))
        return jnp.stack([before - replica * quota, jnp.int32(0)])
    shift = jnp.where(own_count == 0, quota, 0)
    shift = jnp.where(replica == n - 1, quota - own_count, shift)
    shift = jnp.where(replica == 0, 0, shift)
    return jnp.stack([shift, (replica == 1).astype(jnp.int32)])


def place_rows(hot, arrived, local):
    both = jnp.concatenate([arrived, local], axis=0)
    return jnp.dot(hot, both, preferred_element_type=jnp.float32).astype(jnp.bfloat16)


def settle_kernel(shift_ref, docs_ref, arrived_ref, local_ref, out_ref, hot_ref):
    quota = out_ref.shape[0]
    count_before = arrived_ref[:, NOTE:].astype(jnp.float32).astype(jnp.int32)
    shift = jnp.where(shift_ref[1] == 1, count_before - quota, shift_ref[0])
    shift_before = shift - count_before + quota
    row = lax.broadcasted_iota(jnp.int32, (quota, quota), 0)
    col = lax.broadcasted_iota(jnp.int32, (quota, quota), 1)
    turned = row - shift_before
    turned = jnp.where(turned < 0, turned + quota, turned)
    hot_arrived = jnp.where((row < shift) & (col == turned), 1.0, 0.0)
    hot_local = jnp.where(col == row - shift, 1.0, 0.0)
    hot = jnp.concatenate([hot_arrived, hot_local], axis=1).astype(jnp.bfloat16)
    hot_ref[...] = hot
    out_ref[:, :NOTE] = place_rows(hot, arrived_ref[:, :NOTE], local_ref[...])
    docs = jnp.broadcast_to(docs_ref[...].astype(jnp.float32), (quota, quota))
    out_ref[:, NOTE:] = docs.astype(jnp.bfloat16)


def settle_kv(shift, docs, arrived, local):
    quota = arrived.shape[0]
    return pl.pallas_call(
        settle_kernel,
        in_specs=[SCALARS, WHOLE, WHOLE, WHOLE],
        out_specs=[WHOLE, WHOLE],
        out_shape=[
            jax.ShapeDtypeStruct(arrived.shape, jnp.bfloat16),
            jax.ShapeDtypeStruct((quota, 2 * quota), jnp.bfloat16),
        ],
        compiler_params=pltpu.CompilerParams(vmem_limit_bytes=VMEM_GRANT),
        name="settle_kv",
    )(shift, docs, arrived, local)


def block_ranks(rank, core, rounds):
    ranks = [rank]
    for back in range(1, rounds + 1):
        ranks.append(rank - 2 * back)
        if back < rounds:
            ranks.append(rank - 2 * back + jnp.where(core == 0, 1, -1))
    ranks.append(jnp.where(core == 0, rank - 2 * rounds + 1, rank - 1))
    return ranks


def place_kernel(start, hot_ref, arrived_ref, local_hbm, *refs):
    out_hbm, local, placed, in_sem, out_sems = refs[-5:]
    quota, width = arrived_ref.shape
    fetch = pltpu.make_async_copy(
        local_hbm.at[0, 0:quota, start : start + width], local, in_sem
    )
    fetch.start()
    fetch.wait()
    stores = []
    for g in range(width // GROUP_WIDTH):
        cols = slice(g * GROUP_WIDTH, (g + 1) * GROUP_WIDTH)
        placed[:, cols] = place_rows(hot_ref[...], arrived_ref[:, cols], local[:, cols])
        at = start + g * GROUP_WIDTH
        store = pltpu.make_async_copy(
            placed.at[:, cols], out_hbm.at[0, :, at : at + GROUP_WIDTH], out_sems.at[g]
        )
        store.start()
        stores.append(store)
    for store in stores:
        store.wait()


def place_queries(hot, arrived, q_rows, first, out):
    quota, width = arrived.shape
    in_specs = [WHOLE, WHOLE, ANYWHERE]
    operands = [hot, arrived, q_rows]
    aliases = {}
    if out is not None:
        aliases = {len(operands): 0}
        in_specs.append(ANYWHERE)
        operands.append(out)
    return pl.pallas_call(
        functools.partial(place_kernel, first * GROUP_WIDTH),
        in_specs=in_specs,
        out_specs=ANYWHERE,
        out_shape=jax.ShapeDtypeStruct((1, quota, QUERY_HEADS * HEAD_SIZE), jnp.bfloat16),
        input_output_aliases=aliases,
        scratch_shapes=[
            pltpu.VMEM((quota, width), jnp.bfloat16),
            pltpu.VMEM((quota, width), jnp.bfloat16),
            pltpu.SemaphoreType.DMA,
            pltpu.SemaphoreType.DMA((width // GROUP_WIDTH,)),
        ],
        compiler_params=pltpu.CompilerParams(vmem_limit_bytes=VMEM_GRANT),
        name="place_queries",
    )(*operands)


def make_bias(kv_refs, far_ref, mate_ref, bias, rank):
    quota = bias.shape[0]
    core = lax.rem(rank, 2)
    row = lax.broadcasted_iota(jnp.int32, (quota, quota), 0)
    col = lax.broadcasted_iota(jnp.int32, (quota, quota), 1)
    note = slice(NOTE, NOTE + quota)
    q_docs = jnp.where(row == col, kv_refs[0][:, note].astype(jnp.float32), 0.0)
    q_docs = jnp.sum(q_docs, axis=1, keepdims=True)
    blocks = len(kv_refs) + 1
    for b, block_rank in enumerate(block_ranks(rank, core, (blocks - 1) // 2)):
        if b < blocks - 1:
            docs = kv_refs[b][:, note].astype(jnp.float32)
        else:
            far = far_ref[:, note].astype(jnp.float32)
            docs = jnp.where(core == 0, far, mate_ref[:, note].astype(jnp.float32))
        allowed = docs == q_docs
        allowed &= (col <= row) if b == 0 else (block_rank >= 0)
        bias[:, b * quota : (b + 1) * quota] = jnp.where(allowed, 0.0, MASKED)


def attend_heads(first, count, core, kv_refs, far_ref, mate_ref, bias, rest, take, result, put):
    quota = bias.shape[0]
    parts = [(first + part) * HEAD_SIZE for part in (0, KEY_VALUE_HEADS)]

    @pl.when(core == 0)
    def _():
        for at in parts:
            rest[:, at : at + count * HEAD_SIZE] = far_ref[:, at : at + count * HEAD_SIZE]

    @pl.when(core == 1)
    def _():
        for at in parts:
            rest[:, at : at + count * HEAD_SIZE] = mate_ref[:, at : at + count * HEAD_SIZE]

    kv_refs = [*kv_refs, rest]
    unit = math.log2(math.e) / math.sqrt(HEAD_SIZE)
    heads = GROUP // PARTS

    def operands(g):
        at = (first + g) * HEAD_SIZE
        keys = jnp.concatenate([r[:, at : at + HEAD_SIZE] for r in kv_refs], axis=0)
        at += KV_WIDTH
        values = jnp.concatenate([r[:, at : at + HEAD_SIZE] for r in kv_refs], axis=0)
        values = jnp.concatenate([values, jnp.ones_like(values)], axis=1)
        return take(g), keys, values

    def scored(q, keys, part):
        stacked = jnp.concatenate(
            [
                q[:, h * HEAD_SIZE : (h + 1) * HEAD_SIZE]
                for h in range(part * heads, (part + 1) * heads)
            ],
            axis=0,
        )
        return lax.dot_general(
            stacked, keys, (((1,), (1,)), ((), ())), preferred_element_type=jnp.float32
        )

    def finished(scores, values, g, part):
        scores = scores.reshape(heads, quota, -1) * unit + bias[...][None]
        weights = jnp.exp2(scores - jnp.max(scores, axis=2, keepdims=True))
        weights = weights.astype(jnp.bfloat16).reshape(heads * quota, -1)
        mixed = jnp.dot(weights, values, preferred_element_type=jnp.float32)
        mixed = (mixed[:, :HEAD_SIZE] / mixed[:, HEAD_SIZE:]).astype(jnp.bfloat16)
        for h in range(heads):
            at = g * GROUP_WIDTH + (part * heads + h) * HEAD_SIZE
            result[:, at : at + HEAD_SIZE] = mixed[h * quota : (h + 1) * quota]

    stores = []
    q, keys, values = operands(0)
    scores = scored(q, keys, 0)
    for step in range(count * PARTS):
        g, part = divmod(step, PARTS)
        own_values, later = values, None
        if step + 1 < count * PARTS:
            if part == PARTS - 1:
                q, keys, values = operands(g + 1)
            later = scored(q, keys, (part + 1) % PARTS)
        finished(scores, own_values, g, part)
        scores = later
        if part == PARTS - 1:
            stores.append(put(g))
    for store in stores:
        store.wait()


def head_columns(g, start=0):
    return slice(start + g * GROUP_WIDTH, start + (g + 1) * GROUP_WIDTH)


def putting(result, out_hbm, sems, start):
    def put(g):
        store = pltpu.make_async_copy(
            result.at[:, head_columns(g)], out_hbm.at[0, :, head_columns(g, start)], sems.at[g]
        )
        store.start()
        return store

    return put


def early_kernel(blocks, count, rank_ref, *refs):
    kv_refs, far_ref, mate_ref = refs[: blocks - 1], refs[blocks - 1], refs[blocks]
    q_hbm, in_hbm, out_hbm, bias, local = refs[blocks + 1 : blocks + 6]
    queries, result, rest, q_sem, local_sem, out_sems = refs[blocks + 6 :]
    quota = bias.shape[0]
    start = count * GROUP_WIDTH
    fetch = pltpu.make_async_copy(in_hbm.at[0, :, 0:start], queries, q_sem)
    fetch.start()
    ahead = pltpu.make_async_copy(q_hbm.at[0, 0:quota, start:], local, local_sem)
    ahead.start()
    make_bias(kv_refs, far_ref, mate_ref, bias, rank_ref[0])
    fetch.wait()
    attend_heads(
        0,
        count,
        lax.rem(rank_ref[0], 2),
        kv_refs,
        far_ref,
        mate_ref,
        bias,
        rest,
        lambda g: queries[:, head_columns(g)],
        result,
        putting(result, out_hbm, out_sems, 0),
    )
    ahead.wait()


def last_kernel(blocks, first, count, rank_ref, *refs):
    kv_refs, far_ref, mate_ref = refs[: blocks - 1], refs[blocks - 1], refs[blocks]
    hot_ref, arrived_ref, local_ref, bias, _, out_hbm = refs[blocks + 1 : blocks + 7]
    result, rest, out_sems = refs[blocks + 7 :]

    def take(g):
        cols = head_columns(g)
        return place_rows(hot_ref[...], arrived_ref[:, cols], local_ref[:, cols])

    attend_heads(
        first,
        count,
        lax.rem(rank_ref[0], 2),
        kv_refs,
        far_ref,
        mate_ref,
        bias,
        rest,
        take,
        result,
        putting(result, out_hbm, out_sems, first * GROUP_WIDTH),
    )


def attend(rank, hot, arrived, q_rows, kv_blocks, out):
    quota, width = arrived.shape
    blocks = len(kv_blocks) - 1
    last = width // GROUP_WIDTH
    early = KEY_VALUE_HEADS - last
    whole_out = jax.ShapeDtypeStruct((1, quota, QUERY_HEADS * HEAD_SIZE), jnp.bfloat16)
    rest = pltpu.VMEM((quota, NOTE), jnp.bfloat16)
    hints = dict(
        cost_estimate=pl.CostEstimate(flops=0, bytes_accessed=0, transcendentals=0),
        compiler_params=pltpu.CompilerParams(vmem_limit_bytes=VMEM_GRANT),
    )
    out, bias, local = pl.pallas_call(
        functools.partial(early_kernel, blocks, early),
        in_specs=[SCALARS] + [WHOLE] * len(kv_blocks) + [ANYWHERE] * 2,
        out_specs=[ANYWHERE, WHOLE, WHOLE],
        out_shape=[
            whole_out,
            jax.ShapeDtypeStruct((quota, blocks * quota), jnp.float32),
            jax.ShapeDtypeStruct((quota, width), jnp.bfloat16),
        ],
        input_output_aliases={len(kv_blocks) + 2: 0},
        scratch_shapes=[
            pltpu.VMEM((quota, early * GROUP_WIDTH), jnp.bfloat16),
            pltpu.VMEM((quota, early * GROUP_WIDTH), jnp.bfloat16),
            rest,
            pltpu.SemaphoreType.DMA,
            pltpu.SemaphoreType.DMA,
            pltpu.SemaphoreType.DMA((early,)),
        ],
        name="attend_early",
        **hints,
    )(rank, *kv_blocks, q_rows, out)
    return pl.pallas_call(
        functools.partial(last_kernel, blocks, early, last),
        in_specs=[SCALARS] + [WHOLE] * (len(kv_blocks) + 4) + [ANYWHERE],
        out_specs=ANYWHERE,
        out_shape=whole_out,
        input_output_aliases={len(kv_blocks) + 5: 0},
        scratch_shapes=[
            pltpu.VMEM((quota, width), jnp.bfloat16),
            rest,
            pltpu.SemaphoreType.DMA((last,)),
        ],
        name="attend_last",
        **hints,
    )(rank, *kv_blocks, hot, arrived, local, bias, out)


def circular_tail(rows, later):
    quota = later.shape[0]
    return jnp.where(later[:, None], rows[quota:], rows[:quota])


def body(q_rows, k_rows, value_slot_rows, counts, doc_ids):
    quota = doc_ids.shape[1]
    rounds = lax.axis_size("ctx") // 4
    rank = lax.axis_index("ctx")
    own_count = counts[0, 0]

    later = quota + jnp.arange(quota, dtype=jnp.int32) < own_count
    kv_tail = jnp.concatenate(
        [
            circular_tail(k_rows[0], later),
            circular_tail(value_slot_rows[0], later),
            jnp.broadcast_to(own_count.astype(jnp.bfloat16), (quota, quota)),
        ],
        axis=1,
    )
    local_kv = jnp.concatenate([k_rows[0, :quota], value_slot_rows[0, :quota]], axis=1)
    kv_tail, later = lax.optimization_barrier((kv_tail, later))
    local_kv, later = lax.optimization_barrier((local_kv, later))
    arrived_kv = shifted(kv_tail, "dp", 1)
    arrived_q = []
    first = 0
    for size in CHUNKS:
        cols = slice(first * GROUP_WIDTH, (first + size) * GROUP_WIDTH)
        arrived_q.append(shifted(circular_tail(q_rows[0, :, cols], later), "dp", 1))
        first += size

    shift = shift_in_known(own_count, quota)
    own, hot = settle_kv(shift, doc_ids, arrived_kv, local_kv)

    kv_blocks = [own]
    carried, out = own, None
    for back in range(1, rounds + 1):
        carried = shifted(carried, "ctx", 2)
        kv_blocks.append(carried)
        if back <= len(CHUNKS) - 1:
            first = sum(CHUNKS[: back - 1])
            out = place_queries(hot, arrived_q[back - 1], q_rows, first, out)
            carried, out = lax.optimization_barrier((carried, out))
        if back < rounds:
            kv_blocks.append(across_cores(carried))
    kv_blocks += [across_cores(carried, (1,)), across_cores(own, (0,))]
    return attend(rank[None], hot, arrived_q[-1], q_rows, kv_blocks, out)


def solution(mesh):
    return jax.shard_map(
        body,
        mesh=mesh,
        in_specs=(
            P("dp", "ctx", None),
            P("dp", "ctx", None),
            P("dp", "ctx", None),
            P("dp", "ctx"),
            P("dp", "ctx"),
        ),
        out_specs=P("dp", "ctx", None),
        check_vma=False,
    )
```

```python
import functools
import math

import jax
import jax.numpy as jnp
from jax import lax
from jax.experimental import pallas as pl
from jax.experimental.pallas import tpu as pltpu
from jax.sharding import PartitionSpec as P

QUERY_HEADS = 64
KEY_VALUE_HEADS = 8
HEAD_SIZE = 128
GROUP = QUERY_HEADS // KEY_VALUE_HEADS
GROUP_WIDTH = GROUP * HEAD_SIZE
KV_WIDTH = KEY_VALUE_HEADS * HEAD_SIZE
NOTE = 2 * KV_WIDTH
MASKED = -1e30
HALF = GROUP // 2
HALF_WIDTH = HALF * HEAD_SIZE
CHUNKS = (6, 5, 5)
VMEM_GRANT = 48 * 1024 * 1024

WHOLE = pl.BlockSpec(memory_space=pltpu.VMEM)
ANYWHERE = pl.BlockSpec(memory_space=pl.ANY)
SCALARS = pl.BlockSpec(memory_space=pltpu.SMEM)


def shifted(x, axis, steps):
    n = lax.axis_size(axis)
    return lax.ppermute(x, axis, [(i, i + steps) for i in range(n - steps)])


def across_cores(x, sources=(0, 1)):
    n = lax.axis_size("ctx")
    return lax.ppermute(x, "ctx", [(i, i ^ 1) for i in range(n) if i % 2 in sources])


def everyones(x, axis):
    n = lax.axis_size(axis)
    spread = jnp.broadcast_to(x[None], (n,) + x.shape)
    return lax.all_to_all(spread, axis, split_axis=0, concat_axis=0)


def shift_in_known(own_count, quota):
    n = lax.axis_size("dp")
    replica = lax.axis_index("dp")
    if n > 4:
        all_counts = everyones(own_count[None], "dp")[:, 0]
        places = jnp.arange(n, dtype=jnp.int32)
        before = jnp.sum(jnp.where(places < replica, all_counts, 0))
        return jnp.stack([before - replica * quota, jnp.int32(0)])
    shift = jnp.where(own_count == 0, quota, 0)
    shift = jnp.where(replica == n - 1, quota - own_count, shift)
    shift = jnp.where(replica == 0, 0, shift)
    return jnp.stack([shift, (replica == 1).astype(jnp.int32)])


def place_rows(hot, arrived, local):
    both = jnp.concatenate([arrived, local], axis=0)
    return jnp.dot(hot, both, preferred_element_type=jnp.float32).astype(jnp.bfloat16)


def settle_kernel(shift_ref, docs_ref, arrived_ref, local_ref, out_ref, hot_ref):
    quota = out_ref.shape[0]
    count_before = arrived_ref[:, NOTE:].astype(jnp.float32).astype(jnp.int32)
    shift = jnp.where(shift_ref[1] == 1, count_before - quota, shift_ref[0])
    shift_before = shift - count_before + quota
    row = lax.broadcasted_iota(jnp.int32, (quota, quota), 0)
    col = lax.broadcasted_iota(jnp.int32, (quota, quota), 1)
    turned = row - shift_before
    turned = jnp.where(turned < 0, turned + quota, turned)
    hot_arrived = jnp.where((row < shift) & (col == turned), 1.0, 0.0)
    hot_local = jnp.where(col == row - shift, 1.0, 0.0)
    hot = jnp.concatenate([hot_arrived, hot_local], axis=1).astype(jnp.bfloat16)
    hot_ref[...] = hot
    out_ref[:, :NOTE] = place_rows(hot, arrived_ref[:, :NOTE], local_ref[...])
    docs = jnp.broadcast_to(docs_ref[...].astype(jnp.float32), (quota, quota))
    out_ref[:, NOTE:] = docs.astype(jnp.bfloat16)


def settle_kv(shift, docs, arrived, local):
    quota = arrived.shape[0]
    return pl.pallas_call(
        settle_kernel,
        in_specs=[SCALARS, WHOLE, WHOLE, WHOLE],
        out_specs=[WHOLE, WHOLE],
        out_shape=[
            jax.ShapeDtypeStruct(arrived.shape, jnp.bfloat16),
            jax.ShapeDtypeStruct((quota, 2 * quota), jnp.bfloat16),
        ],
        compiler_params=pltpu.CompilerParams(vmem_limit_bytes=VMEM_GRANT),
        name="settle_kv",
    )(shift, docs, arrived, local)


def block_ranks(rank, core, rounds):
    ranks = [rank]
    for back in range(1, rounds + 1):
        ranks.append(rank - 2 * back)
        if back < rounds:
            ranks.append(rank - 2 * back + jnp.where(core == 0, 1, -1))
    ranks.append(jnp.where(core == 0, rank - 2 * rounds + 1, rank - 1))
    return ranks


def half_columns(u, start=0):
    return slice((start + u) * HALF_WIDTH, (start + u + 1) * HALF_WIDTH)


def place_kernel(start, hot_ref, arrived_ref, local_hbm, *refs):
    out_hbm, local, placed, in_sem, out_sems = refs[-5:]
    quota, width = arrived_ref.shape
    at = start * HALF_WIDTH
    fetch = pltpu.make_async_copy(local_hbm.at[0, 0:quota, at : at + width], local, in_sem)
    fetch.start()
    fetch.wait()
    stores = []
    for u in range(width // HALF_WIDTH):
        cols = half_columns(u)
        placed[:, cols] = place_rows(hot_ref[...], arrived_ref[:, cols], local[:, cols])
        store = pltpu.make_async_copy(
            placed.at[:, cols], out_hbm.at[0, :, half_columns(u, start)], out_sems.at[u]
        )
        store.start()
        stores.append(store)
    for store in stores:
        store.wait()


def place_queries(hot, arrived, q_rows, first, out):
    quota, width = arrived.shape
    in_specs = [WHOLE, WHOLE, ANYWHERE]
    operands = [hot, arrived, q_rows]
    aliases = {}
    if out is not None:
        aliases = {len(operands): 0}
        in_specs.append(ANYWHERE)
        operands.append(out)
    return pl.pallas_call(
        functools.partial(place_kernel, first),
        in_specs=in_specs,
        out_specs=ANYWHERE,
        out_shape=jax.ShapeDtypeStruct((1, quota, QUERY_HEADS * HEAD_SIZE), jnp.bfloat16),
        input_output_aliases=aliases,
        scratch_shapes=[
            pltpu.VMEM((quota, width), jnp.bfloat16),
            pltpu.VMEM((quota, width), jnp.bfloat16),
            pltpu.SemaphoreType.DMA,
            pltpu.SemaphoreType.DMA((width // HALF_WIDTH,)),
        ],
        compiler_params=pltpu.CompilerParams(vmem_limit_bytes=VMEM_GRANT),
        name="place_queries",
    )(*operands)


def make_bias(kv_refs, far_ref, mate_ref, bias, rank):
    quota = bias.shape[0]
    core = lax.rem(rank, 2)
    row = lax.broadcasted_iota(jnp.int32, (quota, quota), 0)
    col = lax.broadcasted_iota(jnp.int32, (quota, quota), 1)
    note = slice(NOTE, NOTE + quota)
    q_docs = jnp.where(row == col, kv_refs[0][:, note].astype(jnp.float32), 0.0)
    q_docs = jnp.sum(q_docs, axis=1, keepdims=True)
    blocks = len(kv_refs) + 1
    for b, block_rank in enumerate(block_ranks(rank, core, (blocks - 1) // 2)):
        if b < blocks - 1:
            docs = kv_refs[b][:, note].astype(jnp.float32)
        else:
            far = far_ref[:, note].astype(jnp.float32)
            docs = jnp.where(core == 0, far, mate_ref[:, note].astype(jnp.float32))
        allowed = docs == q_docs
        allowed &= (col <= row) if b == 0 else (block_rank >= 0)
        bias[:, b * quota : (b + 1) * quota] = jnp.where(allowed, 0.0, MASKED)


def attend_kernel(blocks, first, count, late, rank_ref, *refs):
    kv_refs, far_ref, mate_ref = refs[: blocks - 1], refs[blocks - 1], refs[blocks]
    refs = refs[blocks + 1 :]
    if late:
        hot_ref, arrived_hbm, q_hbm, _, out_hbm, bias, rest, result, queries, local = refs[:10]
        sources = [
            lambda u: (arrived_hbm.at[:, half_columns(u)], queries),
            lambda u: (q_hbm.at[0, 0 : bias.shape[0], half_columns(u, first)], local),
        ]
    else:
        in_hbm, out_hbm, bias, rest, result, queries = refs[:6]
        sources = [lambda u: (in_hbm.at[0, :, half_columns(u, first)], queries)]
    in_sems, out_sems = refs[-2:]
    quota = bias.shape[0]
    fetches = []
    for u in range(count):
        fetches.append([])
        for i, source in enumerate(sources):
            origin, target = source(u)
            fetch = pltpu.make_async_copy(origin, target.at[:, half_columns(u)], in_sems.at[i, u])
            fetch.start()
            fetches[u].append(fetch)

    rank = rank_ref[0]
    core = lax.rem(rank, 2)
    make_bias(kv_refs, far_ref, mate_ref, bias, rank)
    first_head, last_head = first // 2, (first + count - 1) // 2
    parts = [(first_head + part) * HEAD_SIZE for part in (0, KEY_VALUE_HEADS)]
    spans = [slice(at, at + (last_head - first_head + 1) * HEAD_SIZE) for at in parts]

    @pl.when(core == 0)
    def _():
        for span in spans:
            rest[:, span] = far_ref[:, span]

    @pl.when(core == 1)
    def _():
        for span in spans:
            rest[:, span] = mate_ref[:, span]

    kv_refs = [*kv_refs, rest]
    unit = math.log2(math.e) / math.sqrt(HEAD_SIZE)

    def key_head(head):
        at = head * HEAD_SIZE
        keys = jnp.concatenate([r[:, at : at + HEAD_SIZE] for r in kv_refs], axis=0)
        at += KV_WIDTH
        values = jnp.concatenate([r[:, at : at + HEAD_SIZE] for r in kv_refs], axis=0)
        return keys, jnp.concatenate([values, jnp.ones_like(values)], axis=1)

    def scored(u, keys):
        for fetch in fetches[u]:
            fetch.wait()
        q = queries[:, half_columns(u)]
        if late:
            q = place_rows(hot_ref[...], q, local[:, half_columns(u)])
        stacked = jnp.concatenate(
            [q[:, h * HEAD_SIZE : (h + 1) * HEAD_SIZE] for h in range(HALF)], axis=0
        )
        return lax.dot_general(
            stacked, keys, (((1,), (1,)), ((), ())), preferred_element_type=jnp.float32
        )

    def finished(u, scores, values):
        scores = scores.reshape(HALF, quota, -1) * unit + bias[...][None]
        weights = jnp.exp2(scores - jnp.max(scores, axis=2, keepdims=True))
        weights = weights.astype(jnp.bfloat16).reshape(HALF * quota, -1)
        mixed = jnp.dot(weights, values, preferred_element_type=jnp.float32)
        totals = mixed[:, HEAD_SIZE:]
        inverse = pl.reciprocal(totals, approx=True)
        inverse = inverse * (2.0 - totals * inverse)
        mixed = (mixed[:, :HEAD_SIZE] * inverse).astype(jnp.bfloat16)
        for h in range(HALF):
            at = u * HALF_WIDTH + h * HEAD_SIZE
            result[:, at : at + HEAD_SIZE] = mixed[h * quota : (h + 1) * quota]
        store = pltpu.make_async_copy(
            result.at[:, half_columns(u)], out_hbm.at[0, :, half_columns(u, first)], out_sems.at[u]
        )
        store.start()
        return store

    stores = []
    keys, values = key_head(first_head)
    scores = scored(0, keys)
    for u in range(count):
        own_values, later = values, None
        if u + 1 < count:
            if (first + u + 1) % 2 == 0:
                keys, values = key_head((first + u + 1) // 2)
            later = scored(u + 1, keys)
        stores.append(finished(u, scores, own_values))
        scores = later
    for store in stores:
        store.wait()


def attend(rank, kv_blocks, late, out, first, count):
    quota = kv_blocks[0].shape[0]
    blocks = len(kv_blocks) - 1
    width = count * HALF_WIDTH
    columns = pltpu.VMEM((quota, width), jnp.bfloat16)
    sources = 2 if late else 1
    return pl.pallas_call(
        functools.partial(attend_kernel, blocks, first, count, bool(late)),
        in_specs=[SCALARS]
        + [WHOLE] * len(kv_blocks)
        + ([WHOLE, ANYWHERE, ANYWHERE] if late else [])
        + [ANYWHERE],
        out_specs=ANYWHERE,
        out_shape=jax.ShapeDtypeStruct((1, quota, QUERY_HEADS * HEAD_SIZE), jnp.bfloat16),
        input_output_aliases={1 + len(kv_blocks) + len(late): 0},
        scratch_shapes=[
            pltpu.VMEM((quota, blocks * quota), jnp.float32),
            pltpu.VMEM((quota, NOTE), jnp.bfloat16),
            columns,
            columns,
            *([columns] if late else []),
            pltpu.SemaphoreType.DMA((sources, count)),
            pltpu.SemaphoreType.DMA((count,)),
        ],
        cost_estimate=pl.CostEstimate(flops=0, bytes_accessed=0, transcendentals=0),
        compiler_params=pltpu.CompilerParams(vmem_limit_bytes=VMEM_GRANT),
        name="attend_late" if late else "attend_early",
    )(rank, *kv_blocks, *late, out)


def circular_tail(rows, later):
    quota = later.shape[0]
    return jnp.where(later[:, None], rows[quota:], rows[:quota])


def body(q_rows, k_rows, value_slot_rows, counts, doc_ids):
    quota = doc_ids.shape[1]
    rounds = lax.axis_size("ctx") // 4
    rank = lax.axis_index("ctx")
    own_count = counts[0, 0]

    later = quota + jnp.arange(quota, dtype=jnp.int32) < own_count
    kv_tail = jnp.concatenate(
        [
            circular_tail(k_rows[0], later),
            circular_tail(value_slot_rows[0], later),
            jnp.broadcast_to(own_count.astype(jnp.bfloat16), (quota, quota)),
        ],
        axis=1,
    )
    local_kv = jnp.concatenate([k_rows[0, :quota], value_slot_rows[0, :quota]], axis=1)
    kv_tail, later = lax.optimization_barrier((kv_tail, later))
    local_kv, later = lax.optimization_barrier((local_kv, later))
    arrived_kv = shifted(kv_tail, "dp", 1)
    arrived_q = []
    first = 0
    for size in CHUNKS:
        cols = slice(first * HALF_WIDTH, (first + size) * HALF_WIDTH)
        arrived_q.append(shifted(circular_tail(q_rows[0, :, cols], later), "dp", 1))
        first += size

    shift = shift_in_known(own_count, quota)
    own, hot = settle_kv(shift, doc_ids, arrived_kv, local_kv)

    kv_blocks = [own]
    carried, out = own, None
    for back in range(1, rounds + 1):
        carried = shifted(carried, "ctx", 2)
        kv_blocks.append(carried)
        if back <= len(CHUNKS) - 1:
            first = sum(CHUNKS[: back - 1])
            out = place_queries(hot, arrived_q[back - 1], q_rows, first, out)
            carried, out = lax.optimization_barrier((carried, out))
        if back < rounds:
            kv_blocks.append(across_cores(carried))
    kv_blocks += [across_cores(carried, (1,)), across_cores(own, (0,))]
    early, late = sum(CHUNKS[:-1]), CHUNKS[-1]
    out = attend(rank[None], kv_blocks, (), out, 0, early)
    return attend(rank[None], kv_blocks, (hot, arrived_q[-1], q_rows), out, early, late)


def solution(mesh):
    return jax.shard_map(
        body,
        mesh=mesh,
        in_specs=(
            P("dp", "ctx", None),
            P("dp", "ctx", None),
            P("dp", "ctx", None),
            P("dp", "ctx"),
            P("dp", "ctx"),
        ),
        out_specs=P("dp", "ctx", None),
        check_vma=False,
    )
```

```python
import functools
import math

import jax
import jax.numpy as jnp
from jax import lax
from jax.experimental import pallas as pl
from jax.experimental.pallas import tpu as pltpu
from jax.sharding import PartitionSpec as P

QUERY_HEADS = 64
KEY_VALUE_HEADS = 8
HEAD_SIZE = 128
GROUP = QUERY_HEADS // KEY_VALUE_HEADS
GROUP_WIDTH = GROUP * HEAD_SIZE
KV_WIDTH = KEY_VALUE_HEADS * HEAD_SIZE
NOTE = 2 * KV_WIDTH
MASKED = -1e30
HALF = GROUP // 2
HALF_WIDTH = HALF * HEAD_SIZE
CHUNKS = (5, 6, 5)
VMEM_GRANT = 48 * 1024 * 1024

WHOLE = pl.BlockSpec(memory_space=pltpu.VMEM)
ANYWHERE = pl.BlockSpec(memory_space=pl.ANY)
SCALARS = pl.BlockSpec(memory_space=pltpu.SMEM)


def shifted(x, axis, steps):
    n = lax.axis_size(axis)
    return lax.ppermute(x, axis, [(i, i + steps) for i in range(n - steps)])


def across_cores(x, sources=(0, 1)):
    n = lax.axis_size("ctx")
    return lax.ppermute(x, "ctx", [(i, i ^ 1) for i in range(n) if i % 2 in sources])


def everyones(x, axis):
    n = lax.axis_size(axis)
    spread = jnp.broadcast_to(x[None], (n,) + x.shape)
    return lax.all_to_all(spread, axis, split_axis=0, concat_axis=0)


def shift_in_known(own_count, quota):
    n = lax.axis_size("dp")
    replica = lax.axis_index("dp")
    if n > 4:
        all_counts = everyones(own_count[None], "dp")[:, 0]
        places = jnp.arange(n, dtype=jnp.int32)
        before = jnp.sum(jnp.where(places < replica, all_counts, 0))
        return jnp.stack([before - replica * quota, jnp.int32(0)])
    shift = jnp.where(own_count == 0, quota, 0)
    shift = jnp.where(replica == n - 1, quota - own_count, shift)
    shift = jnp.where(replica == 0, 0, shift)
    return jnp.stack([shift, (replica == 1).astype(jnp.int32)])


def place_rows(hot, arrived, local):
    both = jnp.concatenate([arrived, local], axis=0)
    return jnp.dot(hot, both, preferred_element_type=jnp.float32).astype(jnp.bfloat16)


def settle_kernel(shift_ref, docs_ref, arrived_ref, local_ref, out_ref, hot_ref):
    quota = out_ref.shape[0]
    count_before = arrived_ref[:, NOTE:].astype(jnp.float32).astype(jnp.int32)
    shift = jnp.where(shift_ref[1] == 1, count_before - quota, shift_ref[0])
    shift_before = shift - count_before + quota
    row = lax.broadcasted_iota(jnp.int32, (quota, quota), 0)
    col = lax.broadcasted_iota(jnp.int32, (quota, quota), 1)
    turned = row - shift_before
    turned = jnp.where(turned < 0, turned + quota, turned)
    hot_arrived = jnp.where((row < shift) & (col == turned), 1.0, 0.0)
    hot_local = jnp.where(col == row - shift, 1.0, 0.0)
    hot = jnp.concatenate([hot_arrived, hot_local], axis=1).astype(jnp.bfloat16)
    hot_ref[...] = hot
    out_ref[:, :NOTE] = place_rows(hot, arrived_ref[:, :NOTE], local_ref[...])
    docs = jnp.broadcast_to(docs_ref[...].astype(jnp.float32), (quota, quota))
    out_ref[:, NOTE:] = docs.astype(jnp.bfloat16)


def settle_kv(shift, docs, arrived, local):
    quota = arrived.shape[0]
    return pl.pallas_call(
        settle_kernel,
        in_specs=[SCALARS, WHOLE, WHOLE, WHOLE],
        out_specs=[WHOLE, WHOLE],
        out_shape=[
            jax.ShapeDtypeStruct(arrived.shape, jnp.bfloat16),
            jax.ShapeDtypeStruct((quota, 2 * quota), jnp.bfloat16),
        ],
        compiler_params=pltpu.CompilerParams(vmem_limit_bytes=VMEM_GRANT),
        name="settle_kv",
    )(shift, docs, arrived, local)


def block_ranks(rank, core, rounds):
    ranks = [rank]
    for back in range(1, rounds + 1):
        ranks.append(rank - 2 * back)
        if back < rounds:
            ranks.append(rank - 2 * back + jnp.where(core == 0, 1, -1))
    ranks.append(jnp.where(core == 0, rank - 2 * rounds + 1, rank - 1))
    return ranks


def half_columns(u, start=0):
    return slice((start + u) * HALF_WIDTH, (start + u + 1) * HALF_WIDTH)


def place_kernel(start, hot_ref, arrived_ref, local_hbm, *refs):
    out_hbm, local, placed, in_sem, out_sems = refs[-5:]
    quota, width = arrived_ref.shape
    at = start * HALF_WIDTH
    fetch = pltpu.make_async_copy(local_hbm.at[0, 0:quota, at : at + width], local, in_sem)
    fetch.start()
    fetch.wait()
    stores = []
    for u in range(width // HALF_WIDTH):
        cols = half_columns(u)
        placed[:, cols] = place_rows(hot_ref[...], arrived_ref[:, cols], local[:, cols])
        store = pltpu.make_async_copy(
            placed.at[:, cols], out_hbm.at[0, :, half_columns(u, start)], out_sems.at[u]
        )
        store.start()
        stores.append(store)
    for store in stores:
        store.wait()


def place_queries(hot, arrived, q_rows, first, out):
    quota, width = arrived.shape
    in_specs = [WHOLE, WHOLE, ANYWHERE]
    operands = [hot, arrived, q_rows]
    aliases = {}
    if out is not None:
        aliases = {len(operands): 0}
        in_specs.append(ANYWHERE)
        operands.append(out)
    return pl.pallas_call(
        functools.partial(place_kernel, first),
        in_specs=in_specs,
        out_specs=ANYWHERE,
        out_shape=jax.ShapeDtypeStruct((1, quota, QUERY_HEADS * HEAD_SIZE), jnp.bfloat16),
        input_output_aliases=aliases,
        scratch_shapes=[
            pltpu.VMEM((quota, width), jnp.bfloat16),
            pltpu.VMEM((quota, width), jnp.bfloat16),
            pltpu.SemaphoreType.DMA,
            pltpu.SemaphoreType.DMA((width // HALF_WIDTH,)),
        ],
        compiler_params=pltpu.CompilerParams(vmem_limit_bytes=VMEM_GRANT),
        name="place_queries",
    )(*operands)


def make_bias(kv_refs, far_ref, mate_ref, bias, rank):
    quota = bias.shape[0]
    core = lax.rem(rank, 2)
    row = lax.broadcasted_iota(jnp.int32, (quota, quota), 0)
    col = lax.broadcasted_iota(jnp.int32, (quota, quota), 1)
    note = slice(NOTE, NOTE + quota)
    q_docs = jnp.where(row == col, kv_refs[0][:, note].astype(jnp.float32), 0.0)
    q_docs = jnp.sum(q_docs, axis=1, keepdims=True)
    blocks = len(kv_refs) + 1
    for b, block_rank in enumerate(block_ranks(rank, core, (blocks - 1) // 2)):
        if b < blocks - 1:
            docs = kv_refs[b][:, note].astype(jnp.float32)
        else:
            far = far_ref[:, note].astype(jnp.float32)
            docs = jnp.where(core == 0, far, mate_ref[:, note].astype(jnp.float32))
        allowed = docs == q_docs
        allowed &= (col <= row) if b == 0 else (block_rank >= 0)
        bias[:, b * quota : (b + 1) * quota] = jnp.where(allowed, 0.0, MASKED)


def attend_halves(first, count, core, kv_refs, far_ref, mate_ref, bias, rest, take, result):
    quota = bias.shape[0]
    first_head, last_head = first // 2, (first + count - 1) // 2
    parts = [(first_head + part) * HEAD_SIZE for part in (0, KEY_VALUE_HEADS)]
    spans = [slice(at, at + (last_head - first_head + 1) * HEAD_SIZE) for at in parts]

    @pl.when(core == 0)
    def _():
        for span in spans:
            rest[:, span] = far_ref[:, span]

    @pl.when(core == 1)
    def _():
        for span in spans:
            rest[:, span] = mate_ref[:, span]

    kv_refs = [*kv_refs, rest]
    unit = math.log2(math.e) / math.sqrt(HEAD_SIZE)

    def key_head(head):
        at = head * HEAD_SIZE
        keys = jnp.concatenate([r[:, at : at + HEAD_SIZE] for r in kv_refs], axis=0)
        at += KV_WIDTH
        values = jnp.concatenate([r[:, at : at + HEAD_SIZE] for r in kv_refs], axis=0)
        return keys, jnp.concatenate([values, jnp.ones_like(values)], axis=1)

    def scored(u, keys):
        q = take(u)
        stacked = jnp.concatenate(
            [q[:, h * HEAD_SIZE : (h + 1) * HEAD_SIZE] for h in range(HALF)], axis=0
        )
        return lax.dot_general(
            stacked, keys, (((1,), (1,)), ((), ())), preferred_element_type=jnp.float32
        )

    def finished(u, scores, values):
        scores = scores.reshape(HALF, quota, -1) * unit + bias[...][None]
        weights = jnp.exp2(scores - jnp.max(scores, axis=2, keepdims=True))
        weights = weights.astype(jnp.bfloat16).reshape(HALF * quota, -1)
        mixed = jnp.dot(weights, values, preferred_element_type=jnp.float32)
        totals = mixed[:, HEAD_SIZE:]
        inverse = pl.reciprocal(totals, approx=True)
        inverse = inverse * (2.0 - totals * inverse)
        mixed = (mixed[:, :HEAD_SIZE] * inverse).astype(jnp.bfloat16)
        for h in range(HALF):
            at = u * HALF_WIDTH + h * HEAD_SIZE
            result[:, at : at + HEAD_SIZE] = mixed[h * quota : (h + 1) * quota]

    keys, values = key_head(first_head)
    scores = scored(0, keys)
    for u in range(count):
        own_values, later = values, None
        if u + 1 < count:
            if (first + u + 1) % 2 == 0:
                keys, values = key_head((first + u + 1) // 2)
            later = scored(u + 1, keys)
        finished(u, scores, own_values)
        scores = later


def early_kernel(blocks, count, rank_ref, *refs):
    kv_refs, far_ref, mate_ref = refs[: blocks - 1], refs[blocks - 1], refs[blocks]
    placed_hbm, result, bias, rest, queries, in_sem = refs[blocks + 1 :]
    fetch = pltpu.make_async_copy(placed_hbm.at[0, :, 0 : count * HALF_WIDTH], queries, in_sem)
    fetch.start()
    rank = rank_ref[0]
    make_bias(kv_refs, far_ref, mate_ref, bias, rank)
    fetch.wait()
    attend_halves(
        0,
        count,
        lax.rem(rank, 2),
        kv_refs,
        far_ref,
        mate_ref,
        bias,
        rest,
        lambda u: queries[:, half_columns(u)],
        result,
    )


def late_kernel(blocks, first, count, rank_ref, *refs):
    kv_refs, far_ref, mate_ref = refs[: blocks - 1], refs[blocks - 1], refs[blocks]
    hot_ref, arrived_hbm, q_hbm, early_ref, _, out_hbm = refs[blocks + 1 : blocks + 7]
    bias, rest, result, arrived, local, sems = refs[blocks + 7 :]
    at, width = first * HALF_WIDTH, count * HALF_WIDTH
    fetches = [
        pltpu.make_async_copy(arrived_hbm, arrived, sems.at[0]),
        pltpu.make_async_copy(
            q_hbm.at[0, 0 : bias.shape[0], at : at + width], local, sems.at[1]
        ),
    ]
    for fetch in fetches:
        fetch.start()
    early = pltpu.make_async_copy(early_ref, out_hbm.at[0, :, 0:at], sems.at[2])
    early.start()
    rank = rank_ref[0]
    make_bias(kv_refs, far_ref, mate_ref, bias, rank)
    for fetch in fetches:
        fetch.wait()

    def take(u):
        cols = half_columns(u)
        return place_rows(hot_ref[...], arrived[:, cols], local[:, cols])

    core = lax.rem(rank, 2)
    attend_halves(
        first, count, core, kv_refs, far_ref, mate_ref, bias, rest, take, result
    )
    store = pltpu.make_async_copy(result, out_hbm.at[0, :, at : at + width], sems.at[3])
    store.start()
    early.wait()
    store.wait()


def attend(rank, hot, arrived, q_rows, kv_blocks, out):
    quota, width = arrived.shape
    blocks = len(kv_blocks) - 1
    late = width // HALF_WIDTH
    early = 2 * KEY_VALUE_HEADS - late
    bias = pltpu.VMEM((quota, blocks * quota), jnp.float32)
    rest = pltpu.VMEM((quota, NOTE), jnp.bfloat16)
    hints = dict(
        cost_estimate=pl.CostEstimate(flops=0, bytes_accessed=0, transcendentals=0),
        compiler_params=pltpu.CompilerParams(vmem_limit_bytes=VMEM_GRANT),
    )
    result = pl.pallas_call(
        functools.partial(early_kernel, blocks, early),
        in_specs=[SCALARS] + [WHOLE] * len(kv_blocks) + [ANYWHERE],
        out_specs=WHOLE,
        out_shape=jax.ShapeDtypeStruct((quota, early * HALF_WIDTH), jnp.bfloat16),
        scratch_shapes=[
            bias,
            rest,
            pltpu.VMEM((quota, early * HALF_WIDTH), jnp.bfloat16),
            pltpu.SemaphoreType.DMA,
        ],
        name="attend_early",
        **hints,
    )(rank, *kv_blocks, out)
    columns = pltpu.VMEM((quota, width), jnp.bfloat16)
    return pl.pallas_call(
        functools.partial(late_kernel, blocks, early, late),
        in_specs=[SCALARS] + [WHOLE] * (len(kv_blocks) + 1) + [ANYWHERE] * 2 + [WHOLE, ANYWHERE],
        out_specs=ANYWHERE,
        out_shape=jax.ShapeDtypeStruct(out.shape, out.dtype),
        input_output_aliases={len(kv_blocks) + 5: 0},
        scratch_shapes=[bias, rest, columns, columns, columns, pltpu.SemaphoreType.DMA((4,))],
        name="attend_late",
        **hints,
    )(rank, *kv_blocks, hot, arrived, q_rows, result, out)


def circular_tail(rows, later):
    quota = later.shape[0]
    return jnp.where(later[:, None], rows[quota:], rows[:quota])


def body(q_rows, k_rows, value_slot_rows, counts, doc_ids):
    quota = doc_ids.shape[1]
    rounds = lax.axis_size("ctx") // 4
    rank = lax.axis_index("ctx")
    own_count = counts[0, 0]

    later = quota + jnp.arange(quota, dtype=jnp.int32) < own_count
    kv_tail = jnp.concatenate(
        [
            circular_tail(k_rows[0], later),
            circular_tail(value_slot_rows[0], later),
            jnp.broadcast_to(own_count.astype(jnp.bfloat16), (quota, quota)),
        ],
        axis=1,
    )
    local_kv = jnp.concatenate([k_rows[0, :quota], value_slot_rows[0, :quota]], axis=1)
    kv_tail, later = lax.optimization_barrier((kv_tail, later))
    local_kv, later = lax.optimization_barrier((local_kv, later))
    arrived_kv = shifted(kv_tail, "dp", 1)
    q_tails = []
    first = 0
    for size in CHUNKS:
        cols = slice(first * HALF_WIDTH, (first + size) * HALF_WIDTH)
        q_tails.append(circular_tail(q_rows[0, :, cols], later))
        first += size
    q_tails = lax.optimization_barrier(q_tails)
    arrived_q = [shifted(tail, "dp", 1) for tail in q_tails]

    shift = shift_in_known(own_count, quota)
    own, hot = settle_kv(shift, doc_ids, arrived_kv, local_kv)

    kv_blocks = [own]
    carried, out = own, None
    for back in range(1, rounds + 1):
        carried = shifted(carried, "ctx", 2)
        kv_blocks.append(carried)
        if back <= len(CHUNKS) - 1:
            first = sum(CHUNKS[: back - 1])
            out = place_queries(hot, arrived_q[back - 1], q_rows, first, out)
            carried, out = lax.optimization_barrier((carried, out))
        if back < rounds:
            kv_blocks.append(across_cores(carried))
    kv_blocks += [across_cores(carried, (1,)), across_cores(own, (0,))]
    return attend(rank[None], hot, arrived_q[-1], q_rows, kv_blocks, out)


def solution(mesh):
    return jax.shard_map(
        body,
        mesh=mesh,
        in_specs=(
            P("dp", "ctx", None),
            P("dp", "ctx", None),
            P("dp", "ctx", None),
            P("dp", "ctx"),
            P("dp", "ctx"),
        ),
        out_specs=P("dp", "ctx", None),
        check_vma=False,
    )
```

```python
import functools
import math

import jax
import jax.numpy as jnp
from jax import lax
from jax.experimental import pallas as pl
from jax.experimental.pallas import tpu as pltpu
from jax.sharding import PartitionSpec as P

QUERY_HEADS = 64
KEY_VALUE_HEADS = 8
HEAD_SIZE = 128
GROUP = QUERY_HEADS // KEY_VALUE_HEADS
KV_WIDTH = KEY_VALUE_HEADS * HEAD_SIZE
NOTE = 2 * KV_WIDTH
MASKED = -1e30
HALF = GROUP // 2
CHUNKS = (20, 20, 18, 6)
PLACED = 2
VMEM_GRANT = 32 * 1024 * 1024

WHOLE = pl.BlockSpec(memory_space=pltpu.VMEM)
ANYWHERE = pl.BlockSpec(memory_space=pl.ANY)
SCALARS = pl.BlockSpec(memory_space=pltpu.SMEM)


def shifted(x, axis, steps):
    n = lax.axis_size(axis)
    return lax.ppermute(x, axis, [(i, i + steps) for i in range(n - steps)])


def across_cores(x, sources=(0, 1)):
    n = lax.axis_size("ctx")
    return lax.ppermute(x, "ctx", [(i, i ^ 1) for i in range(n) if i % 2 in sources])


def everyones(x, axis):
    n = lax.axis_size(axis)
    spread = jnp.broadcast_to(x[None], (n,) + x.shape)
    return lax.all_to_all(spread, axis, split_axis=0, concat_axis=0)


def shift_in_known(own_count, quota):
    n = lax.axis_size("dp")
    replica = lax.axis_index("dp")
    if n > 4:
        all_counts = everyones(own_count[None], "dp")[:, 0]
        places = jnp.arange(n, dtype=jnp.int32)
        before = jnp.sum(jnp.where(places < replica, all_counts, 0))
        return jnp.stack([before - replica * quota, jnp.int32(0)])
    shift = jnp.where(own_count == 0, quota, 0)
    shift = jnp.where(replica == n - 1, quota - own_count, shift)
    shift = jnp.where(replica == 0, 0, shift)
    return jnp.stack([shift, (replica == 1).astype(jnp.int32)])


def place_rows(hot, arrived, local):
    both = jnp.concatenate([arrived, local], axis=0)
    return jnp.dot(hot, both, preferred_element_type=jnp.float32).astype(jnp.bfloat16)


def settle_kernel(shift_ref, docs_ref, arrived_ref, local_ref, out_ref, hot_ref):
    quota = out_ref.shape[0]
    count_before = arrived_ref[:, NOTE:].astype(jnp.float32).astype(jnp.int32)
    shift = jnp.where(shift_ref[1] == 1, count_before - quota, shift_ref[0])
    shift_before = shift - count_before + quota
    row = lax.broadcasted_iota(jnp.int32, (quota, quota), 0)
    col = lax.broadcasted_iota(jnp.int32, (quota, quota), 1)
    turned = row - shift_before
    turned = jnp.where(turned < 0, turned + quota, turned)
    hot_arrived = jnp.where((row < shift) & (col == turned), 1.0, 0.0)
    hot_local = jnp.where(col == row - shift, 1.0, 0.0)
    hot = jnp.concatenate([hot_arrived, hot_local], axis=1).astype(jnp.bfloat16)
    hot_ref[...] = hot
    out_ref[:, :NOTE] = place_rows(hot, arrived_ref[:, :NOTE], local_ref[...])
    docs = jnp.broadcast_to(docs_ref[...].astype(jnp.float32), (quota, quota))
    out_ref[:, NOTE:] = docs.astype(jnp.bfloat16)


def settle_kv(shift, docs, arrived, local):
    quota = arrived.shape[0]
    return pl.pallas_call(
        settle_kernel,
        in_specs=[SCALARS, WHOLE, WHOLE, WHOLE],
        out_specs=[WHOLE, WHOLE],
        out_shape=[
            jax.ShapeDtypeStruct(arrived.shape, jnp.bfloat16),
            jax.ShapeDtypeStruct((quota, 2 * quota), jnp.bfloat16),
        ],
        compiler_params=pltpu.CompilerParams(vmem_limit_bytes=VMEM_GRANT),
        name="settle_kv",
    )(shift, docs, arrived, local)


def block_ranks(rank, core, rounds):
    ranks = [rank]
    for back in range(1, rounds + 1):
        ranks.append(rank - 2 * back)
        if back < rounds:
            ranks.append(rank - 2 * back + jnp.where(core == 0, 1, -1))
    ranks.append(jnp.where(core == 0, rank - 2 * rounds + 1, rank - 1))
    return ranks


def head_columns(head, heads=1):
    return slice(head * HEAD_SIZE, (head + heads) * HEAD_SIZE)


def pieces(first, count):
    at, found = first, []
    while at < first + count:
        end = min(first + count, (at // GROUP + 1) * GROUP)
        heads = end - at
        if heads > HALF:
            heads = min(HALF, -(-heads // 2))
        found.append((at, heads))
        at += heads
    return found


def place_kernel(start, hot_ref, arrived_ref, local_hbm, *refs):
    out_hbm, local, placed, in_sem, out_sems = refs[-5:]
    quota, width = arrived_ref.shape
    at = start * HEAD_SIZE
    fetch = pltpu.make_async_copy(local_hbm.at[0, 0:quota, at : at + width], local, in_sem)
    fetch.start()
    fetch.wait()
    stores = []
    for u, (head, heads) in enumerate(pieces(start, width // HEAD_SIZE)):
        cols = head_columns(head - start, heads)
        placed[:, cols] = place_rows(hot_ref[...], arrived_ref[:, cols], local[:, cols])
        store = pltpu.make_async_copy(
            placed.at[:, cols], out_hbm.at[0, :, head_columns(head, heads)], out_sems.at[u]
        )
        store.start()
        stores.append(store)
    for store in stores:
        store.wait()


def place_queries(hot, arrived, q_rows, first, out):
    quota, width = arrived.shape
    in_specs = [WHOLE, WHOLE, ANYWHERE]
    operands = [hot, arrived, q_rows]
    aliases = {}
    if out is not None:
        aliases = {len(operands): 0}
        in_specs.append(ANYWHERE)
        operands.append(out)
    return pl.pallas_call(
        functools.partial(place_kernel, first),
        in_specs=in_specs,
        out_specs=ANYWHERE,
        out_shape=jax.ShapeDtypeStruct((1, quota, QUERY_HEADS * HEAD_SIZE), jnp.bfloat16),
        input_output_aliases=aliases,
        scratch_shapes=[
            pltpu.VMEM((quota, width), jnp.bfloat16),
            pltpu.VMEM((quota, width), jnp.bfloat16),
            pltpu.SemaphoreType.DMA,
            pltpu.SemaphoreType.DMA((len(pieces(first, width // HEAD_SIZE)),)),
        ],
        compiler_params=pltpu.CompilerParams(vmem_limit_bytes=VMEM_GRANT),
        name="place_queries",
    )(*operands)


def make_bias(kv_refs, far_ref, mate_ref, bias, rank):
    quota = bias.shape[0]
    core = lax.rem(rank, 2)
    row = lax.broadcasted_iota(jnp.int32, (quota, quota), 0)
    col = lax.broadcasted_iota(jnp.int32, (quota, quota), 1)
    note = slice(NOTE, NOTE + quota)
    q_docs = jnp.where(row == col, kv_refs[0][:, note].astype(jnp.float32), 0.0)
    q_docs = jnp.sum(q_docs, axis=1, keepdims=True)
    blocks = len(kv_refs) + 1
    for b, block_rank in enumerate(block_ranks(rank, core, (blocks - 1) // 2)):
        if b < blocks - 1:
            docs = kv_refs[b][:, note].astype(jnp.float32)
        else:
            far = far_ref[:, note].astype(jnp.float32)
            docs = jnp.where(core == 0, far, mate_ref[:, note].astype(jnp.float32))
        allowed = docs == q_docs
        allowed &= (col <= row) if b == 0 else (block_rank >= 0)
        bias[:, b * quota : (b + 1) * quota] = jnp.where(allowed, 0.0, MASKED)


def choose_rest(first, count, core, far_ref, mate_ref, rest):
    first_head, last_head = first // GROUP, (first + count - 1) // GROUP
    keys = head_columns(first_head, last_head - first_head + 1)
    values = slice(KV_WIDTH + keys.start, KV_WIDTH + keys.stop)

    @pl.when(core == 0)
    def _():
        rest[:, keys] = far_ref[:, keys]
        rest[:, values] = far_ref[:, values]

    @pl.when(core == 1)
    def _():
        rest[:, keys] = mate_ref[:, keys]
        rest[:, values] = mate_ref[:, values]


def attend_heads(first, count, kv_refs, bias, take, result):
    quota = bias.shape[0]
    unit = math.log2(math.e) / math.sqrt(HEAD_SIZE)

    def key_head(head):
        cols = head_columns(head)
        keys = jnp.concatenate([r[:, cols] for r in kv_refs], axis=0)
        cols = head_columns(KEY_VALUE_HEADS + head)
        values = jnp.concatenate([r[:, cols] for r in kv_refs], axis=0)
        return keys, jnp.concatenate([values, jnp.ones_like(values)], axis=1)

    def scored(head, heads, keys):
        q = take(head_columns(head - first, heads))
        stacked = jnp.concatenate([q[:, head_columns(h)] for h in range(heads)], axis=0)
        return lax.dot_general(
            stacked, keys, (((1,), (1,)), ((), ())), preferred_element_type=jnp.float32
        )

    def finished(head, heads, scores, values):
        scores = scores.reshape(heads, quota, -1) * unit + bias[...][None]
        weights = jnp.exp2(scores - jnp.max(scores, axis=2, keepdims=True))
        weights = weights.astype(jnp.bfloat16).reshape(heads * quota, -1)
        mixed = jnp.dot(weights, values, preferred_element_type=jnp.float32)
        totals = mixed[:, HEAD_SIZE:]
        inverse = pl.reciprocal(totals, approx=True)
        inverse = inverse * (2.0 - totals * inverse)
        mixed = (mixed[:, :HEAD_SIZE] * inverse).astype(jnp.bfloat16)
        for h in range(heads):
            result[:, head_columns(head - first + h)] = mixed[h * quota : (h + 1) * quota]

    steps = pieces(first, count)
    keys, values = key_head(first // GROUP)
    scores = scored(*steps[0], keys)
    for i, (head, heads) in enumerate(steps):
        own_values, later = values, None
        if i + 1 < len(steps):
            if steps[i + 1][0] // GROUP != head // GROUP:
                keys, values = key_head(steps[i + 1][0] // GROUP)
            later = scored(*steps[i + 1], keys)
        finished(head, heads, scores, own_values)
        scores = later


def early_kernel(blocks, count, rank_ref, *refs):
    kv_refs, far_ref, mate_ref = refs[: blocks - 1], refs[blocks - 1], refs[blocks]
    placed_hbm, result, bias, rest, queries, in_sem = refs[blocks + 1 :]
    fetch = pltpu.make_async_copy(placed_hbm.at[0, :, head_columns(0, count)], queries, in_sem)
    fetch.start()
    rank = rank_ref[0]
    make_bias(kv_refs, far_ref, mate_ref, bias, rank)
    choose_rest(0, count, lax.rem(rank, 2), far_ref, mate_ref, rest)
    fetch.wait()
    attend_heads(0, count, [*kv_refs, rest], bias, lambda cols: queries[:, cols], result)


def late_kernel(blocks, before, first, count, last, rank_ref, *refs):
    kv_refs, far_ref, mate_ref = refs[: blocks - 1], refs[blocks - 1], refs[blocks]
    hot_ref, arrived_hbm, q_hbm, before_ref, _, out_hbm = refs[blocks + 1 : blocks + 7]
    result, bias, rest, arrived, local, sems = refs[blocks + 7 :]
    cols = head_columns(first, count)
    fetches = [
        pltpu.make_async_copy(arrived_hbm, arrived, sems.at[0]),
        pltpu.make_async_copy(q_hbm.at[0, 0 : bias.shape[0], cols], local, sems.at[1]),
    ]
    for fetch in fetches:
        fetch.start()
    rank = rank_ref[0]
    make_bias(kv_refs, far_ref, mate_ref, bias, rank)
    choose_rest(first, count, lax.rem(rank, 2), far_ref, mate_ref, rest)
    for fetch in fetches:
        fetch.wait()
    stores = [
        pltpu.make_async_copy(
            before_ref, out_hbm.at[0, :, head_columns(first - before, before)], sems.at[2]
        )
    ]
    stores[0].start()

    def take(cols):
        return place_rows(hot_ref[...], arrived[:, cols], local[:, cols])

    attend_heads(first, count, [*kv_refs, rest], bias, take, result)
    if last:
        stores.append(pltpu.make_async_copy(result, out_hbm.at[0, :, cols], sems.at[3]))
        stores[1].start()
    for store in stores:
        store.wait()


def attend(rank, hot, arrived_q, q_rows, kv_blocks, out):
    quota = hot.shape[0]
    blocks = len(kv_blocks) - 1
    counts = [arrived.shape[1] // HEAD_SIZE for arrived in arrived_q]
    first = QUERY_HEADS - sum(counts)
    bias = pltpu.VMEM((quota, blocks * quota), jnp.float32)
    rest = pltpu.VMEM((quota, NOTE), jnp.bfloat16)
    hints = dict(
        cost_estimate=pl.CostEstimate(flops=0, bytes_accessed=0, transcendentals=0),
        compiler_params=pltpu.CompilerParams(vmem_limit_bytes=VMEM_GRANT),
    )

    def columns(count):
        return (quota, count * HEAD_SIZE), jnp.bfloat16

    result = pl.pallas_call(
        functools.partial(early_kernel, blocks, first),
        in_specs=[SCALARS] + [WHOLE] * len(kv_blocks) + [ANYWHERE],
        out_specs=WHOLE,
        out_shape=jax.ShapeDtypeStruct(*columns(first)),
        scratch_shapes=[bias, rest, pltpu.VMEM(*columns(first)), pltpu.SemaphoreType.DMA],
        name="attend_early",
        **hints,
    )(rank, *kv_blocks, out)
    before = first
    for i, (arrived, count) in enumerate(zip(arrived_q, counts)):
        last = i + 1 == len(counts)
        own = columns(count)
        handed_on = [] if last else [jax.ShapeDtypeStruct(*own)]
        out, *result = pl.pallas_call(
            functools.partial(late_kernel, blocks, before, first, count, last),
            in_specs=[SCALARS]
            + [WHOLE] * (len(kv_blocks) + 1)
            + [ANYWHERE] * 2
            + [WHOLE, ANYWHERE],
            out_specs=[ANYWHERE] + [WHOLE] * len(handed_on),
            out_shape=[jax.ShapeDtypeStruct(out.shape, out.dtype)] + handed_on,
            input_output_aliases={len(kv_blocks) + 5: 0},
            scratch_shapes=[
                *([pltpu.VMEM(*own)] if last else []),
                bias,
                rest,
                pltpu.VMEM(*own),
                pltpu.VMEM(*own),
                pltpu.SemaphoreType.DMA((4,)),
            ],
            name="attend_late",
            **hints,
        )(rank, *kv_blocks, hot, arrived, q_rows, result, out)
        result = result[0] if result else None
        before, first = count, first + count
    return out


def circular_tail(rows, later):
    quota = later.shape[0]
    return jnp.where(later[:, None], rows[quota:], rows[:quota])


def body(q_rows, k_rows, value_slot_rows, counts, doc_ids):
    quota = doc_ids.shape[1]
    rounds = lax.axis_size("ctx") // 4
    rank = lax.axis_index("ctx")
    own_count = counts[0, 0]

    later = quota + jnp.arange(quota, dtype=jnp.int32) < own_count
    kv_tail = jnp.concatenate(
        [
            circular_tail(k_rows[0], later),
            circular_tail(value_slot_rows[0], later),
            jnp.broadcast_to(own_count.astype(jnp.bfloat16), (quota, quota)),
        ],
        axis=1,
    )
    local_kv = jnp.concatenate([k_rows[0, :quota], value_slot_rows[0, :quota]], axis=1)
    kv_tail, later = lax.optimization_barrier((kv_tail, later))
    local_kv, later = lax.optimization_barrier((local_kv, later))
    arrived_kv = shifted(kv_tail, "dp", 1)
    q_tails = []
    first = 0
    for size in CHUNKS:
        q_tails.append(circular_tail(q_rows[0, :, head_columns(first, size)], later))
        first += size
    q_tails[:3] = lax.optimization_barrier(q_tails[:3])
    arrived_q = [shifted(tail, "dp", 1) for tail in q_tails]

    shift = shift_in_known(own_count, quota)
    own, hot = settle_kv(shift, doc_ids, arrived_kv, local_kv)

    kv_blocks = [own]
    carried, out = own, None
    for back in range(1, rounds + 1):
        carried = shifted(carried, "ctx", 2)
        kv_blocks.append(carried)
        if back <= PLACED:
            first = sum(CHUNKS[: back - 1])
            out = place_queries(hot, arrived_q[back - 1], q_rows, first, out)
            carried, out = lax.optimization_barrier((carried, out))
        if back < rounds:
            kv_blocks.append(across_cores(carried))
    kv_blocks += [across_cores(carried, (1,)), across_cores(own, (0,))]
    return attend(rank[None], hot, arrived_q[PLACED:], q_rows, kv_blocks, out)


def solution(mesh):
    return jax.shard_map(
        body,
        mesh=mesh,
        in_specs=(
            P("dp", "ctx", None),
            P("dp", "ctx", None),
            P("dp", "ctx", None),
            P("dp", "ctx"),
            P("dp", "ctx"),
        ),
        out_specs=P("dp", "ctx", None),
        check_vma=False,
    )
```

```python
import functools
import math

import jax
import jax.numpy as jnp
from jax import lax
from jax.experimental import pallas as pl
from jax.experimental.pallas import tpu as pltpu
from jax.sharding import PartitionSpec as P

QUERY_HEADS = 64
KEY_VALUE_HEADS = 8
HEAD_SIZE = 128
GROUP = QUERY_HEADS // KEY_VALUE_HEADS
KV_WIDTH = KEY_VALUE_HEADS * HEAD_SIZE
NOTE = 2 * KV_WIDTH
MASKED = -1e30
HALF = GROUP // 2
CHUNKS = (20, 24, 20)
VMEM_GRANT = 48 * 1024 * 1024

WHOLE = pl.BlockSpec(memory_space=pltpu.VMEM)
ANYWHERE = pl.BlockSpec(memory_space=pl.ANY)
SCALARS = pl.BlockSpec(memory_space=pltpu.SMEM)


def shifted(x, axis, steps):
    n = lax.axis_size(axis)
    return lax.ppermute(x, axis, [(i, i + steps) for i in range(n - steps)])


def across_cores(x, sources=(0, 1)):
    n = lax.axis_size("ctx")
    return lax.ppermute(x, "ctx", [(i, i ^ 1) for i in range(n) if i % 2 in sources])


def everyones(x, axis):
    n = lax.axis_size(axis)
    spread = jnp.broadcast_to(x[None], (n,) + x.shape)
    return lax.all_to_all(spread, axis, split_axis=0, concat_axis=0)


def shift_in_known(own_count, quota):
    n = lax.axis_size("dp")
    replica = lax.axis_index("dp")
    if n > 4:
        all_counts = everyones(own_count[None], "dp")[:, 0]
        places = jnp.arange(n, dtype=jnp.int32)
        before = jnp.sum(jnp.where(places < replica, all_counts, 0))
        return jnp.stack([before - replica * quota, jnp.int32(0)])
    shift = jnp.where(own_count == 0, quota, 0)
    shift = jnp.where(replica == n - 1, quota - own_count, shift)
    shift = jnp.where(replica == 0, 0, shift)
    return jnp.stack([shift, (replica == 1).astype(jnp.int32)])


def place_rows(hot, arrived, local):
    both = jnp.concatenate([arrived, local], axis=0)
    return jnp.dot(hot, both, preferred_element_type=jnp.float32).astype(jnp.bfloat16)


def settle_kernel(shift_ref, docs_ref, arrived_ref, local_ref, out_ref, hot_ref):
    quota = out_ref.shape[0]
    count_before = arrived_ref[:, NOTE:].astype(jnp.float32).astype(jnp.int32)
    shift = jnp.where(shift_ref[1] == 1, count_before - quota, shift_ref[0])
    shift_before = shift - count_before + quota
    row = lax.broadcasted_iota(jnp.int32, (quota, quota), 0)
    col = lax.broadcasted_iota(jnp.int32, (quota, quota), 1)
    turned = row - shift_before
    turned = jnp.where(turned < 0, turned + quota, turned)
    hot_arrived = jnp.where((row < shift) & (col == turned), 1.0, 0.0)
    hot_local = jnp.where(col == row - shift, 1.0, 0.0)
    hot = jnp.concatenate([hot_arrived, hot_local], axis=1).astype(jnp.bfloat16)
    hot_ref[...] = hot
    out_ref[:, :NOTE] = place_rows(hot, arrived_ref[:, :NOTE], local_ref[...])
    docs = jnp.broadcast_to(docs_ref[...].astype(jnp.float32), (quota, quota))
    out_ref[:, NOTE:] = docs.astype(jnp.bfloat16)


def settle_kv(shift, docs, arrived, local):
    quota = arrived.shape[0]
    return pl.pallas_call(
        settle_kernel,
        in_specs=[SCALARS, WHOLE, WHOLE, WHOLE],
        out_specs=[WHOLE, WHOLE],
        out_shape=[
            jax.ShapeDtypeStruct(arrived.shape, jnp.bfloat16),
            jax.ShapeDtypeStruct((quota, 2 * quota), jnp.bfloat16),
        ],
        compiler_params=pltpu.CompilerParams(vmem_limit_bytes=VMEM_GRANT),
        name="settle_kv",
    )(shift, docs, arrived, local)


def block_ranks(rank, core, rounds):
    ranks = [rank]
    for back in range(1, rounds + 1):
        ranks.append(rank - 2 * back)
        if back < rounds:
            ranks.append(rank - 2 * back + jnp.where(core == 0, 1, -1))
    ranks.append(jnp.where(core == 0, rank - 2 * rounds + 1, rank - 1))
    return ranks


def head_columns(head, heads=1):
    return slice(head * HEAD_SIZE, (head + heads) * HEAD_SIZE)


def pieces(first, count):
    at, found = first, []
    while at < first + count:
        end = min(first + count, (at // GROUP + 1) * GROUP)
        heads = end - at
        if heads > HALF:
            heads = min(HALF, -(-heads // 2))
        found.append((at, heads))
        at += heads
    return found


def in_place(kernel, operands, out, more_out=(), more_specs=(), **arguments):
    specs = arguments.pop("in_specs") + [ANYWHERE]
    return pl.pallas_call(
        kernel,
        in_specs=specs,
        out_specs=[ANYWHERE, *more_specs],
        out_shape=[jax.ShapeDtypeStruct(out.shape, out.dtype), *more_out],
        input_output_aliases={len(operands): 0},
        cost_estimate=pl.CostEstimate(flops=0, bytes_accessed=0, transcendentals=0),
        compiler_params=pltpu.CompilerParams(vmem_limit_bytes=VMEM_GRANT),
        **arguments,
    )(*operands, out)


def stage_kernel(q_hbm, out_hbm, sem):
    copy = pltpu.make_async_copy(q_hbm.at[:, 0 : out_hbm.shape[1]], out_hbm, sem)
    copy.start()
    copy.wait()


def stage_local(q_rows, quota):
    return pl.pallas_call(
        stage_kernel,
        in_specs=[ANYWHERE],
        out_specs=ANYWHERE,
        out_shape=jax.ShapeDtypeStruct((1, quota, QUERY_HEADS * HEAD_SIZE), jnp.bfloat16),
        scratch_shapes=[pltpu.SemaphoreType.DMA],
        compiler_params=pltpu.CompilerParams(vmem_limit_bytes=VMEM_GRANT),
        name="stage_local",
    )(q_rows)


def place_kernel(first, hot_ref, arrived_ref, in_hbm, out_hbm, local, placed, in_sem, out_sem):
    quota, width = arrived_ref.shape
    cols = head_columns(first, width // HEAD_SIZE)
    fetch = pltpu.make_async_copy(in_hbm.at[0, :, cols], local, in_sem)
    fetch.start()
    fetch.wait()
    for head, heads in pieces(first, width // HEAD_SIZE):
        own = head_columns(head - first, heads)
        placed[:, own] = place_rows(hot_ref[...], arrived_ref[:, own], local[:, own])
    store = pltpu.make_async_copy(placed, out_hbm.at[0, :, cols], out_sem)
    store.start()
    store.wait()


def place_queries(hot, arrived, first, out):
    return in_place(
        functools.partial(place_kernel, first),
        [hot, arrived],
        out,
        in_specs=[WHOLE, WHOLE],
        scratch_shapes=[
            pltpu.VMEM(arrived.shape, jnp.bfloat16),
            pltpu.VMEM(arrived.shape, jnp.bfloat16),
            pltpu.SemaphoreType.DMA,
            pltpu.SemaphoreType.DMA,
        ],
        name="place_queries",
    )[0]


def make_bias(kv_refs, far_ref, mate_ref, bias, rank):
    quota = bias.shape[0]
    core = lax.rem(rank, 2)
    row = lax.broadcasted_iota(jnp.int32, (quota, quota), 0)
    col = lax.broadcasted_iota(jnp.int32, (quota, quota), 1)
    note = slice(NOTE, NOTE + quota)
    q_docs = jnp.where(row == col, kv_refs[0][:, note].astype(jnp.float32), 0.0)
    q_docs = jnp.sum(q_docs, axis=1, keepdims=True)
    blocks = len(kv_refs) + 1
    for b, block_rank in enumerate(block_ranks(rank, core, (blocks - 1) // 2)):
        if b < blocks - 1:
            docs = kv_refs[b][:, note].astype(jnp.float32)
        else:
            far = far_ref[:, note].astype(jnp.float32)
            docs = jnp.where(core == 0, far, mate_ref[:, note].astype(jnp.float32))
        allowed = docs == q_docs
        allowed &= (col <= row) if b == 0 else (block_rank >= 0)
        bias[:, b * quota : (b + 1) * quota] = jnp.where(allowed, 0.0, MASKED)


def choose_rest(first, count, core, far_ref, mate_ref, rest):
    first_head, last_head = first // GROUP, (first + count - 1) // GROUP
    keys = head_columns(first_head, last_head - first_head + 1)
    values = slice(KV_WIDTH + keys.start, KV_WIDTH + keys.stop)

    @pl.when(core == 0)
    def _():
        rest[:, keys] = far_ref[:, keys]
        rest[:, values] = far_ref[:, values]

    @pl.when(core == 1)
    def _():
        rest[:, keys] = mate_ref[:, keys]
        rest[:, values] = mate_ref[:, values]


def attend_heads(first, count, kv_refs, bias, take, result):
    quota = bias.shape[0]
    unit = math.log2(math.e) / math.sqrt(HEAD_SIZE)

    def key_head(head):
        cols = head_columns(head)
        keys = jnp.concatenate([r[:, cols] for r in kv_refs], axis=0)
        cols = head_columns(KEY_VALUE_HEADS + head)
        values = jnp.concatenate([r[:, cols] for r in kv_refs], axis=0)
        return keys, jnp.concatenate([values, jnp.ones_like(values)], axis=1)

    def scored(head, heads, keys):
        q = take(head_columns(head - first, heads))
        stacked = jnp.concatenate([q[:, head_columns(h)] for h in range(heads)], axis=0)
        return lax.dot_general(
            stacked, keys, (((1,), (1,)), ((), ())), preferred_element_type=jnp.float32
        )

    def finished(head, heads, scores, values):
        scores = scores.reshape(heads, quota, -1) * unit + bias[...][None]
        weights = jnp.exp2(scores - jnp.max(scores, axis=2, keepdims=True))
        weights = weights.astype(jnp.bfloat16).reshape(heads * quota, -1)
        mixed = jnp.dot(weights, values, preferred_element_type=jnp.float32)
        totals = mixed[:, HEAD_SIZE:]
        inverse = pl.reciprocal(totals, approx=True)
        inverse = inverse * (2.0 - totals * inverse)
        mixed = (mixed[:, :HEAD_SIZE] * inverse).astype(jnp.bfloat16)
        for h in range(heads):
            result[:, head_columns(head - first + h)] = mixed[h * quota : (h + 1) * quota]

    steps = pieces(first, count)
    keys, values = key_head(first // GROUP)
    scores = scored(*steps[0], keys)
    for i, (head, heads) in enumerate(steps):
        own_values, later = values, None
        if i + 1 < len(steps):
            if steps[i + 1][0] // GROUP != head // GROUP:
                keys, values = key_head(steps[i + 1][0] // GROUP)
            later = scored(*steps[i + 1], keys)
        finished(head, heads, scores, own_values)
        scores = later


def early_kernel(blocks, count, rank_ref, *refs):
    kv_refs, far_ref, mate_ref = refs[: blocks - 1], refs[blocks - 1], refs[blocks]
    in_hbm, _, result, local, bias, rest, queries, sems = refs[blocks + 1 :]
    late = head_columns(count, QUERY_HEADS - count)
    fetch = pltpu.make_async_copy(in_hbm.at[0, :, head_columns(0, count)], queries, sems.at[0])
    fetch.start()
    rank = rank_ref[0]
    make_bias(kv_refs, far_ref, mate_ref, bias, rank)
    choose_rest(0, count, lax.rem(rank, 2), far_ref, mate_ref, rest)
    fetch.wait()
    ahead = pltpu.make_async_copy(in_hbm.at[0, :, late], local, sems.at[1])
    ahead.start()
    attend_heads(0, count, [*kv_refs, rest], bias, lambda cols: queries[:, cols], result)
    ahead.wait()


def late_kernel(blocks, first, rank_ref, *refs):
    kv_refs, far_ref, mate_ref = refs[: blocks - 1], refs[blocks - 1], refs[blocks]
    hot_ref, arrived_hbm, early_ref, local_ref, _, out_hbm = refs[blocks + 1 : blocks + 7]
    bias, rest, arrived, result, sems = refs[blocks + 7 :]
    count = QUERY_HEADS - first
    fetch = pltpu.make_async_copy(arrived_hbm, arrived, sems.at[0])
    fetch.start()
    rank = rank_ref[0]
    make_bias(kv_refs, far_ref, mate_ref, bias, rank)
    choose_rest(first, count, lax.rem(rank, 2), far_ref, mate_ref, rest)
    fetch.wait()
    early = pltpu.make_async_copy(early_ref, out_hbm.at[0, :, head_columns(0, first)], sems.at[1])
    early.start()

    def take(cols):
        return place_rows(hot_ref[...], arrived[:, cols], local_ref[:, cols])

    attend_heads(first, count, [*kv_refs, rest], bias, take, result)
    store = pltpu.make_async_copy(result, out_hbm.at[0, :, head_columns(first, count)], sems.at[2])
    store.start()
    early.wait()
    store.wait()


def attend(rank, hot, arrived, kv_blocks, out):
    quota, width = arrived.shape
    blocks = len(kv_blocks) - 1
    first = QUERY_HEADS - width // HEAD_SIZE
    bias = pltpu.VMEM((quota, blocks * quota), jnp.float32)
    rest = pltpu.VMEM((quota, NOTE), jnp.bfloat16)
    own = (arrived.shape, jnp.bfloat16)
    others = ((quota, first * HEAD_SIZE), jnp.bfloat16)
    out, result, local = in_place(
        functools.partial(early_kernel, blocks, first),
        [rank, *kv_blocks],
        out,
        more_out=[jax.ShapeDtypeStruct(*others), jax.ShapeDtypeStruct(*own)],
        more_specs=[WHOLE, WHOLE],
        in_specs=[SCALARS] + [WHOLE] * len(kv_blocks),
        scratch_shapes=[bias, rest, pltpu.VMEM(*others), pltpu.SemaphoreType.DMA((2,))],
        name="attend_early",
    )
    return in_place(
        functools.partial(late_kernel, blocks, first),
        [rank, *kv_blocks, hot, arrived, result, local],
        out,
        in_specs=[SCALARS] + [WHOLE] * (len(kv_blocks) + 1) + [ANYWHERE, WHOLE, WHOLE],
        scratch_shapes=[
            bias,
            rest,
            pltpu.VMEM(*own),
            pltpu.VMEM(*own),
            pltpu.SemaphoreType.DMA((3,)),
        ],
        name="attend_late",
    )[0]


def circular_tail(rows, later):
    quota = later.shape[0]
    return jnp.where(later[:, None], rows[quota:], rows[:quota])


def body(q_rows, k_rows, value_slot_rows, counts, doc_ids):
    quota = doc_ids.shape[1]
    rounds = lax.axis_size("ctx") // 4
    rank = lax.axis_index("ctx")
    own_count = counts[0, 0]

    later = quota + jnp.arange(quota, dtype=jnp.int32) < own_count
    kv_tail = jnp.concatenate(
        [
            circular_tail(k_rows[0], later),
            circular_tail(value_slot_rows[0], later),
            jnp.broadcast_to(own_count.astype(jnp.bfloat16), (quota, quota)),
        ],
        axis=1,
    )
    local_kv = jnp.concatenate([k_rows[0, :quota], value_slot_rows[0, :quota]], axis=1)
    kv_tail, later = lax.optimization_barrier((kv_tail, later))
    local_kv, later = lax.optimization_barrier((local_kv, later))
    arrived_kv = shifted(kv_tail, "dp", 1)
    q_tails = []
    first = 0
    for size in CHUNKS:
        q_tails.append(circular_tail(q_rows[0, :, head_columns(first, size)], later))
        first += size
    q_tails = lax.optimization_barrier(q_tails)
    arrived_q = [shifted(tail, "dp", 1) for tail in q_tails]

    shift = shift_in_known(own_count, quota)
    out = stage_local(q_rows, quota)
    local_kv, out = lax.optimization_barrier((local_kv, out))
    own, hot = settle_kv(shift, doc_ids, arrived_kv, local_kv)

    kv_blocks = [own]
    carried = own
    for back in range(1, rounds + 1):
        carried = shifted(carried, "ctx", 2)
        kv_blocks.append(carried)
        if back < len(CHUNKS):
            first = sum(CHUNKS[: back - 1])
            out = place_queries(hot, arrived_q[back - 1], first, out)
            carried, out = lax.optimization_barrier((carried, out))
        if back < rounds:
            kv_blocks.append(across_cores(carried))
    kv_blocks += [across_cores(carried, (1,)), across_cores(own, (0,))]
    return attend(rank[None], hot, arrived_q[-1], kv_blocks, out)


def solution(mesh):
    return jax.shard_map(
        body,
        mesh=mesh,
        in_specs=(
            P("dp", "ctx", None),
            P("dp", "ctx", None),
            P("dp", "ctx", None),
            P("dp", "ctx"),
            P("dp", "ctx"),
        ),
        out_specs=P("dp", "ctx", None),
        check_vma=False,
    )
```

```python
import functools
import math

import jax
import jax.numpy as jnp
from jax import lax
from jax.experimental import pallas as pl
from jax.experimental.pallas import tpu as pltpu
from jax.sharding import PartitionSpec as P

QUERY_HEADS = 64
KEY_VALUE_HEADS = 8
HEAD_SIZE = 128
GROUP = QUERY_HEADS // KEY_VALUE_HEADS
KV_WIDTH = KEY_VALUE_HEADS * HEAD_SIZE
NOTE = 2 * KV_WIDTH
MASKED = -1e30
HALF = GROUP // 2
CHUNKS = (20, 26, 18)
VMEM_GRANT = 48 * 1024 * 1024

WHOLE = pl.BlockSpec(memory_space=pltpu.VMEM)
ANYWHERE = pl.BlockSpec(memory_space=pl.ANY)
SCALARS = pl.BlockSpec(memory_space=pltpu.SMEM)


def shifted(x, axis, steps):
    n = lax.axis_size(axis)
    return lax.ppermute(x, axis, [(i, i + steps) for i in range(n - steps)])


def across_cores(x, sources=(0, 1)):
    n = lax.axis_size("ctx")
    return lax.ppermute(x, "ctx", [(i, i ^ 1) for i in range(n) if i % 2 in sources])


def everyones(x, axis):
    n = lax.axis_size(axis)
    spread = jnp.broadcast_to(x[None], (n,) + x.shape)
    return lax.all_to_all(spread, axis, split_axis=0, concat_axis=0)


def shift_in_known(own_count, quota):
    n = lax.axis_size("dp")
    replica = lax.axis_index("dp")
    if n > 4:
        all_counts = everyones(own_count[None], "dp")[:, 0]
        places = jnp.arange(n, dtype=jnp.int32)
        before = jnp.sum(jnp.where(places < replica, all_counts, 0))
        return jnp.stack([before - replica * quota, jnp.int32(0)])
    shift = jnp.where(own_count == 0, quota, 0)
    shift = jnp.where(replica == n - 1, quota - own_count, shift)
    shift = jnp.where(replica == 0, 0, shift)
    return jnp.stack([shift, (replica == 1).astype(jnp.int32)])


def place_rows(hot, arrived, local):
    both = jnp.concatenate([arrived, local], axis=0)
    return jnp.dot(hot, both, preferred_element_type=jnp.float32).astype(jnp.bfloat16)


def pack_kernel(counts_ref, k_ref, v_ref, tail_ref, local_ref):
    quota = tail_ref.shape[0]
    own_count = counts_ref[0, 0]
    row = lax.broadcasted_iota(jnp.int32, (quota, KV_WIDTH), 0)
    later = quota + row < own_count
    for at, ref in ((0, k_ref), (KV_WIDTH, v_ref)):
        first = ref[0, :quota]
        local_ref[:, at : at + KV_WIDTH] = first
        tail_ref[:, at : at + KV_WIDTH] = jnp.where(later, ref[0, quota:], first)
    note = jnp.full((quota, quota), own_count, jnp.int32).astype(jnp.float32)
    tail_ref[:, NOTE:] = note.astype(jnp.bfloat16)


def pack_kv(counts, k_rows, v_rows, quota):
    return pl.pallas_call(
        pack_kernel,
        in_specs=[SCALARS, WHOLE, WHOLE],
        out_specs=[WHOLE, WHOLE],
        out_shape=[
            jax.ShapeDtypeStruct((quota, NOTE + quota), jnp.bfloat16),
            jax.ShapeDtypeStruct((quota, NOTE), jnp.bfloat16),
        ],
        compiler_params=pltpu.CompilerParams(vmem_limit_bytes=VMEM_GRANT),
        name="pack_kv",
    )(counts, k_rows, v_rows)


def settle_kernel(shift_ref, docs_ref, arrived_ref, local_ref, out_ref, hot_ref):
    quota = out_ref.shape[0]
    count_before = arrived_ref[:, NOTE:].astype(jnp.float32).astype(jnp.int32)
    shift = jnp.where(shift_ref[1] == 1, count_before - quota, shift_ref[0])
    shift_before = shift - count_before + quota
    row = lax.broadcasted_iota(jnp.int32, (quota, quota), 0)
    col = lax.broadcasted_iota(jnp.int32, (quota, quota), 1)
    turned = row - shift_before
    turned = jnp.where(turned < 0, turned + quota, turned)
    hot_arrived = jnp.where((row < shift) & (col == turned), 1.0, 0.0)
    hot_local = jnp.where(col == row - shift, 1.0, 0.0)
    hot = jnp.concatenate([hot_arrived, hot_local], axis=1).astype(jnp.bfloat16)
    hot_ref[...] = hot
    out_ref[:, :NOTE] = place_rows(hot, arrived_ref[:, :NOTE], local_ref[...])
    docs = jnp.broadcast_to(docs_ref[...].astype(jnp.float32), (quota, quota))
    out_ref[:, NOTE:] = docs.astype(jnp.bfloat16)


def settle_kv(shift, docs, arrived, local):
    quota = arrived.shape[0]
    return pl.pallas_call(
        settle_kernel,
        in_specs=[SCALARS, WHOLE, WHOLE, WHOLE],
        out_specs=[WHOLE, WHOLE],
        out_shape=[
            jax.ShapeDtypeStruct(arrived.shape, jnp.bfloat16),
            jax.ShapeDtypeStruct((quota, 2 * quota), jnp.bfloat16),
        ],
        compiler_params=pltpu.CompilerParams(vmem_limit_bytes=VMEM_GRANT),
        name="settle_kv",
    )(shift, docs, arrived, local)


def block_ranks(rank, core, rounds):
    ranks = [rank]
    for back in range(1, rounds + 1):
        ranks.append(rank - 2 * back)
        if back < rounds:
            ranks.append(rank - 2 * back + jnp.where(core == 0, 1, -1))
    ranks.append(jnp.where(core == 0, rank - 2 * rounds + 1, rank - 1))
    return ranks


def head_columns(head, heads=1):
    return slice(head * HEAD_SIZE, (head + heads) * HEAD_SIZE)


def pieces(first, count):
    at, found = first, []
    while at < first + count:
        end = min(first + count, (at // GROUP + 1) * GROUP)
        heads = end - at
        if heads > HALF:
            heads = min(HALF, -(-heads // 2))
        found.append((at, heads))
        at += heads
    return found


def copies(origin, target, steps, at, to, sem):
    return [
        pltpu.make_async_copy(
            origin.at[:, head_columns(head - at, heads)],
            target.at[:, head_columns(head - to, heads)],
            sem.at[i],
        )
        for i, (head, heads) in enumerate(steps)
    ]


def start_all(started):
    for copy in started:
        copy.start()


def wait_all(started):
    for copy in started:
        copy.wait()


def in_place(kernel, operands, out, more_out=(), more_specs=(), **arguments):
    specs = arguments.pop("in_specs") + [ANYWHERE]
    return pl.pallas_call(
        kernel,
        in_specs=specs,
        out_specs=[ANYWHERE, *more_specs],
        out_shape=[jax.ShapeDtypeStruct(out.shape, out.dtype), *more_out],
        input_output_aliases={len(operands): 0},
        cost_estimate=pl.CostEstimate(flops=0, bytes_accessed=0, transcendentals=0),
        compiler_params=pltpu.CompilerParams(vmem_limit_bytes=VMEM_GRANT),
        **arguments,
    )(*operands, out)


def stage_kernel(q_hbm, out_hbm, sem):
    copy = pltpu.make_async_copy(q_hbm.at[:, 0 : out_hbm.shape[1]], out_hbm, sem)
    copy.start()
    copy.wait()


def stage_local(q_rows, quota):
    return pl.pallas_call(
        stage_kernel,
        in_specs=[ANYWHERE],
        out_specs=ANYWHERE,
        out_shape=jax.ShapeDtypeStruct((1, quota, QUERY_HEADS * HEAD_SIZE), jnp.bfloat16),
        scratch_shapes=[pltpu.SemaphoreType.DMA],
        compiler_params=pltpu.CompilerParams(vmem_limit_bytes=VMEM_GRANT),
        name="stage_local",
    )(q_rows)


def place_kernel(first, hot_ref, arrived_ref, in_hbm, out_hbm, local, placed, in_sems, out_sems):
    steps = pieces(first, arrived_ref.shape[1] // HEAD_SIZE)
    fetches = copies(in_hbm.at[0], local, steps, 0, first, in_sems)
    stores = copies(placed, out_hbm.at[0], steps, first, 0, out_sems)
    start_all(fetches)
    for i, (head, heads) in enumerate(steps):
        cols = head_columns(head - first, heads)
        fetches[i].wait()
        placed[:, cols] = place_rows(hot_ref[...], arrived_ref[:, cols], local[:, cols])
        stores[i].start()
    wait_all(stores)


def place_queries(hot, arrived, first, out):
    return in_place(
        functools.partial(place_kernel, first),
        [hot, arrived],
        out,
        in_specs=[WHOLE, WHOLE],
        scratch_shapes=[
            pltpu.VMEM(arrived.shape, jnp.bfloat16),
            pltpu.VMEM(arrived.shape, jnp.bfloat16),
            pltpu.SemaphoreType.DMA((QUERY_HEADS,)),
            pltpu.SemaphoreType.DMA((QUERY_HEADS,)),
        ],
        name="place_queries",
    )[0]


def make_bias(kv_refs, far_ref, mate_ref, bias, rank):
    quota = bias.shape[0]
    core = lax.rem(rank, 2)
    row = lax.broadcasted_iota(jnp.int32, (quota, quota), 0)
    col = lax.broadcasted_iota(jnp.int32, (quota, quota), 1)
    note = slice(NOTE, NOTE + quota)
    q_docs = jnp.where(row == col, kv_refs[0][:, note].astype(jnp.float32), 0.0)
    q_docs = jnp.sum(q_docs, axis=1, keepdims=True)
    blocks = len(kv_refs) + 1
    for b, block_rank in enumerate(block_ranks(rank, core, (blocks - 1) // 2)):
        if b < blocks - 1:
            docs = kv_refs[b][:, note].astype(jnp.float32)
        else:
            far = far_ref[:, note].astype(jnp.float32)
            docs = jnp.where(core == 0, far, mate_ref[:, note].astype(jnp.float32))
        allowed = docs == q_docs
        allowed &= (col <= row) if b == 0 else (block_rank >= 0)
        bias[:, b * quota : (b + 1) * quota] = jnp.where(allowed, 0.0, MASKED)


def choose_rest(first, count, core, far_ref, mate_ref, rest):
    first_head, last_head = first // GROUP, (first + count - 1) // GROUP
    keys = head_columns(first_head, last_head - first_head + 1)
    values = slice(KV_WIDTH + keys.start, KV_WIDTH + keys.stop)

    @pl.when(core == 0)
    def _():
        rest[:, keys] = far_ref[:, keys]
        rest[:, values] = far_ref[:, values]

    @pl.when(core == 1)
    def _():
        rest[:, keys] = mate_ref[:, keys]
        rest[:, values] = mate_ref[:, values]


def attend_heads(first, count, kv_refs, bias, take, result):
    quota = bias.shape[0]
    unit = math.log2(math.e) / math.sqrt(HEAD_SIZE)

    def key_head(head):
        cols = head_columns(head)
        keys = jnp.concatenate([r[:, cols] for r in kv_refs], axis=0)
        cols = head_columns(KEY_VALUE_HEADS + head)
        values = jnp.concatenate([r[:, cols] for r in kv_refs], axis=0)
        return keys, jnp.concatenate([values, jnp.ones_like(values)], axis=1)

    def scored(head, heads, keys):
        q = take(head_columns(head - first, heads))
        stacked = jnp.concatenate([q[:, head_columns(h)] for h in range(heads)], axis=0)
        return lax.dot_general(
            stacked, keys, (((1,), (1,)), ((), ())), preferred_element_type=jnp.float32
        )

    def finished(head, heads, scores, values):
        scores = scores.reshape(heads, quota, -1) * unit + bias[...][None]
        weights = jnp.exp2(scores - jnp.max(scores, axis=2, keepdims=True))
        weights = weights.astype(jnp.bfloat16).reshape(heads * quota, -1)
        mixed = jnp.dot(weights, values, preferred_element_type=jnp.float32)
        totals = mixed[:, HEAD_SIZE:]
        inverse = pl.reciprocal(totals, approx=True)
        inverse = inverse * (2.0 - totals * inverse)
        mixed = (mixed[:, :HEAD_SIZE] * inverse).astype(jnp.bfloat16)
        for h in range(heads):
            result[:, head_columns(head - first + h)] = mixed[h * quota : (h + 1) * quota]

    steps = pieces(first, count)
    keys, values = key_head(first // GROUP)
    scores = scored(*steps[0], keys)
    for i, (head, heads) in enumerate(steps):
        own_values, later = values, None
        if i + 1 < len(steps):
            if steps[i + 1][0] // GROUP != head // GROUP:
                keys, values = key_head(steps[i + 1][0] // GROUP)
            later = scored(*steps[i + 1], keys)
        finished(head, heads, scores, own_values)
        scores = later


def early_kernel(blocks, count, rank_ref, *refs):
    kv_refs, far_ref, mate_ref = refs[: blocks - 1], refs[blocks - 1], refs[blocks]
    in_hbm, _, result, local, bias, rest, queries, sems, late_sems = refs[blocks + 1 :]
    fetches = copies(in_hbm.at[0], queries, pieces(0, count), 0, 0, sems)
    ahead = copies(in_hbm.at[0], local, pieces(count, QUERY_HEADS - count), 0, count, late_sems)
    start_all(fetches)
    rank = rank_ref[0]
    make_bias(kv_refs, far_ref, mate_ref, bias, rank)
    choose_rest(0, count, lax.rem(rank, 2), far_ref, mate_ref, rest)
    wait_all(fetches)
    start_all(ahead)
    attend_heads(0, count, [*kv_refs, rest], bias, lambda cols: queries[:, cols], result)
    wait_all(ahead)


def late_kernel(blocks, first, rank_ref, *refs):
    kv_refs, far_ref, mate_ref = refs[: blocks - 1], refs[blocks - 1], refs[blocks]
    hot_ref, arrived_hbm, early_ref, local_ref, _, out_hbm = refs[blocks + 1 : blocks + 7]
    bias, rest, arrived, result, early_sems, in_sems, out_sems = refs[blocks + 7 :]
    count = QUERY_HEADS - first
    steps = pieces(first, count)
    fetches = copies(arrived_hbm, arrived, steps, first, first, in_sems)
    early = copies(early_ref, out_hbm.at[0], pieces(0, first), 0, 0, early_sems)
    stores = copies(result, out_hbm.at[0], steps, first, 0, out_sems)
    start_all(fetches)
    rank = rank_ref[0]
    make_bias(kv_refs, far_ref, mate_ref, bias, rank)
    choose_rest(first, count, lax.rem(rank, 2), far_ref, mate_ref, rest)
    wait_all(fetches)
    start_all(early)

    def take(cols):
        return place_rows(hot_ref[...], arrived[:, cols], local_ref[:, cols])

    attend_heads(first, count, [*kv_refs, rest], bias, take, result)
    start_all(stores)
    wait_all(early)
    wait_all(stores)


def attend(rank, hot, arrived, kv_blocks, out):
    quota, width = arrived.shape
    blocks = len(kv_blocks) - 1
    first = QUERY_HEADS - width // HEAD_SIZE
    bias = pltpu.VMEM((quota, blocks * quota), jnp.float32)
    rest = pltpu.VMEM((quota, NOTE), jnp.bfloat16)
    sems = pltpu.SemaphoreType.DMA((QUERY_HEADS,))
    own = (arrived.shape, jnp.bfloat16)
    others = ((quota, first * HEAD_SIZE), jnp.bfloat16)
    out, result, local = in_place(
        functools.partial(early_kernel, blocks, first),
        [rank, *kv_blocks],
        out,
        more_out=[jax.ShapeDtypeStruct(*others), jax.ShapeDtypeStruct(*own)],
        more_specs=[WHOLE, WHOLE],
        in_specs=[SCALARS] + [WHOLE] * len(kv_blocks),
        scratch_shapes=[bias, rest, pltpu.VMEM(*others), sems, sems],
        name="attend_early",
    )
    return in_place(
        functools.partial(late_kernel, blocks, first),
        [rank, *kv_blocks, hot, arrived, result, local],
        out,
        in_specs=[SCALARS] + [WHOLE] * (len(kv_blocks) + 1) + [ANYWHERE, WHOLE, WHOLE],
        scratch_shapes=[
            bias,
            rest,
            pltpu.VMEM(*own),
            pltpu.VMEM(*own),
            sems,
            sems,
            sems,
        ],
        name="attend_late",
    )[0]


def circular_tail(rows, later):
    quota = later.shape[0]
    return jnp.where(later[:, None], rows[quota:], rows[:quota])


def body(q_rows, k_rows, value_slot_rows, counts, doc_ids):
    quota = doc_ids.shape[1]
    rounds = lax.axis_size("ctx") // 4
    rank = lax.axis_index("ctx")
    own_count = counts[0, 0]

    later = quota + jnp.arange(quota, dtype=jnp.int32) < own_count
    kv_tail, local_kv = pack_kv(counts, k_rows, value_slot_rows, quota)
    arrived_kv = shifted(kv_tail, "dp", 1)
    local_kv, later = lax.optimization_barrier((local_kv, later))
    q_tails = []
    first = 0
    for size in CHUNKS:
        q_tails.append(circular_tail(q_rows[0, :, head_columns(first, size)], later))
        first += size
    q_tails = lax.optimization_barrier(q_tails)
    arrived_q = [shifted(tail, "dp", 1) for tail in q_tails]

    shift = shift_in_known(own_count, quota)
    out = stage_local(q_rows, quota)
    local_kv, out = lax.optimization_barrier((local_kv, out))
    own, hot = settle_kv(shift, doc_ids, arrived_kv, local_kv)

    kv_blocks = [own]
    carried = own
    for back in range(1, rounds + 1):
        carried = shifted(carried, "ctx", 2)
        kv_blocks.append(carried)
        if back < len(CHUNKS):
            first = sum(CHUNKS[: back - 1])
            out = place_queries(hot, arrived_q[back - 1], first, out)
            carried, out = lax.optimization_barrier((carried, out))
        if back < rounds:
            kv_blocks.append(across_cores(carried))
    kv_blocks += [across_cores(carried), across_cores(own, (0,))]
    return attend(rank[None], hot, arrived_q[-1], kv_blocks, out)


def solution(mesh):
    return jax.shard_map(
        body,
        mesh=mesh,
        in_specs=(
            P("dp", "ctx", None),
            P("dp", "ctx", None),
            P("dp", "ctx", None),
            P("dp", "ctx"),
            P("dp", "ctx"),
        ),
        out_specs=P("dp", "ctx", None),
        check_vma=False,
    )
```

```python
import functools
import math

import jax
import jax.numpy as jnp
from jax import lax
from jax.experimental import pallas as pl
from jax.experimental.pallas import tpu as pltpu
from jax.sharding import PartitionSpec as P

QUERY_HEADS = 64
KEY_VALUE_HEADS = 8
HEAD_SIZE = 128
GROUP = QUERY_HEADS // KEY_VALUE_HEADS
KV_WIDTH = KEY_VALUE_HEADS * HEAD_SIZE
NOTE = 2 * KV_WIDTH
MASKED = -1e30
HALF = GROUP // 2
CHUNKS = (20, 26, 18)
VMEM_GRANT = 48 * 1024 * 1024

WHOLE = pl.BlockSpec(memory_space=pltpu.VMEM)
ANYWHERE = pl.BlockSpec(memory_space=pl.ANY)
SCALARS = pl.BlockSpec(memory_space=pltpu.SMEM)


def shifted(x, axis, steps):
    n = lax.axis_size(axis)
    return lax.ppermute(x, axis, [(i, i + steps) for i in range(n - steps)])


def across_cores(x, sources=(0, 1)):
    n = lax.axis_size("ctx")
    return lax.ppermute(x, "ctx", [(i, i ^ 1) for i in range(n) if i % 2 in sources])


def everyones(x, axis):
    n = lax.axis_size(axis)
    spread = jnp.broadcast_to(x[None], (n,) + x.shape)
    return lax.all_to_all(spread, axis, split_axis=0, concat_axis=0)


def shift_in_known(own_count, quota):
    n = lax.axis_size("dp")
    replica = lax.axis_index("dp")
    if n > 4:
        all_counts = everyones(own_count[None], "dp")[:, 0]
        places = jnp.arange(n, dtype=jnp.int32)
        before = jnp.sum(jnp.where(places < replica, all_counts, 0))
        return jnp.stack([before - replica * quota, jnp.int32(0)])
    shift = jnp.where(own_count == 0, quota, 0)
    shift = jnp.where(replica == n - 1, quota - own_count, shift)
    shift = jnp.where(replica == 0, 0, shift)
    return jnp.stack([shift, (replica == 1).astype(jnp.int32)])


def place_rows(hot, arrived, local):
    both = jnp.concatenate([arrived, local], axis=0)
    return jnp.dot(hot, both, preferred_element_type=jnp.float32).astype(jnp.bfloat16)


def settle_kernel(shift_ref, docs_ref, arrived_ref, local_ref, out_ref, hot_ref):
    quota = out_ref.shape[0]
    count_before = arrived_ref[:, NOTE:].astype(jnp.float32).astype(jnp.int32)
    shift = jnp.where(shift_ref[1] == 1, count_before - quota, shift_ref[0])
    shift_before = shift - count_before + quota
    row = lax.broadcasted_iota(jnp.int32, (quota, quota), 0)
    col = lax.broadcasted_iota(jnp.int32, (quota, quota), 1)
    turned = row - shift_before
    turned = jnp.where(turned < 0, turned + quota, turned)
    hot_arrived = jnp.where((row < shift) & (col == turned), 1.0, 0.0)
    hot_local = jnp.where(col == row - shift, 1.0, 0.0)
    hot = jnp.concatenate([hot_arrived, hot_local], axis=1).astype(jnp.bfloat16)
    hot_ref[...] = hot
    out_ref[:, :NOTE] = place_rows(hot, arrived_ref[:, :NOTE], local_ref[...])
    docs = jnp.broadcast_to(docs_ref[...].astype(jnp.float32), (quota, quota))
    out_ref[:, NOTE:] = docs.astype(jnp.bfloat16)


def settle_kv(shift, docs, arrived, local):
    quota = arrived.shape[0]
    return pl.pallas_call(
        settle_kernel,
        in_specs=[SCALARS, WHOLE, WHOLE, WHOLE],
        out_specs=[WHOLE, WHOLE],
        out_shape=[
            jax.ShapeDtypeStruct(arrived.shape, jnp.bfloat16),
            jax.ShapeDtypeStruct((quota, 2 * quota), jnp.bfloat16),
        ],
        compiler_params=pltpu.CompilerParams(vmem_limit_bytes=VMEM_GRANT),
        name="settle_kv",
    )(shift, docs, arrived, local)


def block_ranks(rank, core, rounds):
    ranks = [rank]
    for back in range(1, rounds + 1):
        ranks.append(rank - 2 * back)
        if back < rounds:
            ranks.append(rank - 2 * back + jnp.where(core == 0, 1, -1))
    ranks.append(jnp.where(core == 0, rank - 2 * rounds + 1, rank - 1))
    return ranks


def head_columns(head, heads=1):
    return slice(head * HEAD_SIZE, (head + heads) * HEAD_SIZE)


def pieces(first, count):
    at, found = first, []
    while at < first + count:
        end = min(first + count, (at // GROUP + 1) * GROUP)
        heads = end - at
        if heads > HALF:
            heads = min(HALF, -(-heads // 2))
        found.append((at, heads))
        at += heads
    return found


def in_place(kernel, operands, out, more_out=(), more_specs=(), **arguments):
    specs = arguments.pop("in_specs") + [ANYWHERE]
    return pl.pallas_call(
        kernel,
        in_specs=specs,
        out_specs=[ANYWHERE, *more_specs],
        out_shape=[jax.ShapeDtypeStruct(out.shape, out.dtype), *more_out],
        input_output_aliases={len(operands): 0},
        cost_estimate=pl.CostEstimate(flops=0, bytes_accessed=0, transcendentals=0),
        compiler_params=pltpu.CompilerParams(vmem_limit_bytes=VMEM_GRANT),
        **arguments,
    )(*operands, out)


def place_kernel(first, hot_ref, arrived_ref, q_hbm, *refs):
    out_hbm, local, placed, in_sem, out_sem = refs[-5:]
    quota, width = arrived_ref.shape
    cols = head_columns(first, width // HEAD_SIZE)
    fetch = pltpu.make_async_copy(q_hbm.at[0, 0:quota, cols], local, in_sem)
    fetch.start()
    fetch.wait()
    for head, heads in pieces(first, width // HEAD_SIZE):
        own = head_columns(head - first, heads)
        placed[:, own] = place_rows(hot_ref[...], arrived_ref[:, own], local[:, own])
    store = pltpu.make_async_copy(placed, out_hbm.at[0, :, cols], out_sem)
    store.start()
    store.wait()


def place_queries(hot, arrived, q_rows, first, out):
    quota = arrived.shape[0]
    arguments = dict(
        in_specs=[WHOLE, WHOLE, ANYWHERE],
        scratch_shapes=[
            pltpu.VMEM(arrived.shape, jnp.bfloat16),
            pltpu.VMEM(arrived.shape, jnp.bfloat16),
            pltpu.SemaphoreType.DMA,
            pltpu.SemaphoreType.DMA,
        ],
        name="place_queries",
    )
    kernel = functools.partial(place_kernel, first)
    if out is not None:
        return in_place(kernel, [hot, arrived, q_rows], out, **arguments)[0]
    return pl.pallas_call(
        kernel,
        out_specs=ANYWHERE,
        out_shape=jax.ShapeDtypeStruct((1, quota, QUERY_HEADS * HEAD_SIZE), jnp.bfloat16),
        compiler_params=pltpu.CompilerParams(vmem_limit_bytes=VMEM_GRANT),
        **arguments,
    )(hot, arrived, q_rows)


def make_bias(kv_refs, far_ref, mate_ref, bias, rank):
    quota = bias.shape[0]
    core = lax.rem(rank, 2)
    row = lax.broadcasted_iota(jnp.int32, (quota, quota), 0)
    col = lax.broadcasted_iota(jnp.int32, (quota, quota), 1)
    note = slice(NOTE, NOTE + quota)
    q_docs = jnp.where(row == col, kv_refs[0][:, note].astype(jnp.float32), 0.0)
    q_docs = jnp.sum(q_docs, axis=1, keepdims=True)
    blocks = len(kv_refs) + 1
    for b, block_rank in enumerate(block_ranks(rank, core, (blocks - 1) // 2)):
        if b < blocks - 1:
            docs = kv_refs[b][:, note].astype(jnp.float32)
        else:
            far = far_ref[:, note].astype(jnp.float32)
            docs = jnp.where(core == 0, far, mate_ref[:, note].astype(jnp.float32))
        allowed = docs == q_docs
        allowed &= (col <= row) if b == 0 else (block_rank >= 0)
        bias[:, b * quota : (b + 1) * quota] = jnp.where(allowed, 0.0, MASKED)


def choose_rest(first, count, core, far_ref, mate_ref, rest):
    first_head, last_head = first // GROUP, (first + count - 1) // GROUP
    keys = head_columns(first_head, last_head - first_head + 1)
    values = slice(KV_WIDTH + keys.start, KV_WIDTH + keys.stop)

    @pl.when(core == 0)
    def _():
        rest[:, keys] = far_ref[:, keys]
        rest[:, values] = far_ref[:, values]

    @pl.when(core == 1)
    def _():
        rest[:, keys] = mate_ref[:, keys]
        rest[:, values] = mate_ref[:, values]


def attend_heads(first, count, kv_refs, bias, take, result):
    quota = bias.shape[0]
    unit = math.log2(math.e) / math.sqrt(HEAD_SIZE)

    def key_head(head):
        cols = head_columns(head)
        keys = jnp.concatenate([r[:, cols] for r in kv_refs], axis=0)
        cols = head_columns(KEY_VALUE_HEADS + head)
        values = jnp.concatenate([r[:, cols] for r in kv_refs], axis=0)
        return keys, jnp.concatenate([values, jnp.ones_like(values)], axis=1)

    def scored(head, heads, keys):
        q = take(head_columns(head - first, heads))
        stacked = jnp.concatenate([q[:, head_columns(h)] for h in range(heads)], axis=0)
        return lax.dot_general(
            stacked, keys, (((1,), (1,)), ((), ())), preferred_element_type=jnp.float32
        )

    def finished(head, heads, scores, values):
        scores = scores.reshape(heads, quota, -1) * unit + bias[...][None]
        weights = jnp.exp2(scores - jnp.max(scores, axis=2, keepdims=True))
        weights = weights.astype(jnp.bfloat16).reshape(heads * quota, -1)
        mixed = jnp.dot(weights, values, preferred_element_type=jnp.float32)
        totals = mixed[:, HEAD_SIZE:]
        inverse = pl.reciprocal(totals, approx=True)
        inverse = inverse * (2.0 - totals * inverse)
        mixed = (mixed[:, :HEAD_SIZE] * inverse).astype(jnp.bfloat16)
        for h in range(heads):
            result[:, head_columns(head - first + h)] = mixed[h * quota : (h + 1) * quota]

    steps = pieces(first, count)
    keys, values = key_head(first // GROUP)
    scores = scored(*steps[0], keys)
    for i, (head, heads) in enumerate(steps):
        own_values, later = values, None
        if i + 1 < len(steps):
            if steps[i + 1][0] // GROUP != head // GROUP:
                keys, values = key_head(steps[i + 1][0] // GROUP)
            later = scored(*steps[i + 1], keys)
        finished(head, heads, scores, own_values)
        scores = later


def early_kernel(blocks, count, rank_ref, *refs):
    kv_refs, far_ref, mate_ref = refs[: blocks - 1], refs[blocks - 1], refs[blocks]
    q_hbm, in_hbm, out_hbm, local, bias, rest, queries, result, sems = refs[blocks + 1 :]
    own, others = head_columns(0, count), head_columns(count, QUERY_HEADS - count)
    fetch = pltpu.make_async_copy(in_hbm.at[0, :, own], queries, sems.at[0])
    fetch.start()
    rank = rank_ref[0]
    make_bias(kv_refs, far_ref, mate_ref, bias, rank)
    choose_rest(0, count, lax.rem(rank, 2), far_ref, mate_ref, rest)
    fetch.wait()
    attend_heads(0, count, [*kv_refs, rest], bias, lambda cols: queries[:, cols], result)
    store = pltpu.make_async_copy(result, out_hbm.at[0, :, own], sems.at[1])
    store.start()
    ahead = pltpu.make_async_copy(q_hbm.at[0, 0 : bias.shape[0], others], local, sems.at[2])
    ahead.start()
    store.wait()
    ahead.wait()


def late_kernel(blocks, first, rank_ref, *refs):
    kv_refs, far_ref, mate_ref = refs[: blocks - 1], refs[blocks - 1], refs[blocks]
    hot_ref, arrived_hbm, local_ref, _, out_hbm = refs[blocks + 1 : blocks + 6]
    bias, rest, arrived, result, sems = refs[blocks + 6 :]
    count = QUERY_HEADS - first
    fetch = pltpu.make_async_copy(arrived_hbm, arrived, sems.at[0])
    fetch.start()
    rank = rank_ref[0]
    make_bias(kv_refs, far_ref, mate_ref, bias, rank)
    choose_rest(first, count, lax.rem(rank, 2), far_ref, mate_ref, rest)
    fetch.wait()

    def take(cols):
        return place_rows(hot_ref[...], arrived[:, cols], local_ref[:, cols])

    attend_heads(first, count, [*kv_refs, rest], bias, take, result)
    store = pltpu.make_async_copy(result, out_hbm.at[0, :, head_columns(first, count)], sems.at[1])
    store.start()
    store.wait()


def attend(rank, hot, arrived, q_rows, kv_blocks, out):
    quota, width = arrived.shape
    blocks = len(kv_blocks) - 1
    first = QUERY_HEADS - width // HEAD_SIZE
    bias = pltpu.VMEM((quota, blocks * quota), jnp.float32)
    rest = pltpu.VMEM((quota, NOTE), jnp.bfloat16)
    own = pltpu.VMEM(arrived.shape, jnp.bfloat16)
    others = pltpu.VMEM((quota, first * HEAD_SIZE), jnp.bfloat16)
    out, local = in_place(
        functools.partial(early_kernel, blocks, first),
        [rank, *kv_blocks, q_rows],
        out,
        more_out=[jax.ShapeDtypeStruct(arrived.shape, jnp.bfloat16)],
        more_specs=[WHOLE],
        in_specs=[SCALARS] + [WHOLE] * len(kv_blocks) + [ANYWHERE],
        scratch_shapes=[bias, rest, others, others, pltpu.SemaphoreType.DMA((3,))],
        name="attend_early",
    )
    return in_place(
        functools.partial(late_kernel, blocks, first),
        [rank, *kv_blocks, hot, arrived, local],
        out,
        in_specs=[SCALARS] + [WHOLE] * (len(kv_blocks) + 1) + [ANYWHERE, WHOLE],
        scratch_shapes=[bias, rest, own, own, pltpu.SemaphoreType.DMA((2,))],
        name="attend_late",
    )[0]


def circular_tail(rows, later):
    quota = later.shape[0]
    return jnp.where(later[:, None], rows[quota:], rows[:quota])


def body(q_rows, k_rows, value_slot_rows, counts, doc_ids):
    quota = doc_ids.shape[1]
    rounds = lax.axis_size("ctx") // 4
    rank = lax.axis_index("ctx")
    own_count = counts[0, 0]

    later = quota + jnp.arange(quota, dtype=jnp.int32) < own_count
    kv_tail = jnp.concatenate(
        [
            circular_tail(k_rows[0], later),
            circular_tail(value_slot_rows[0], later),
            jnp.broadcast_to(own_count.astype(jnp.bfloat16), (quota, quota)),
        ],
        axis=1,
    )
    local_kv = jnp.concatenate([k_rows[0, :quota], value_slot_rows[0, :quota]], axis=1)
    kv_tail, later = lax.optimization_barrier((kv_tail, later))
    local_kv, later = lax.optimization_barrier((local_kv, later))
    arrived_kv = shifted(kv_tail, "dp", 1)
    q_tails = []
    first = 0
    for size in CHUNKS:
        q_tails.append(circular_tail(q_rows[0, :, head_columns(first, size)], later))
        first += size
    q_tails = lax.optimization_barrier(q_tails)
    arrived_q = [shifted(tail, "dp", 1) for tail in q_tails]

    shift = shift_in_known(own_count, quota)
    own, hot = settle_kv(shift, doc_ids, arrived_kv, local_kv)

    kv_blocks = [own]
    carried, out = own, None
    for back in range(1, rounds + 1):
        carried = shifted(carried, "ctx", 2)
        kv_blocks.append(carried)
        if back < len(CHUNKS):
            first = sum(CHUNKS[: back - 1])
            out = place_queries(hot, arrived_q[back - 1], q_rows, first, out)
            carried, out = lax.optimization_barrier((carried, out))
        if back < rounds:
            kv_blocks.append(across_cores(carried))
    kv_blocks += [across_cores(carried), across_cores(own, (0,))]
    return attend(rank[None], hot, arrived_q[-1], q_rows, kv_blocks, out)


def solution(mesh):
    return jax.shard_map(
        body,
        mesh=mesh,
        in_specs=(
            P("dp", "ctx", None),
            P("dp", "ctx", None),
            P("dp", "ctx", None),
            P("dp", "ctx"),
            P("dp", "ctx"),
        ),
        out_specs=P("dp", "ctx", None),
        check_vma=False,
    )
```

```python
import functools
import math

import jax
import jax.numpy as jnp
from jax import lax
from jax.experimental import pallas as pl
from jax.experimental.pallas import tpu as pltpu
from jax.sharding import PartitionSpec as P

QUERY_HEADS = 64
KEY_VALUE_HEADS = 8
HEAD_SIZE = 128
GROUP = QUERY_HEADS // KEY_VALUE_HEADS
KV_WIDTH = KEY_VALUE_HEADS * HEAD_SIZE
NOTE = 2 * KV_WIDTH
MASKED = -1e30
HALF = GROUP // 2
CHUNKS = (20, 26, 18)
VMEM_GRANT = 24 * 1024 * 1024

WHOLE = pl.BlockSpec(memory_space=pltpu.VMEM)
ANYWHERE = pl.BlockSpec(memory_space=pl.ANY)
SCALARS = pl.BlockSpec(memory_space=pltpu.SMEM)


def shifted(x, axis, steps):
    n = lax.axis_size(axis)
    return lax.ppermute(x, axis, [(i, i + steps) for i in range(n - steps)])


def across_cores(x, sources=(0, 1)):
    n = lax.axis_size("ctx")
    return lax.ppermute(x, "ctx", [(i, i ^ 1) for i in range(n) if i % 2 in sources])


def everyones(x, axis):
    n = lax.axis_size(axis)
    spread = jnp.broadcast_to(x[None], (n,) + x.shape)
    return lax.all_to_all(spread, axis, split_axis=0, concat_axis=0)


def shifts_in(own_count, quota):
    n = lax.axis_size("dp")
    replica = lax.axis_index("dp")
    if n > 4:
        all_counts = everyones(own_count[None], "dp")[:, 0]
        places = jnp.arange(n, dtype=jnp.int32)
        before = jnp.sum(jnp.where(places < replica, all_counts, 0))
        before_last = jnp.sum(jnp.where(places < replica - 1, all_counts, 0))
        return jnp.stack([before - replica * quota, before_last - (replica - 1) * quota])
    return jnp.stack([jnp.maximum(quota - own_count, 0), jnp.int32(0)])


def place_rows(hot, arrived, local):
    both = jnp.concatenate([arrived, local], axis=0)
    return jnp.dot(hot, both, preferred_element_type=jnp.float32).astype(jnp.bfloat16)


def settle_kernel(shift_ref, docs_ref, arrived_ref, local_ref, out_ref, hot_ref):
    quota = out_ref.shape[0]
    shift, shift_before = shift_ref[0], shift_ref[1]
    row = lax.broadcasted_iota(jnp.int32, (quota, quota), 0)
    col = lax.broadcasted_iota(jnp.int32, (quota, quota), 1)
    turned = row - shift_before
    turned = jnp.where(turned < 0, turned + quota, turned)
    hot_arrived = jnp.where((row < shift) & (col == turned), 1.0, 0.0)
    hot_local = jnp.where(col == row - shift, 1.0, 0.0)
    hot = jnp.concatenate([hot_arrived, hot_local], axis=1).astype(jnp.bfloat16)
    hot_ref[...] = hot
    out_ref[:, :NOTE] = place_rows(hot, arrived_ref[...], local_ref[...])
    docs = jnp.broadcast_to(docs_ref[...].astype(jnp.float32), (quota, quota))
    out_ref[:, NOTE:] = docs.astype(jnp.bfloat16)


def settle_kv(shift, docs, arrived, local):
    quota = arrived.shape[0]
    return pl.pallas_call(
        settle_kernel,
        in_specs=[SCALARS, WHOLE, WHOLE, WHOLE],
        out_specs=[WHOLE, WHOLE],
        out_shape=[
            jax.ShapeDtypeStruct((quota, NOTE + quota), jnp.bfloat16),
            jax.ShapeDtypeStruct((quota, 2 * quota), jnp.bfloat16),
        ],
        compiler_params=pltpu.CompilerParams(vmem_limit_bytes=VMEM_GRANT),
        name="settle_kv",
    )(shift, docs, arrived, local)


def block_ranks(rank, core, rounds):
    ranks = [rank]
    for back in range(1, rounds + 1):
        ranks.append(rank - 2 * back)
        if back < rounds:
            ranks.append(rank - 2 * back + jnp.where(core == 0, 1, -1))
    ranks.append(jnp.where(core == 0, rank - 2 * rounds + 1, rank - 1))
    return ranks


def head_columns(head, heads=1):
    return slice(head * HEAD_SIZE, (head + heads) * HEAD_SIZE)


def pieces(first, count):
    at, found = first, []
    while at < first + count:
        end = min(first + count, (at // GROUP + 1) * GROUP)
        heads = end - at
        if heads > HALF:
            heads = min(HALF, -(-heads // 2))
        found.append((at, heads))
        at += heads
    return found


def stage_kernel(q_hbm, *refs):
    targets, sems = refs[:-1], refs[-1]
    first, started = 0, []
    for i, target in enumerate(targets):
        quota, width = target.shape
        copy = pltpu.make_async_copy(
            q_hbm.at[0, 0:quota, first : first + width], target, sems.at[i]
        )
        copy.start()
        started.append(copy)
        first += width
    for copy in started:
        copy.wait()


def stage_local(q_rows, quota):
    return pl.pallas_call(
        stage_kernel,
        in_specs=[ANYWHERE],
        out_specs=[WHOLE] * len(CHUNKS),
        out_shape=[
            jax.ShapeDtypeStruct((quota, heads * HEAD_SIZE), jnp.bfloat16) for heads in CHUNKS
        ],
        scratch_shapes=[pltpu.SemaphoreType.DMA((len(CHUNKS),))],
        compiler_params=pltpu.CompilerParams(vmem_limit_bytes=VMEM_GRANT),
        name="stage_local",
    )(q_rows)


def place_kernel(hot_ref, arrived_ref, local_ref, placed_ref):
    for cols in (head_columns(*piece) for piece in pieces(0, placed_ref.shape[1] // HEAD_SIZE)):
        placed_ref[:, cols] = place_rows(hot_ref[...], arrived_ref[:, cols], local_ref[:, cols])


def place_queries(hot, arrived, local):
    return pl.pallas_call(
        place_kernel,
        in_specs=[WHOLE, WHOLE, WHOLE],
        out_specs=WHOLE,
        out_shape=jax.ShapeDtypeStruct(arrived.shape, jnp.bfloat16),
        compiler_params=pltpu.CompilerParams(vmem_limit_bytes=VMEM_GRANT),
        name="place_queries",
    )(hot, arrived, local)


def make_bias(kv_refs, far_ref, mate_ref, bias, rank):
    quota = bias.shape[0]
    core = lax.rem(rank, 2)
    row = lax.broadcasted_iota(jnp.int32, (quota, quota), 0)
    col = lax.broadcasted_iota(jnp.int32, (quota, quota), 1)
    note = slice(NOTE, NOTE + quota)
    q_docs = jnp.where(row == col, kv_refs[0][:, note].astype(jnp.float32), 0.0)
    q_docs = jnp.sum(q_docs, axis=1, keepdims=True)
    blocks = len(kv_refs) + 1
    for b, block_rank in enumerate(block_ranks(rank, core, (blocks - 1) // 2)):
        if b < blocks - 1:
            docs = kv_refs[b][:, note].astype(jnp.float32)
        else:
            far = far_ref[:, note].astype(jnp.float32)
            docs = jnp.where(core == 0, far, mate_ref[:, note].astype(jnp.float32))
        allowed = docs == q_docs
        allowed &= (col <= row) if b == 0 else (block_rank >= 0)
        bias[:, b * quota : (b + 1) * quota] = jnp.where(allowed, 0.0, MASKED)


def choose_rest(first, count, core, far_ref, mate_ref, rest):
    first_head, last_head = first // GROUP, (first + count - 1) // GROUP
    keys = head_columns(first_head, last_head - first_head + 1)
    values = slice(KV_WIDTH + keys.start, KV_WIDTH + keys.stop)

    @pl.when(core == 0)
    def _():
        rest[:, keys] = far_ref[:, keys]
        rest[:, values] = far_ref[:, values]

    @pl.when(core == 1)
    def _():
        rest[:, keys] = mate_ref[:, keys]
        rest[:, values] = mate_ref[:, values]


def attend_heads(first, count, kv_refs, bias, take, result):
    quota = bias.shape[0]
    unit = math.log2(math.e) / math.sqrt(HEAD_SIZE)

    def key_head(head):
        cols = head_columns(head)
        keys = jnp.concatenate([r[:, cols] for r in kv_refs], axis=0)
        cols = head_columns(KEY_VALUE_HEADS + head)
        values = jnp.concatenate([r[:, cols] for r in kv_refs], axis=0)
        return keys, jnp.concatenate([values, jnp.ones_like(values)], axis=1)

    def scored(head, heads, keys):
        q = take(head_columns(head - first, heads))
        stacked = jnp.concatenate([q[:, head_columns(h)] for h in range(heads)], axis=0)
        return lax.dot_general(
            stacked, keys, (((1,), (1,)), ((), ())), preferred_element_type=jnp.float32
        )

    def finished(head, heads, scores, values):
        scores = scores.reshape(heads, quota, -1) * unit + bias[...][None]
        weights = jnp.exp2(scores - jnp.max(scores, axis=2, keepdims=True))
        weights = weights.astype(jnp.bfloat16).reshape(heads * quota, -1)
        mixed = jnp.dot(weights, values, preferred_element_type=jnp.float32)
        totals = mixed[:, HEAD_SIZE:]
        inverse = pl.reciprocal(totals, approx=True)
        inverse = inverse * (2.0 - totals * inverse)
        mixed = (mixed[:, :HEAD_SIZE] * inverse).astype(jnp.bfloat16)
        for h in range(heads):
            result[:, head_columns(head - first + h)] = mixed[h * quota : (h + 1) * quota]

    steps = pieces(first, count)
    keys, values = key_head(first // GROUP)
    scores = scored(*steps[0], keys)
    for i, (head, heads) in enumerate(steps):
        own_values, later = values, None
        if i + 1 < len(steps):
            if steps[i + 1][0] // GROUP != head // GROUP:
                keys, values = key_head(steps[i + 1][0] // GROUP)
            later = scored(*steps[i + 1], keys)
        finished(head, heads, scores, own_values)
        scores = later


def early_kernel(blocks, chunks, rank_ref, *refs):
    kv_refs, far_ref, mate_ref = refs[: blocks - 1], refs[blocks - 1], refs[blocks]
    placed_refs = refs[blocks + 1 : blocks + 1 + len(chunks)]
    result, bias, rest = refs[blocks + 1 + len(chunks) :]
    count = sum(chunks)
    rank = rank_ref[0]
    make_bias(kv_refs, far_ref, mate_ref, bias, rank)
    choose_rest(0, count, lax.rem(rank, 2), far_ref, mate_ref, rest)

    def take(cols):
        found, at = [], 0
        for ref in placed_refs:
            start, stop = max(cols.start - at, 0), min(cols.stop - at, ref.shape[1])
            if start < stop:
                found.append(ref[:, start:stop])
            at += ref.shape[1]
        return found[0] if len(found) == 1 else jnp.concatenate(found, axis=1)

    attend_heads(0, count, [*kv_refs, rest], bias, take, result)


def late_kernel(blocks, first, rank_ref, *refs):
    kv_refs, far_ref, mate_ref = refs[: blocks - 1], refs[blocks - 1], refs[blocks]
    hot_ref, arrived_hbm, local_ref, early_ref, out_hbm = refs[blocks + 1 : blocks + 6]
    bias, rest, arrived, result, sems = refs[blocks + 6 :]
    count = QUERY_HEADS - first
    fetch = pltpu.make_async_copy(arrived_hbm, arrived, sems.at[0])
    fetch.start()
    rank = rank_ref[0]
    make_bias(kv_refs, far_ref, mate_ref, bias, rank)
    choose_rest(first, count, lax.rem(rank, 2), far_ref, mate_ref, rest)
    fetch.wait()
    early = pltpu.make_async_copy(early_ref, out_hbm.at[0, :, head_columns(0, first)], sems.at[1])
    early.start()

    def take(cols):
        return place_rows(hot_ref[...], arrived[:, cols], local_ref[:, cols])

    attend_heads(first, count, [*kv_refs, rest], bias, take, result)
    store = pltpu.make_async_copy(result, out_hbm.at[0, :, head_columns(first, count)], sems.at[2])
    store.start()
    early.wait()
    store.wait()


def attend(rank, hot, placed, arrived, local, kv_blocks):
    quota, width = arrived.shape
    blocks = len(kv_blocks) - 1
    chunks = [chunk.shape[1] // HEAD_SIZE for chunk in placed]
    first = sum(chunks)
    bias = pltpu.VMEM((quota, blocks * quota), jnp.float32)
    rest = pltpu.VMEM((quota, NOTE), jnp.bfloat16)
    own = pltpu.VMEM(arrived.shape, jnp.bfloat16)
    hints = dict(
        cost_estimate=pl.CostEstimate(flops=0, bytes_accessed=0, transcendentals=0),
        compiler_params=pltpu.CompilerParams(vmem_limit_bytes=VMEM_GRANT),
    )
    result = pl.pallas_call(
        functools.partial(early_kernel, blocks, chunks),
        in_specs=[SCALARS] + [WHOLE] * (len(kv_blocks) + len(placed)),
        out_specs=WHOLE,
        out_shape=jax.ShapeDtypeStruct((quota, first * HEAD_SIZE), jnp.bfloat16),
        scratch_shapes=[bias, rest],
        name="attend_early",
        **hints,
    )(rank, *kv_blocks, *placed)
    return pl.pallas_call(
        functools.partial(late_kernel, blocks, first),
        in_specs=[SCALARS] + [WHOLE] * (len(kv_blocks) + 1) + [ANYWHERE, WHOLE, ANYWHERE],
        out_specs=ANYWHERE,
        out_shape=jax.ShapeDtypeStruct((1, quota, QUERY_HEADS * HEAD_SIZE), jnp.bfloat16),
        scratch_shapes=[bias, rest, own, own, pltpu.SemaphoreType.DMA((3,))],
        name="attend_late",
        **hints,
    )(rank, *kv_blocks, hot, arrived, local, result)


def circular_tail(rows, later):
    quota = later.shape[0]
    return jnp.where(later[:, None], rows[quota:], rows[:quota])


def body(q_rows, k_rows, value_slot_rows, counts, doc_ids):
    quota = doc_ids.shape[1]
    rounds = lax.axis_size("ctx") // 4
    rank = lax.axis_index("ctx")
    own_count = counts[0, 0]

    later = quota + jnp.arange(quota, dtype=jnp.int32) < own_count
    kv_tail = jnp.concatenate(
        [circular_tail(k_rows[0], later), circular_tail(value_slot_rows[0], later)], axis=1
    )
    local_kv = jnp.concatenate([k_rows[0, :quota], value_slot_rows[0, :quota]], axis=1)
    kv_tail, later = lax.optimization_barrier((kv_tail, later))
    local_kv, later = lax.optimization_barrier((local_kv, later))
    arrived_kv = shifted(kv_tail, "dp", 1)
    q_tails = []
    first = 0
    for size in CHUNKS:
        q_tails.append(circular_tail(q_rows[0, :, head_columns(first, size)], later))
        first += size
    q_tails = lax.optimization_barrier(q_tails)
    arrived_q = [shifted(tail, "dp", 1) for tail in q_tails]

    shift = shifts_in(own_count, quota)
    local_q = stage_local(q_rows, quota)
    local_kv, local_q = lax.optimization_barrier((local_kv, local_q))
    own, hot = settle_kv(shift, doc_ids, arrived_kv, local_kv)

    kv_blocks, placed = [own], []
    carried = own
    for back in range(1, rounds + 1):
        carried = shifted(carried, "ctx", 2)
        kv_blocks.append(carried)
        if back < len(CHUNKS):
            placed.append(place_queries(hot, arrived_q[back - 1], local_q[back - 1]))
            carried, placed[-1] = lax.optimization_barrier((carried, placed[-1]))
        if back < rounds:
            kv_blocks.append(across_cores(carried))
    kv_blocks += [across_cores(carried), across_cores(own, (0,))]
    return attend(rank[None], hot, placed, arrived_q[-1], local_q[-1], kv_blocks)


def solution(mesh):
    return jax.shard_map(
        body,
        mesh=mesh,
        in_specs=(
            P("dp", "ctx", None),
            P("dp", "ctx", None),
            P("dp", "ctx", None),
            P("dp", "ctx"),
            P("dp", "ctx"),
        ),
        out_specs=P("dp", "ctx", None),
        check_vma=False,
    )
```

```python
import functools
import math

import jax
import jax.numpy as jnp
from jax import lax
from jax.experimental import pallas as pl
from jax.experimental.pallas import tpu as pltpu
from jax.sharding import PartitionSpec as P

QUERY_HEADS = 64
KEY_VALUE_HEADS = 8
HEAD_SIZE = 128
GROUP = QUERY_HEADS // KEY_VALUE_HEADS
KV_WIDTH = KEY_VALUE_HEADS * HEAD_SIZE
NOTE = 2 * KV_WIDTH
MASKED = -1e30
HALF = GROUP // 2
CHUNKS = (20, 26, 18)
VMEM_GRANT = 48 * 1024 * 1024

WHOLE = pl.BlockSpec(memory_space=pltpu.VMEM)
ANYWHERE = pl.BlockSpec(memory_space=pl.ANY)
SCALARS = pl.BlockSpec(memory_space=pltpu.SMEM)


def shifted(x, axis, steps):
    n = lax.axis_size(axis)
    return lax.ppermute(x, axis, [(i, i + steps) for i in range(n - steps)])


def across_cores(x, sources=(0, 1)):
    n = lax.axis_size("ctx")
    return lax.ppermute(x, "ctx", [(i, i ^ 1) for i in range(n) if i % 2 in sources])


def everyones(x, axis):
    n = lax.axis_size(axis)
    spread = jnp.broadcast_to(x[None], (n,) + x.shape)
    return lax.all_to_all(spread, axis, split_axis=0, concat_axis=0)


def shifts_in(own_count, quota):
    n = lax.axis_size("dp")
    replica = lax.axis_index("dp")
    if n > 4:
        all_counts = everyones(own_count[None], "dp")[:, 0]
        places = jnp.arange(n, dtype=jnp.int32)
        before = jnp.sum(jnp.where(places < replica, all_counts, 0))
        before_last = jnp.sum(jnp.where(places < replica - 1, all_counts, 0))
        return jnp.stack([before - replica * quota, before_last - (replica - 1) * quota])
    return jnp.stack([jnp.maximum(quota - own_count, 0), jnp.int32(0)])


def place_rows(hot, arrived, local):
    both = jnp.concatenate([arrived, local], axis=0)
    return jnp.dot(hot, both, preferred_element_type=jnp.float32).astype(jnp.bfloat16)


def settle_kernel(shift_ref, docs_ref, arrived_ref, local_ref, out_ref, hot_ref):
    quota = out_ref.shape[0]
    shift, shift_before = shift_ref[0], shift_ref[1]
    row = lax.broadcasted_iota(jnp.int32, (quota, quota), 0)
    col = lax.broadcasted_iota(jnp.int32, (quota, quota), 1)
    turned = row - shift_before
    turned = jnp.where(turned < 0, turned + quota, turned)
    hot_arrived = jnp.where((row < shift) & (col == turned), 1.0, 0.0)
    hot_local = jnp.where(col == row - shift, 1.0, 0.0)
    hot = jnp.concatenate([hot_arrived, hot_local], axis=1).astype(jnp.bfloat16)
    hot_ref[...] = hot
    out_ref[:, :NOTE] = place_rows(hot, arrived_ref[...], local_ref[...])
    docs = jnp.broadcast_to(docs_ref[...].astype(jnp.float32), (quota, quota))
    out_ref[:, NOTE:] = docs.astype(jnp.bfloat16)


def settle_kv(shift, docs, arrived, local):
    quota = arrived.shape[0]
    return pl.pallas_call(
        settle_kernel,
        in_specs=[SCALARS, WHOLE, WHOLE, WHOLE],
        out_specs=[WHOLE, WHOLE],
        out_shape=[
            jax.ShapeDtypeStruct((quota, NOTE + quota), jnp.bfloat16),
            jax.ShapeDtypeStruct((quota, 2 * quota), jnp.bfloat16),
        ],
        compiler_params=pltpu.CompilerParams(vmem_limit_bytes=VMEM_GRANT),
        name="settle_kv",
    )(shift, docs, arrived, local)


def block_ranks(rank, core, rounds):
    ranks = [rank]
    for back in range(1, rounds + 1):
        ranks.append(rank - 2 * back)
        if back < rounds:
            ranks.append(rank - 2 * back + jnp.where(core == 0, 1, -1))
    ranks.append(jnp.where(core == 0, rank - 2 * rounds + 1, rank - 1))
    return ranks


def head_columns(head, heads=1):
    return slice(head * HEAD_SIZE, (head + heads) * HEAD_SIZE)


def pieces(first, count):
    at, found = first, []
    while at < first + count:
        end = min(first + count, (at // GROUP + 1) * GROUP)
        heads = end - at
        if heads > HALF:
            heads = min(HALF, -(-heads // 2))
        found.append((at, heads))
        at += heads
    return found


def stage_kernel(q_hbm, *refs):
    targets, sems = refs[:-1], refs[-1]
    first, started = 0, []
    for i, target in enumerate(targets):
        quota, width = target.shape
        copy = pltpu.make_async_copy(
            q_hbm.at[0, 0:quota, first : first + width], target, sems.at[i]
        )
        copy.start()
        started.append(copy)
        first += width
    for copy in started:
        copy.wait()


def stage_local(q_rows, quota):
    return pl.pallas_call(
        stage_kernel,
        in_specs=[ANYWHERE],
        out_specs=[WHOLE] * len(CHUNKS),
        out_shape=[
            jax.ShapeDtypeStruct((quota, heads * HEAD_SIZE), jnp.bfloat16) for heads in CHUNKS
        ],
        scratch_shapes=[pltpu.SemaphoreType.DMA((len(CHUNKS),))],
        compiler_params=pltpu.CompilerParams(vmem_limit_bytes=VMEM_GRANT),
        name="stage_local",
    )(q_rows)


def place_kernel(hot_ref, arrived_ref, local_ref, placed_ref):
    for cols in (head_columns(*piece) for piece in pieces(0, placed_ref.shape[1] // HEAD_SIZE)):
        placed_ref[:, cols] = place_rows(hot_ref[...], arrived_ref[:, cols], local_ref[:, cols])


def place_queries(hot, arrived, local):
    return pl.pallas_call(
        place_kernel,
        in_specs=[WHOLE, WHOLE, WHOLE],
        out_specs=WHOLE,
        out_shape=jax.ShapeDtypeStruct(arrived.shape, jnp.bfloat16),
        compiler_params=pltpu.CompilerParams(vmem_limit_bytes=VMEM_GRANT),
        name="place_queries",
    )(hot, arrived, local)


def make_bias(kv_refs, far_ref, mate_ref, bias, rank):
    quota = bias.shape[0]
    core = lax.rem(rank, 2)
    row = lax.broadcasted_iota(jnp.int32, (quota, quota), 0)
    col = lax.broadcasted_iota(jnp.int32, (quota, quota), 1)
    note = slice(NOTE, NOTE + quota)
    q_docs = jnp.where(row == col, kv_refs[0][:, note].astype(jnp.float32), 0.0)
    q_docs = jnp.sum(q_docs, axis=1, keepdims=True)
    blocks = len(kv_refs) + 1
    for b, block_rank in enumerate(block_ranks(rank, core, (blocks - 1) // 2)):
        if b < blocks - 1:
            docs = kv_refs[b][:, note].astype(jnp.float32)
        else:
            far = far_ref[:, note].astype(jnp.float32)
            docs = jnp.where(core == 0, far, mate_ref[:, note].astype(jnp.float32))
        allowed = docs == q_docs
        allowed &= (col <= row) if b == 0 else (block_rank >= 0)
        bias[:, b * quota : (b + 1) * quota] = jnp.where(allowed, 0.0, MASKED)


def choose_rest(first, count, core, far_ref, mate_ref, rest):
    first_head, last_head = first // GROUP, (first + count - 1) // GROUP
    keys = head_columns(first_head, last_head - first_head + 1)
    values = slice(KV_WIDTH + keys.start, KV_WIDTH + keys.stop)

    @pl.when(core == 0)
    def _():
        rest[:, keys] = far_ref[:, keys]
        rest[:, values] = far_ref[:, values]

    @pl.when(core == 1)
    def _():
        rest[:, keys] = mate_ref[:, keys]
        rest[:, values] = mate_ref[:, values]


def attend_heads(first, count, kv_refs, bias, take, result):
    quota = bias.shape[0]
    unit = math.log2(math.e) / math.sqrt(HEAD_SIZE)

    def key_head(head):
        cols = head_columns(head)
        keys = jnp.concatenate([r[:, cols] for r in kv_refs], axis=0)
        cols = head_columns(KEY_VALUE_HEADS + head)
        values = jnp.concatenate([r[:, cols] for r in kv_refs], axis=0)
        return keys, jnp.concatenate([values, jnp.ones_like(values)], axis=1)

    def scored(head, heads, keys):
        q = take(head_columns(head - first, heads))
        stacked = jnp.concatenate([q[:, head_columns(h)] for h in range(heads)], axis=0)
        return lax.dot_general(
            stacked, keys, (((1,), (1,)), ((), ())), preferred_element_type=jnp.float32
        )

    def finished(head, heads, scores, values):
        scores = scores.reshape(heads, quota, -1) * unit + bias[...][None]
        weights = jnp.exp2(scores - jnp.max(scores, axis=2, keepdims=True))
        weights = weights.astype(jnp.bfloat16).reshape(heads * quota, -1)
        mixed = jnp.dot(weights, values, preferred_element_type=jnp.float32)
        totals = mixed[:, HEAD_SIZE:]
        inverse = pl.reciprocal(totals, approx=True)
        inverse = inverse * (2.0 - totals * inverse)
        mixed = (mixed[:, :HEAD_SIZE] * inverse).astype(jnp.bfloat16)
        for h in range(heads):
            result[:, head_columns(head - first + h)] = mixed[h * quota : (h + 1) * quota]

    steps = pieces(first, count)
    keys, values = key_head(first // GROUP)
    scores = scored(*steps[0], keys)
    for i, (head, heads) in enumerate(steps):
        own_values, later = values, None
        if i + 1 < len(steps):
            if steps[i + 1][0] // GROUP != head // GROUP:
                keys, values = key_head(steps[i + 1][0] // GROUP)
            later = scored(*steps[i + 1], keys)
        finished(head, heads, scores, own_values)
        scores = later


def early_kernel(blocks, chunks, rank_ref, *refs):
    kv_refs, far_ref, mate_ref = refs[: blocks - 1], refs[blocks - 1], refs[blocks]
    placed_refs = refs[blocks + 1 : blocks + 1 + len(chunks)]
    out_hbm, bias, rest, result, sem = refs[blocks + 1 + len(chunks) :]
    count = sum(chunks)
    rank = rank_ref[0]
    make_bias(kv_refs, far_ref, mate_ref, bias, rank)
    choose_rest(0, count, lax.rem(rank, 2), far_ref, mate_ref, rest)

    def take(cols):
        found, at = [], 0
        for ref in placed_refs:
            start, stop = max(cols.start - at, 0), min(cols.stop - at, ref.shape[1])
            if start < stop:
                found.append(ref[:, start:stop])
            at += ref.shape[1]
        return found[0] if len(found) == 1 else jnp.concatenate(found, axis=1)

    attend_heads(0, count, [*kv_refs, rest], bias, take, result)
    store = pltpu.make_async_copy(result, out_hbm.at[0, :, head_columns(0, count)], sem)
    store.start()
    store.wait()


def late_kernel(blocks, first, rank_ref, *refs):
    kv_refs, far_ref, mate_ref = refs[: blocks - 1], refs[blocks - 1], refs[blocks]
    hot_ref, arrived_hbm, local_ref, _, out_hbm = refs[blocks + 1 : blocks + 6]
    bias, rest, arrived, result, sems = refs[blocks + 6 :]
    count = QUERY_HEADS - first
    fetch = pltpu.make_async_copy(arrived_hbm, arrived, sems.at[0])
    fetch.start()
    rank = rank_ref[0]
    make_bias(kv_refs, far_ref, mate_ref, bias, rank)
    choose_rest(first, count, lax.rem(rank, 2), far_ref, mate_ref, rest)
    fetch.wait()

    def take(cols):
        return place_rows(hot_ref[...], arrived[:, cols], local_ref[:, cols])

    attend_heads(first, count, [*kv_refs, rest], bias, take, result)
    store = pltpu.make_async_copy(result, out_hbm.at[0, :, head_columns(first, count)], sems.at[1])
    store.start()
    store.wait()


def attend(rank, hot, placed, arrived, local, kv_blocks):
    quota, width = arrived.shape
    blocks = len(kv_blocks) - 1
    chunks = [chunk.shape[1] // HEAD_SIZE for chunk in placed]
    first = sum(chunks)
    bias = pltpu.VMEM((quota, blocks * quota), jnp.float32)
    rest = pltpu.VMEM((quota, NOTE), jnp.bfloat16)
    own = pltpu.VMEM(arrived.shape, jnp.bfloat16)
    hints = dict(
        cost_estimate=pl.CostEstimate(flops=0, bytes_accessed=0, transcendentals=0),
        compiler_params=pltpu.CompilerParams(vmem_limit_bytes=VMEM_GRANT),
    )
    whole = jax.ShapeDtypeStruct((1, quota, QUERY_HEADS * HEAD_SIZE), jnp.bfloat16)
    out = pl.pallas_call(
        functools.partial(early_kernel, blocks, chunks),
        in_specs=[SCALARS] + [WHOLE] * (len(kv_blocks) + len(placed)),
        out_specs=ANYWHERE,
        out_shape=whole,
        scratch_shapes=[
            bias,
            rest,
            pltpu.VMEM((quota, first * HEAD_SIZE), jnp.bfloat16),
            pltpu.SemaphoreType.DMA,
        ],
        name="attend_early",
        **hints,
    )(rank, *kv_blocks, *placed)
    operands = [rank, *kv_blocks, hot, arrived, local]
    return pl.pallas_call(
        functools.partial(late_kernel, blocks, first),
        in_specs=[SCALARS] + [WHOLE] * (len(kv_blocks) + 1) + [ANYWHERE, WHOLE, ANYWHERE],
        out_specs=ANYWHERE,
        out_shape=whole,
        input_output_aliases={len(operands): 0},
        scratch_shapes=[bias, rest, own, own, pltpu.SemaphoreType.DMA((2,))],
        name="attend_late",
        **hints,
    )(*operands, out)


def circular_tail(rows, later):
    quota = later.shape[0]
    return jnp.where(later[:, None], rows[quota:], rows[:quota])


def body(q_rows, k_rows, value_slot_rows, counts, doc_ids):
    quota = doc_ids.shape[1]
    rounds = lax.axis_size("ctx") // 4
    rank = lax.axis_index("ctx")
    own_count = counts[0, 0]

    later = quota + jnp.arange(quota, dtype=jnp.int32) < own_count
    kv_tail = jnp.concatenate(
        [circular_tail(k_rows[0], later), circular_tail(value_slot_rows[0], later)], axis=1
    )
    local_kv = jnp.concatenate([k_rows[0, :quota], value_slot_rows[0, :quota]], axis=1)
    kv_tail, later = lax.optimization_barrier((kv_tail, later))
    local_kv, later = lax.optimization_barrier((local_kv, later))
    arrived_kv = shifted(kv_tail, "dp", 1)
    q_tails = []
    first = 0
    for size in CHUNKS:
        q_tails.append(circular_tail(q_rows[0, :, head_columns(first, size)], later))
        first += size
    q_tails = lax.optimization_barrier(q_tails)
    arrived_q = [shifted(tail, "dp", 1) for tail in q_tails]

    shift = shifts_in(own_count, quota)
    local_q = stage_local(q_rows, quota)
    local_kv, local_q = lax.optimization_barrier((local_kv, local_q))
    own, hot = settle_kv(shift, doc_ids, arrived_kv, local_kv)

    kv_blocks, placed = [own], []
    carried = own
    for back in range(1, rounds + 1):
        carried = shifted(carried, "ctx", 2)
        kv_blocks.append(carried)
        if back < len(CHUNKS):
            placed.append(place_queries(hot, arrived_q[back - 1], local_q[back - 1]))
            carried, placed[-1] = lax.optimization_barrier((carried, placed[-1]))
        if back < rounds:
            kv_blocks.append(across_cores(carried))
    kv_blocks += [across_cores(carried), across_cores(own, (0,))]
    return attend(rank[None], hot, placed, arrived_q[-1], local_q[-1], kv_blocks)


def solution(mesh):
    return jax.shard_map(
        body,
        mesh=mesh,
        in_specs=(
            P("dp", "ctx", None),
            P("dp", "ctx", None),
            P("dp", "ctx", None),
            P("dp", "ctx"),
            P("dp", "ctx"),
        ),
        out_specs=P("dp", "ctx", None),
        check_vma=False,
    )
```

```python
import functools
import math

import jax
import jax.numpy as jnp
from jax import lax
from jax.experimental import pallas as pl
from jax.experimental.pallas import tpu as pltpu
from jax.sharding import PartitionSpec as P

QUERY_HEADS = 64
KEY_VALUE_HEADS = 8
HEAD_SIZE = 128
GROUP = QUERY_HEADS // KEY_VALUE_HEADS
KV_WIDTH = KEY_VALUE_HEADS * HEAD_SIZE
NOTE = 2 * KV_WIDTH
MASKED = -1e30
HALF = GROUP // 2
CHUNKS = (20, 24, 20)
VMEM_GRANT = 48 * 1024 * 1024

WHOLE = pl.BlockSpec(memory_space=pltpu.VMEM)
ANYWHERE = pl.BlockSpec(memory_space=pl.ANY)
SCALARS = pl.BlockSpec(memory_space=pltpu.SMEM)


def shifted(x, axis, steps):
    n = lax.axis_size(axis)
    return lax.ppermute(x, axis, [(i, i + steps) for i in range(n - steps)])


def across_cores(x, sources=(0, 1)):
    n = lax.axis_size("ctx")
    return lax.ppermute(x, "ctx", [(i, i ^ 1) for i in range(n) if i % 2 in sources])


def everyones(x, axis):
    n = lax.axis_size(axis)
    spread = jnp.broadcast_to(x[None], (n,) + x.shape)
    return lax.all_to_all(spread, axis, split_axis=0, concat_axis=0)


def shifts_in(own_count, quota):
    n = lax.axis_size("dp")
    replica = lax.axis_index("dp")
    if n > 4:
        all_counts = everyones(own_count[None], "dp")[:, 0]
        places = jnp.arange(n, dtype=jnp.int32)
        before = jnp.sum(jnp.where(places < replica, all_counts, 0))
        before_last = jnp.sum(jnp.where(places < replica - 1, all_counts, 0))
        return jnp.stack([before - replica * quota, before_last - (replica - 1) * quota])
    return jnp.stack([jnp.maximum(quota - own_count, 0), jnp.int32(0)])


def place_rows(hot, arrived, local):
    both = jnp.concatenate([arrived, local], axis=0)
    return jnp.dot(hot, both, preferred_element_type=jnp.float32).astype(jnp.bfloat16)


def settle_kernel(shift_ref, docs_ref, arrived_ref, local_ref, out_ref, hot_ref):
    quota = out_ref.shape[0]
    shift, shift_before = shift_ref[0], shift_ref[1]
    row = lax.broadcasted_iota(jnp.int32, (quota, quota), 0)
    col = lax.broadcasted_iota(jnp.int32, (quota, quota), 1)
    turned = row - shift_before
    turned = jnp.where(turned < 0, turned + quota, turned)
    hot_arrived = jnp.where((row < shift) & (col == turned), 1.0, 0.0)
    hot_local = jnp.where(col == row - shift, 1.0, 0.0)
    hot = jnp.concatenate([hot_arrived, hot_local], axis=1).astype(jnp.bfloat16)
    hot_ref[...] = hot
    out_ref[:, :NOTE] = place_rows(hot, arrived_ref[...], local_ref[...])
    docs = jnp.broadcast_to(docs_ref[...].astype(jnp.float32), (quota, quota))
    out_ref[:, NOTE:] = docs.astype(jnp.bfloat16)


def settle_kv(shift, docs, arrived, local):
    quota = arrived.shape[0]
    return pl.pallas_call(
        settle_kernel,
        in_specs=[SCALARS, WHOLE, WHOLE, WHOLE],
        out_specs=[WHOLE, WHOLE],
        out_shape=[
            jax.ShapeDtypeStruct((quota, NOTE + quota), jnp.bfloat16),
            jax.ShapeDtypeStruct((quota, 2 * quota), jnp.bfloat16),
        ],
        compiler_params=pltpu.CompilerParams(vmem_limit_bytes=VMEM_GRANT),
        name="settle_kv",
    )(shift, docs, arrived, local)


def block_ranks(rank, core, rounds):
    ranks = [rank]
    for back in range(1, rounds + 1):
        ranks.append(rank - 2 * back)
        if back < rounds:
            ranks.append(rank - 2 * back + jnp.where(core == 0, 1, -1))
    ranks.append(jnp.where(core == 0, rank - 2 * rounds + 1, rank - 1))
    return ranks


def head_columns(head, heads=1):
    return slice(head * HEAD_SIZE, (head + heads) * HEAD_SIZE)


def pieces(first, count):
    at, found = first, []
    while at < first + count:
        end = min(first + count, (at // GROUP + 1) * GROUP)
        heads = end - at
        if heads > HALF:
            heads = min(HALF, -(-heads // 2))
        found.append((at, heads))
        at += heads
    return found


def in_place(kernel, operands, out, more_out=(), more_specs=(), **arguments):
    specs = arguments.pop("in_specs") + [ANYWHERE]
    return pl.pallas_call(
        kernel,
        in_specs=specs,
        out_specs=[ANYWHERE, *more_specs],
        out_shape=[jax.ShapeDtypeStruct(out.shape, out.dtype), *more_out],
        input_output_aliases={len(operands): 0},
        cost_estimate=pl.CostEstimate(flops=0, bytes_accessed=0, transcendentals=0),
        compiler_params=pltpu.CompilerParams(vmem_limit_bytes=VMEM_GRANT),
        **arguments,
    )(*operands, out)


def place_kernel(first, hot_ref, arrived_ref, q_hbm, *refs):
    out_hbm, local, placed, in_sem, out_sem = refs[-5:]
    quota, width = arrived_ref.shape
    cols = head_columns(first, width // HEAD_SIZE)
    fetch = pltpu.make_async_copy(q_hbm.at[0, 0:quota, cols], local, in_sem)
    fetch.start()
    fetch.wait()
    for head, heads in pieces(first, width // HEAD_SIZE):
        own = head_columns(head - first, heads)
        placed[:, own] = place_rows(hot_ref[...], arrived_ref[:, own], local[:, own])
    store = pltpu.make_async_copy(placed, out_hbm.at[0, :, cols], out_sem)
    store.start()
    store.wait()


def place_queries(hot, arrived, q_rows, first, out):
    quota = arrived.shape[0]
    arguments = dict(
        in_specs=[WHOLE, WHOLE, ANYWHERE],
        scratch_shapes=[
            pltpu.VMEM(arrived.shape, jnp.bfloat16),
            pltpu.VMEM(arrived.shape, jnp.bfloat16),
            pltpu.SemaphoreType.DMA,
            pltpu.SemaphoreType.DMA,
        ],
        name="place_queries",
    )
    kernel = functools.partial(place_kernel, first)
    if out is not None:
        return in_place(kernel, [hot, arrived, q_rows], out, **arguments)[0]
    return pl.pallas_call(
        kernel,
        out_specs=ANYWHERE,
        out_shape=jax.ShapeDtypeStruct((1, quota, QUERY_HEADS * HEAD_SIZE), jnp.bfloat16),
        compiler_params=pltpu.CompilerParams(vmem_limit_bytes=VMEM_GRANT),
        **arguments,
    )(hot, arrived, q_rows)


def make_bias(kv_refs, far_ref, mate_ref, bias, rank):
    quota = bias.shape[0]
    core = lax.rem(rank, 2)
    row = lax.broadcasted_iota(jnp.int32, (quota, quota), 0)
    col = lax.broadcasted_iota(jnp.int32, (quota, quota), 1)
    note = slice(NOTE, NOTE + quota)
    q_docs = jnp.where(row == col, kv_refs[0][:, note].astype(jnp.float32), 0.0)
    q_docs = jnp.sum(q_docs, axis=1, keepdims=True)
    blocks = len(kv_refs) + 1
    for b, block_rank in enumerate(block_ranks(rank, core, (blocks - 1) // 2)):
        if b < blocks - 1:
            docs = kv_refs[b][:, note].astype(jnp.float32)
        else:
            far = far_ref[:, note].astype(jnp.float32)
            docs = jnp.where(core == 0, far, mate_ref[:, note].astype(jnp.float32))
        allowed = docs == q_docs
        allowed &= (col <= row) if b == 0 else (block_rank >= 0)
        bias[:, b * quota : (b + 1) * quota] = jnp.where(allowed, 0.0, MASKED)


def choose_rest(first, count, core, far_ref, mate_ref, rest):
    first_head, last_head = first // GROUP, (first + count - 1) // GROUP
    keys = head_columns(first_head, last_head - first_head + 1)
    values = slice(KV_WIDTH + keys.start, KV_WIDTH + keys.stop)

    @pl.when(core == 0)
    def _():
        rest[:, keys] = far_ref[:, keys]
        rest[:, values] = far_ref[:, values]

    @pl.when(core == 1)
    def _():
        rest[:, keys] = mate_ref[:, keys]
        rest[:, values] = mate_ref[:, values]


def attend_heads(first, count, kv_refs, bias, take, result):
    quota = bias.shape[0]
    unit = math.log2(math.e) / math.sqrt(HEAD_SIZE)

    def key_head(head):
        cols = head_columns(head)
        keys = jnp.concatenate([r[:, cols] for r in kv_refs], axis=0)
        cols = head_columns(KEY_VALUE_HEADS + head)
        values = jnp.concatenate([r[:, cols] for r in kv_refs], axis=0)
        return keys, jnp.concatenate([values, jnp.ones_like(values)], axis=1)

    def scored(head, heads, keys):
        q = take(head_columns(head - first, heads))
        stacked = jnp.concatenate([q[:, head_columns(h)] for h in range(heads)], axis=0)
        return lax.dot_general(
            stacked, keys, (((1,), (1,)), ((), ())), preferred_element_type=jnp.float32
        )

    def finished(head, heads, scores, values):
        scores = scores.reshape(heads, quota, -1) * unit + bias[...][None]
        weights = jnp.exp2(scores - jnp.max(scores, axis=2, keepdims=True))
        weights = weights.astype(jnp.bfloat16).reshape(heads * quota, -1)
        mixed = jnp.dot(weights, values, preferred_element_type=jnp.float32)
        totals = mixed[:, HEAD_SIZE:]
        inverse = pl.reciprocal(totals, approx=True)
        inverse = inverse * (2.0 - totals * inverse)
        mixed = (mixed[:, :HEAD_SIZE] * inverse).astype(jnp.bfloat16)
        for h in range(heads):
            result[:, head_columns(head - first + h)] = mixed[h * quota : (h + 1) * quota]

    steps = pieces(first, count)
    keys, values = key_head(first // GROUP)
    scores = scored(*steps[0], keys)
    for i, (head, heads) in enumerate(steps):
        own_values, later = values, None
        if i + 1 < len(steps):
            if steps[i + 1][0] // GROUP != head // GROUP:
                keys, values = key_head(steps[i + 1][0] // GROUP)
            later = scored(*steps[i + 1], keys)
        finished(head, heads, scores, own_values)
        scores = later


def early_kernel(blocks, count, rank_ref, *refs):
    kv_refs, far_ref, mate_ref = refs[: blocks - 1], refs[blocks - 1], refs[blocks]
    q_hbm, in_hbm, out_hbm, local, bias, rest, queries, result, sems = refs[blocks + 1 :]
    own, others = head_columns(0, count), head_columns(count, QUERY_HEADS - count)
    fetch = pltpu.make_async_copy(in_hbm.at[0, :, own], queries, sems.at[0])
    fetch.start()
    rank = rank_ref[0]
    make_bias(kv_refs, far_ref, mate_ref, bias, rank)
    choose_rest(0, count, lax.rem(rank, 2), far_ref, mate_ref, rest)
    fetch.wait()
    attend_heads(0, count, [*kv_refs, rest], bias, lambda cols: queries[:, cols], result)
    store = pltpu.make_async_copy(result, out_hbm.at[0, :, own], sems.at[1])
    store.start()
    ahead = pltpu.make_async_copy(q_hbm.at[0, 0 : bias.shape[0], others], local, sems.at[2])
    ahead.start()
    store.wait()
    ahead.wait()


def late_kernel(blocks, first, rank_ref, *refs):
    kv_refs, far_ref, mate_ref = refs[: blocks - 1], refs[blocks - 1], refs[blocks]
    hot_ref, arrived_hbm, local_ref, _, out_hbm = refs[blocks + 1 : blocks + 6]
    bias, rest, arrived, result, sems = refs[blocks + 6 :]
    count = QUERY_HEADS - first
    fetch = pltpu.make_async_copy(arrived_hbm, arrived, sems.at[0])
    fetch.start()
    rank = rank_ref[0]
    make_bias(kv_refs, far_ref, mate_ref, bias, rank)
    choose_rest(first, count, lax.rem(rank, 2), far_ref, mate_ref, rest)
    fetch.wait()

    def take(cols):
        return place_rows(hot_ref[...], arrived[:, cols], local_ref[:, cols])

    attend_heads(first, count, [*kv_refs, rest], bias, take, result)
    store = pltpu.make_async_copy(result, out_hbm.at[0, :, head_columns(first, count)], sems.at[1])
    store.start()
    store.wait()


def attend(rank, hot, arrived, q_rows, kv_blocks, out):
    quota, width = arrived.shape
    blocks = len(kv_blocks) - 1
    first = QUERY_HEADS - width // HEAD_SIZE
    bias = pltpu.VMEM((quota, blocks * quota), jnp.float32)
    rest = pltpu.VMEM((quota, NOTE), jnp.bfloat16)
    own = pltpu.VMEM(arrived.shape, jnp.bfloat16)
    others = pltpu.VMEM((quota, first * HEAD_SIZE), jnp.bfloat16)
    out, local = in_place(
        functools.partial(early_kernel, blocks, first),
        [rank, *kv_blocks, q_rows],
        out,
        more_out=[jax.ShapeDtypeStruct(arrived.shape, jnp.bfloat16)],
        more_specs=[WHOLE],
        in_specs=[SCALARS] + [WHOLE] * len(kv_blocks) + [ANYWHERE],
        scratch_shapes=[bias, rest, others, others, pltpu.SemaphoreType.DMA((3,))],
        name="attend_early",
    )
    return in_place(
        functools.partial(late_kernel, blocks, first),
        [rank, *kv_blocks, hot, arrived, local],
        out,
        in_specs=[SCALARS] + [WHOLE] * (len(kv_blocks) + 1) + [ANYWHERE, WHOLE],
        scratch_shapes=[bias, rest, own, own, pltpu.SemaphoreType.DMA((2,))],
        name="attend_late",
    )[0]


def circular_tail(rows, later):
    quota = later.shape[0]
    return jnp.where(later[:, None], rows[quota:], rows[:quota])


def body(q_rows, k_rows, value_slot_rows, counts, doc_ids):
    quota = doc_ids.shape[1]
    rounds = lax.axis_size("ctx") // 4
    rank = lax.axis_index("ctx")
    own_count = counts[0, 0]

    later = quota + jnp.arange(quota, dtype=jnp.int32) < own_count
    kv_tail = jnp.concatenate(
        [circular_tail(k_rows[0], later), circular_tail(value_slot_rows[0], later)], axis=1
    )
    local_kv = jnp.concatenate([k_rows[0, :quota], value_slot_rows[0, :quota]], axis=1)
    kv_tail, later = lax.optimization_barrier((kv_tail, later))
    local_kv, later = lax.optimization_barrier((local_kv, later))
    arrived_kv = shifted(kv_tail, "dp", 1)
    q_tails = []
    first = 0
    for size in CHUNKS:
        q_tails.append(circular_tail(q_rows[0, :, head_columns(first, size)], later))
        first += size
    q_tails = lax.optimization_barrier(q_tails)
    arrived_q = [shifted(tail, "dp", 1) for tail in q_tails]

    shift = shifts_in(own_count, quota)
    own, hot = settle_kv(shift, doc_ids, arrived_kv, local_kv)

    kv_blocks = [own]
    carried, out = own, None
    for back in range(1, rounds + 1):
        carried = shifted(carried, "ctx", 2)
        kv_blocks.append(carried)
        if back < len(CHUNKS):
            first = sum(CHUNKS[: back - 1])
            out = place_queries(hot, arrived_q[back - 1], q_rows, first, out)
            carried, out = lax.optimization_barrier((carried, out))
        if back < rounds:
            kv_blocks.append(across_cores(carried))
    kv_blocks += [across_cores(carried), across_cores(own, (0,))]
    return attend(rank[None], hot, arrived_q[-1], q_rows, kv_blocks, out)


def solution(mesh):
    return jax.shard_map(
        body,
        mesh=mesh,
        in_specs=(
            P("dp", "ctx", None),
            P("dp", "ctx", None),
            P("dp", "ctx", None),
            P("dp", "ctx"),
            P("dp", "ctx"),
        ),
        out_specs=P("dp", "ctx", None),
        check_vma=False,
    )
```

```python
import functools
import math

import jax
import jax.numpy as jnp
from jax import lax
from jax.experimental import pallas as pl
from jax.experimental.pallas import tpu as pltpu
from jax.sharding import PartitionSpec as P

QUERY_HEADS = 64
KEY_VALUE_HEADS = 8
HEAD_SIZE = 128
GROUP = QUERY_HEADS // KEY_VALUE_HEADS
KV_WIDTH = KEY_VALUE_HEADS * HEAD_SIZE
NOTE = 2 * KV_WIDTH
MASKED = -1e30
HALF = GROUP // 2
CHUNKS = (20, 26, 18)
VMEM_GRANT = 48 * 1024 * 1024

WHOLE = pl.BlockSpec(memory_space=pltpu.VMEM)
ANYWHERE = pl.BlockSpec(memory_space=pl.ANY)
SCALARS = pl.BlockSpec(memory_space=pltpu.SMEM)


def shifted(x, axis, steps):
    n = lax.axis_size(axis)
    return lax.ppermute(x, axis, [(i, i + steps) for i in range(n - steps)])


def across_cores(x, sources=(0, 1)):
    n = lax.axis_size("ctx")
    return lax.ppermute(x, "ctx", [(i, i ^ 1) for i in range(n) if i % 2 in sources])


def everyones(x, axis):
    n = lax.axis_size(axis)
    spread = jnp.broadcast_to(x[None], (n,) + x.shape)
    return lax.all_to_all(spread, axis, split_axis=0, concat_axis=0)


def shifts_in(own_count, quota):
    n = lax.axis_size("dp")
    replica = lax.axis_index("dp")
    if n > 4:
        all_counts = everyones(own_count[None], "dp")[:, 0]
        places = jnp.arange(n, dtype=jnp.int32)
        before = jnp.sum(jnp.where(places < replica, all_counts, 0))
        before_last = jnp.sum(jnp.where(places < replica - 1, all_counts, 0))
        return jnp.stack([before - replica * quota, before_last - (replica - 1) * quota])
    return jnp.stack([jnp.maximum(quota - own_count, 0), jnp.int32(0)])


def place_rows(hot, arrived, local):
    both = jnp.concatenate([arrived, local], axis=0)
    return jnp.dot(hot, both, preferred_element_type=jnp.float32).astype(jnp.bfloat16)


def settle_kernel(shift_ref, docs_ref, arrived_ref, local_ref, out_ref, hot_ref):
    quota = out_ref.shape[0]
    shift, shift_before = shift_ref[0], shift_ref[1]
    row = lax.broadcasted_iota(jnp.int32, (quota, quota), 0)
    col = lax.broadcasted_iota(jnp.int32, (quota, quota), 1)
    turned = row - shift_before
    turned = jnp.where(turned < 0, turned + quota, turned)
    hot_arrived = jnp.where((row < shift) & (col == turned), 1.0, 0.0)
    hot_local = jnp.where(col == row - shift, 1.0, 0.0)
    hot = jnp.concatenate([hot_arrived, hot_local], axis=1).astype(jnp.bfloat16)
    hot_ref[...] = hot
    out_ref[:, :NOTE] = place_rows(hot, arrived_ref[...], local_ref[...])
    docs = jnp.broadcast_to(docs_ref[...].astype(jnp.float32), (quota, quota))
    out_ref[:, NOTE:] = docs.astype(jnp.bfloat16)


def settle_kv(shift, docs, arrived, local):
    quota = arrived.shape[0]
    return pl.pallas_call(
        settle_kernel,
        in_specs=[SCALARS, WHOLE, WHOLE, WHOLE],
        out_specs=[WHOLE, WHOLE],
        out_shape=[
            jax.ShapeDtypeStruct((quota, NOTE + quota), jnp.bfloat16),
            jax.ShapeDtypeStruct((quota, 2 * quota), jnp.bfloat16),
        ],
        compiler_params=pltpu.CompilerParams(vmem_limit_bytes=VMEM_GRANT),
        name="settle_kv",
    )(shift, docs, arrived, local)


def block_ranks(rank, core, rounds):
    ranks = [rank]
    for back in range(1, rounds + 1):
        ranks.append(rank - 2 * back)
        if back < rounds:
            ranks.append(rank - 2 * back + jnp.where(core == 0, 1, -1))
    ranks.append(jnp.where(core == 0, rank - 2 * rounds + 1, rank - 1))
    return ranks


def head_columns(head, heads=1):
    return slice(head * HEAD_SIZE, (head + heads) * HEAD_SIZE)


def pieces(first, count):
    at, found = first, []
    while at < first + count:
        end = min(first + count, (at // GROUP + 1) * GROUP)
        heads = end - at
        if heads > HALF:
            heads = min(HALF, -(-heads // 2))
        found.append((at, heads))
        at += heads
    return found


def in_place(kernel, operands, out, more_out=(), more_specs=(), **arguments):
    specs = arguments.pop("in_specs") + [ANYWHERE]
    return pl.pallas_call(
        kernel,
        in_specs=specs,
        out_specs=[ANYWHERE, *more_specs],
        out_shape=[jax.ShapeDtypeStruct(out.shape, out.dtype), *more_out],
        input_output_aliases={len(operands): 0},
        cost_estimate=pl.CostEstimate(flops=0, bytes_accessed=0, transcendentals=0),
        compiler_params=pltpu.CompilerParams(vmem_limit_bytes=VMEM_GRANT),
        **arguments,
    )(*operands, out)


def place_kernel(first, hot_ref, arrived_ref, q_hbm, *refs):
    out_hbm, local, placed, in_sem, out_sem = refs[-5:]
    quota, width = arrived_ref.shape
    cols = head_columns(first, width // HEAD_SIZE)
    fetch = pltpu.make_async_copy(q_hbm.at[0, 0:quota, cols], local, in_sem)
    fetch.start()
    fetch.wait()
    for head, heads in pieces(first, width // HEAD_SIZE):
        own = head_columns(head - first, heads)
        placed[:, own] = place_rows(hot_ref[...], arrived_ref[:, own], local[:, own])
    store = pltpu.make_async_copy(placed, out_hbm.at[0, :, cols], out_sem)
    store.start()
    store.wait()


def place_queries(hot, arrived, q_rows, first, out):
    quota = arrived.shape[0]
    arguments = dict(
        in_specs=[WHOLE, WHOLE, ANYWHERE],
        scratch_shapes=[
            pltpu.VMEM(arrived.shape, jnp.bfloat16),
            pltpu.VMEM(arrived.shape, jnp.bfloat16),
            pltpu.SemaphoreType.DMA,
            pltpu.SemaphoreType.DMA,
        ],
        name="place_queries",
    )
    kernel = functools.partial(place_kernel, first)
    if out is not None:
        return in_place(kernel, [hot, arrived, q_rows], out, **arguments)[0]
    return pl.pallas_call(
        kernel,
        out_specs=ANYWHERE,
        out_shape=jax.ShapeDtypeStruct((1, quota, QUERY_HEADS * HEAD_SIZE), jnp.bfloat16),
        compiler_params=pltpu.CompilerParams(vmem_limit_bytes=VMEM_GRANT),
        **arguments,
    )(hot, arrived, q_rows)


def make_bias(kv_refs, far_ref, mate_ref, bias, rank):
    quota = bias.shape[0]
    core = lax.rem(rank, 2)
    row = lax.broadcasted_iota(jnp.int32, (quota, quota), 0)
    col = lax.broadcasted_iota(jnp.int32, (quota, quota), 1)
    note = slice(NOTE, NOTE + quota)
    q_docs = jnp.where(row == col, kv_refs[0][:, note].astype(jnp.float32), 0.0)
    q_docs = jnp.sum(q_docs, axis=1, keepdims=True)
    blocks = len(kv_refs) + 1
    for b, block_rank in enumerate(block_ranks(rank, core, (blocks - 1) // 2)):
        if b < blocks - 1:
            docs = kv_refs[b][:, note].astype(jnp.float32)
        else:
            far = far_ref[:, note].astype(jnp.float32)
            docs = jnp.where(core == 0, far, mate_ref[:, note].astype(jnp.float32))
        allowed = docs == q_docs
        allowed &= (col <= row) if b == 0 else (block_rank >= 0)
        bias[:, b * quota : (b + 1) * quota] = jnp.where(allowed, 0.0, MASKED)


def choose_rest(first, count, core, far_ref, mate_ref, rest):
    first_head, last_head = first // GROUP, (first + count - 1) // GROUP
    keys = head_columns(first_head, last_head - first_head + 1)
    values = slice(KV_WIDTH + keys.start, KV_WIDTH + keys.stop)

    @pl.when(core == 0)
    def _():
        rest[:, keys] = far_ref[:, keys]
        rest[:, values] = far_ref[:, values]

    @pl.when(core == 1)
    def _():
        rest[:, keys] = mate_ref[:, keys]
        rest[:, values] = mate_ref[:, values]


def attend_heads(first, steps, kv_refs, bias, take, result):
    quota = bias.shape[0]
    unit = math.log2(math.e) / math.sqrt(HEAD_SIZE)

    def key_head(head):
        cols = head_columns(head)
        keys = jnp.concatenate([r[:, cols] for r in kv_refs], axis=0)
        cols = head_columns(KEY_VALUE_HEADS + head)
        values = jnp.concatenate([r[:, cols] for r in kv_refs], axis=0)
        return keys, jnp.concatenate([values, jnp.ones_like(values)], axis=1)

    def scored(head, heads, keys):
        q = take(head_columns(head - first, heads))
        stacked = jnp.concatenate([q[:, head_columns(h)] for h in range(heads)], axis=0)
        return lax.dot_general(
            stacked, keys, (((1,), (1,)), ((), ())), preferred_element_type=jnp.float32
        )

    def finished(head, heads, scores, values):
        scores = scores.reshape(heads, quota, -1) * unit + bias[...][None]
        weights = jnp.exp2(scores - jnp.max(scores, axis=2, keepdims=True))
        weights = weights.astype(jnp.bfloat16).reshape(heads * quota, -1)
        mixed = jnp.dot(weights, values, preferred_element_type=jnp.float32)
        totals = mixed[:, HEAD_SIZE:]
        inverse = pl.reciprocal(totals, approx=True)
        inverse = inverse * (2.0 - totals * inverse)
        mixed = (mixed[:, :HEAD_SIZE] * inverse).astype(jnp.bfloat16)
        for h in range(heads):
            result[:, head_columns(head - first + h)] = mixed[h * quota : (h + 1) * quota]

    keys, values = key_head(steps[0][0] // GROUP)
    scores = scored(*steps[0], keys)
    for i, (head, heads) in enumerate(steps):
        own_values, later = values, None
        if i + 1 < len(steps):
            if steps[i + 1][0] // GROUP != head // GROUP:
                keys, values = key_head(steps[i + 1][0] // GROUP)
            later = scored(*steps[i + 1], keys)
        finished(head, heads, scores, own_values)
        scores = later


def early_kernel(blocks, count, rank_ref, *refs):
    kv_refs, far_ref, mate_ref = refs[: blocks - 1], refs[blocks - 1], refs[blocks]
    q_hbm, in_hbm, out_hbm, local, bias, rest, queries, result, sems = refs[blocks + 1 :]
    own, others = head_columns(0, count), head_columns(count, QUERY_HEADS - count)
    fetch = pltpu.make_async_copy(in_hbm.at[0, :, own], queries, sems.at[0])
    fetch.start()
    rank = rank_ref[0]
    make_bias(kv_refs, far_ref, mate_ref, bias, rank)
    choose_rest(0, count, lax.rem(rank, 2), far_ref, mate_ref, rest)
    fetch.wait()
    attend_heads(0, pieces(0, count), [*kv_refs, rest], bias, lambda cols: queries[:, cols], result)
    store = pltpu.make_async_copy(result, out_hbm.at[0, :, own], sems.at[1])
    store.start()
    ahead = pltpu.make_async_copy(q_hbm.at[0, 0 : bias.shape[0], others], local, sems.at[2])
    ahead.start()
    store.wait()
    ahead.wait()


def late_kernel(blocks, first, rank_ref, *refs):
    kv_refs, far_ref, mate_ref = refs[: blocks - 1], refs[blocks - 1], refs[blocks]
    hot_ref, arrived_hbm, local_ref, _, out_hbm = refs[blocks + 1 : blocks + 6]
    bias, rest, arrived, result, sems = refs[blocks + 6 :]
    count = QUERY_HEADS - first
    fetch = pltpu.make_async_copy(arrived_hbm, arrived, sems.at[0])
    fetch.start()
    rank = rank_ref[0]
    make_bias(kv_refs, far_ref, mate_ref, bias, rank)
    choose_rest(first, count, lax.rem(rank, 2), far_ref, mate_ref, rest)
    fetch.wait()

    def take(cols):
        return place_rows(hot_ref[...], arrived[:, cols], local_ref[:, cols])

    steps = sorted(pieces(first, count), key=lambda piece: -piece[1])
    attend_heads(first, steps, [*kv_refs, rest], bias, take, result)
    store = pltpu.make_async_copy(result, out_hbm.at[0, :, head_columns(first, count)], sems.at[1])
    store.start()
    store.wait()


def attend(rank, hot, arrived, q_rows, kv_blocks, out):
    quota, width = arrived.shape
    blocks = len(kv_blocks) - 1
    first = QUERY_HEADS - width // HEAD_SIZE
    bias = pltpu.VMEM((quota, blocks * quota), jnp.float32)
    rest = pltpu.VMEM((quota, NOTE), jnp.bfloat16)
    own = pltpu.VMEM(arrived.shape, jnp.bfloat16)
    others = pltpu.VMEM((quota, first * HEAD_SIZE), jnp.bfloat16)
    out, local = in_place(
        functools.partial(early_kernel, blocks, first),
        [rank, *kv_blocks, q_rows],
        out,
        more_out=[jax.ShapeDtypeStruct(arrived.shape, jnp.bfloat16)],
        more_specs=[WHOLE],
        in_specs=[SCALARS] + [WHOLE] * len(kv_blocks) + [ANYWHERE],
        scratch_shapes=[bias, rest, others, others, pltpu.SemaphoreType.DMA((3,))],
        name="attend_early",
    )
    return in_place(
        functools.partial(late_kernel, blocks, first),
        [rank, *kv_blocks, hot, arrived, local],
        out,
        in_specs=[SCALARS] + [WHOLE] * (len(kv_blocks) + 1) + [ANYWHERE, WHOLE],
        scratch_shapes=[bias, rest, own, own, pltpu.SemaphoreType.DMA((2,))],
        name="attend_late",
    )[0]


def circular_tail(rows, later):
    quota = later.shape[0]
    return jnp.where(later[:, None], rows[quota:], rows[:quota])


def body(q_rows, k_rows, value_slot_rows, counts, doc_ids):
    quota = doc_ids.shape[1]
    rounds = lax.axis_size("ctx") // 4
    rank = lax.axis_index("ctx")
    own_count = counts[0, 0]

    later = quota + jnp.arange(quota, dtype=jnp.int32) < own_count
    kv_tail = jnp.concatenate(
        [circular_tail(k_rows[0], later), circular_tail(value_slot_rows[0], later)], axis=1
    )
    local_kv = jnp.concatenate([k_rows[0, :quota], value_slot_rows[0, :quota]], axis=1)
    kv_tail, later = lax.optimization_barrier((kv_tail, later))
    local_kv, later = lax.optimization_barrier((local_kv, later))
    arrived_kv = shifted(kv_tail, "dp", 1)
    q_tails = []
    first = 0
    for size in CHUNKS:
        q_tails.append(circular_tail(q_rows[0, :, head_columns(first, size)], later))
        first += size
    q_tails = lax.optimization_barrier(q_tails)
    arrived_q = [shifted(tail, "dp", 1) for tail in q_tails]

    shift = shifts_in(own_count, quota)
    own, hot = settle_kv(shift, doc_ids, arrived_kv, local_kv)

    kv_blocks = [own]
    carried, out = own, None
    for back in range(1, rounds + 1):
        carried = shifted(carried, "ctx", 2)
        kv_blocks.append(carried)
        if back < len(CHUNKS):
            first, arrived = sum(CHUNKS[: back - 1]), arrived_q[back - 1]
            if back < rounds:
                out = place_queries(hot, arrived, q_rows, first, out)
                carried, out = lax.optimization_barrier((carried, out))
            else:
                carried, arrived = lax.optimization_barrier((carried, arrived))
                out = place_queries(hot, arrived, q_rows, first, out)
        if back < rounds:
            kv_blocks.append(across_cores(carried))
    kv_blocks += [across_cores(carried), across_cores(own, (0,))]
    return attend(rank[None], hot, arrived_q[-1], q_rows, kv_blocks, out)


def solution(mesh):
    return jax.shard_map(
        body,
        mesh=mesh,
        in_specs=(
            P("dp", "ctx", None),
            P("dp", "ctx", None),
            P("dp", "ctx", None),
            P("dp", "ctx"),
            P("dp", "ctx"),
        ),
        out_specs=P("dp", "ctx", None),
        check_vma=False,
    )
```

```python
import functools
import math

import jax
import jax.numpy as jnp
from jax import lax
from jax.experimental import pallas as pl
from jax.experimental.pallas import tpu as pltpu
from jax.sharding import PartitionSpec as P

QUERY_HEADS = 64
KEY_VALUE_HEADS = 8
HEAD_SIZE = 128
GROUP = QUERY_HEADS // KEY_VALUE_HEADS
KV_WIDTH = KEY_VALUE_HEADS * HEAD_SIZE
NOTE = 2 * KV_WIDTH
MASKED = -1e30
HALF = GROUP // 2
CHUNKS = (20, 26, 18)
VMEM_GRANT = 48 * 1024 * 1024

WHOLE = pl.BlockSpec(memory_space=pltpu.VMEM)
ANYWHERE = pl.BlockSpec(memory_space=pl.ANY)
SCALARS = pl.BlockSpec(memory_space=pltpu.SMEM)


def shifted(x, axis, steps):
    n = lax.axis_size(axis)
    return lax.ppermute(x, axis, [(i, i + steps) for i in range(n - steps)])


def across_cores(x, sources=(0, 1)):
    n = lax.axis_size("ctx")
    return lax.ppermute(x, "ctx", [(i, i ^ 1) for i in range(n) if i % 2 in sources])


def everyones(x, axis):
    n = lax.axis_size(axis)
    spread = jnp.broadcast_to(x[None], (n,) + x.shape)
    return lax.all_to_all(spread, axis, split_axis=0, concat_axis=0)


def shifts_in(own_count, quota):
    n = lax.axis_size("dp")
    replica = lax.axis_index("dp")
    if n > 4:
        all_counts = everyones(own_count[None], "dp")[:, 0]
        places = jnp.arange(n, dtype=jnp.int32)
        before = jnp.sum(jnp.where(places < replica, all_counts, 0))
        before_last = jnp.sum(jnp.where(places < replica - 1, all_counts, 0))
        return jnp.stack([before - replica * quota, before_last - (replica - 1) * quota])
    return jnp.stack([jnp.maximum(quota - own_count, 0), jnp.int32(0)])


def place_rows(hot, arrived, local):
    both = jnp.concatenate([arrived, local], axis=0)
    return jnp.dot(hot, both, preferred_element_type=jnp.float32).astype(jnp.bfloat16)


def settle_kernel(shift_ref, docs_ref, arrived_ref, local_ref, out_ref, hot_ref):
    quota = out_ref.shape[0]
    shift, shift_before = shift_ref[0], shift_ref[1]
    row = lax.broadcasted_iota(jnp.int32, (quota, quota), 0)
    col = lax.broadcasted_iota(jnp.int32, (quota, quota), 1)
    turned = row - shift_before
    turned = jnp.where(turned < 0, turned + quota, turned)
    hot_arrived = jnp.where((row < shift) & (col == turned), 1.0, 0.0)
    hot_local = jnp.where(col == row - shift, 1.0, 0.0)
    hot = jnp.concatenate([hot_arrived, hot_local], axis=1).astype(jnp.bfloat16)
    hot_ref[...] = hot
    out_ref[:, :NOTE] = place_rows(hot, arrived_ref[...], local_ref[...])
    docs = jnp.broadcast_to(docs_ref[...].astype(jnp.float32), (quota, quota))
    out_ref[:, NOTE:] = docs.astype(jnp.bfloat16)


def settle_kv(shift, docs, arrived, local):
    quota = arrived.shape[0]
    return pl.pallas_call(
        settle_kernel,
        in_specs=[SCALARS, WHOLE, WHOLE, WHOLE],
        out_specs=[WHOLE, WHOLE],
        out_shape=[
            jax.ShapeDtypeStruct((quota, NOTE + quota), jnp.bfloat16),
            jax.ShapeDtypeStruct((quota, 2 * quota), jnp.bfloat16),
        ],
        compiler_params=pltpu.CompilerParams(vmem_limit_bytes=VMEM_GRANT),
        name="settle_kv",
    )(shift, docs, arrived, local)


def block_ranks(rank, core, rounds):
    ranks = [rank]
    for back in range(1, rounds + 1):
        ranks.append(rank - 2 * back)
        if back < rounds:
            ranks.append(rank - 2 * back + jnp.where(core == 0, 1, -1))
    ranks.append(jnp.where(core == 0, rank - 2 * rounds + 1, rank - 1))
    return ranks


def head_columns(head, heads=1):
    return slice(head * HEAD_SIZE, (head + heads) * HEAD_SIZE)


def pieces(first, count):
    at, found = first, []
    while at < first + count:
        end = min(first + count, (at // GROUP + 1) * GROUP)
        heads = end - at
        if heads > HALF:
            heads = min(HALF, -(-heads // 2))
        found.append((at, heads))
        at += heads
    return found


def in_place(kernel, operands, out, more_out=(), more_specs=(), **arguments):
    specs = arguments.pop("in_specs") + [ANYWHERE]
    return pl.pallas_call(
        kernel,
        in_specs=specs,
        out_specs=[ANYWHERE, *more_specs],
        out_shape=[jax.ShapeDtypeStruct(out.shape, out.dtype), *more_out],
        input_output_aliases={len(operands): 0},
        cost_estimate=pl.CostEstimate(flops=0, bytes_accessed=0, transcendentals=0),
        compiler_params=pltpu.CompilerParams(vmem_limit_bytes=VMEM_GRANT),
        **arguments,
    )(*operands, out)


def place_kernel(first, hot_ref, arrived_ref, q_hbm, *refs):
    out_hbm, local, placed, in_sem, out_sem = refs[-5:]
    quota, width = arrived_ref.shape
    cols = head_columns(first, width // HEAD_SIZE)
    fetch = pltpu.make_async_copy(q_hbm.at[0, 0:quota, cols], local, in_sem)
    fetch.start()
    fetch.wait()
    for head, heads in pieces(first, width // HEAD_SIZE):
        own = head_columns(head - first, heads)
        placed[:, own] = place_rows(hot_ref[...], arrived_ref[:, own], local[:, own])
    store = pltpu.make_async_copy(placed, out_hbm.at[0, :, cols], out_sem)
    store.start()
    store.wait()


def place_queries(hot, arrived, q_rows, first, out):
    quota = arrived.shape[0]
    arguments = dict(
        in_specs=[WHOLE, WHOLE, ANYWHERE],
        scratch_shapes=[
            pltpu.VMEM(arrived.shape, jnp.bfloat16),
            pltpu.VMEM(arrived.shape, jnp.bfloat16),
            pltpu.SemaphoreType.DMA,
            pltpu.SemaphoreType.DMA,
        ],
        name="place_queries",
    )
    kernel = functools.partial(place_kernel, first)
    if out is not None:
        return in_place(kernel, [hot, arrived, q_rows], out, **arguments)[0]
    return pl.pallas_call(
        kernel,
        out_specs=ANYWHERE,
        out_shape=jax.ShapeDtypeStruct((1, quota, QUERY_HEADS * HEAD_SIZE), jnp.bfloat16),
        compiler_params=pltpu.CompilerParams(vmem_limit_bytes=VMEM_GRANT),
        **arguments,
    )(hot, arrived, q_rows)


def place_soon_kernel(first, hot_ref, arrived_ref, q_hbm, placed_ref, local, sem):
    quota, width = arrived_ref.shape
    fetch = pltpu.make_async_copy(
        q_hbm.at[0, 0:quota, head_columns(first, width // HEAD_SIZE)], local, sem
    )
    fetch.start()
    fetch.wait()
    for head, heads in pieces(first, width // HEAD_SIZE):
        own = head_columns(head - first, heads)
        placed_ref[:, own] = place_rows(hot_ref[...], arrived_ref[:, own], local[:, own])


def place_soon(hot, arrived, q_rows, first):
    return pl.pallas_call(
        functools.partial(place_soon_kernel, first),
        in_specs=[WHOLE, WHOLE, ANYWHERE],
        out_specs=WHOLE,
        out_shape=jax.ShapeDtypeStruct(arrived.shape, jnp.bfloat16),
        scratch_shapes=[pltpu.VMEM(arrived.shape, jnp.bfloat16), pltpu.SemaphoreType.DMA],
        compiler_params=pltpu.CompilerParams(vmem_limit_bytes=VMEM_GRANT),
        name="place_soon",
    )(hot, arrived, q_rows)


def make_bias(kv_refs, far_ref, mate_ref, bias, rank):
    quota = bias.shape[0]
    core = lax.rem(rank, 2)
    row = lax.broadcasted_iota(jnp.int32, (quota, quota), 0)
    col = lax.broadcasted_iota(jnp.int32, (quota, quota), 1)
    note = slice(NOTE, NOTE + quota)
    q_docs = jnp.where(row == col, kv_refs[0][:, note].astype(jnp.float32), 0.0)
    q_docs = jnp.sum(q_docs, axis=1, keepdims=True)
    blocks = len(kv_refs) + 1
    for b, block_rank in enumerate(block_ranks(rank, core, (blocks - 1) // 2)):
        if b < blocks - 1:
            docs = kv_refs[b][:, note].astype(jnp.float32)
        else:
            far = far_ref[:, note].astype(jnp.float32)
            docs = jnp.where(core == 0, far, mate_ref[:, note].astype(jnp.float32))
        allowed = docs == q_docs
        allowed &= (col <= row) if b == 0 else (block_rank >= 0)
        bias[:, b * quota : (b + 1) * quota] = jnp.where(allowed, 0.0, MASKED)


def choose_rest(first, count, core, far_ref, mate_ref, rest):
    first_head, last_head = first // GROUP, (first + count - 1) // GROUP
    keys = head_columns(first_head, last_head - first_head + 1)
    values = slice(KV_WIDTH + keys.start, KV_WIDTH + keys.stop)

    @pl.when(core == 0)
    def _():
        rest[:, keys] = far_ref[:, keys]
        rest[:, values] = far_ref[:, values]

    @pl.when(core == 1)
    def _():
        rest[:, keys] = mate_ref[:, keys]
        rest[:, values] = mate_ref[:, values]


def attend_heads(first, steps, kv_refs, bias, take, result):
    quota = bias.shape[0]
    unit = math.log2(math.e) / math.sqrt(HEAD_SIZE)

    def key_head(head):
        cols = head_columns(head)
        keys = jnp.concatenate([r[:, cols] for r in kv_refs], axis=0)
        cols = head_columns(KEY_VALUE_HEADS + head)
        values = jnp.concatenate([r[:, cols] for r in kv_refs], axis=0)
        return keys, jnp.concatenate([values, jnp.ones_like(values)], axis=1)

    def scored(head, heads, keys):
        q = take(head_columns(head - first, heads))
        stacked = jnp.concatenate([q[:, head_columns(h)] for h in range(heads)], axis=0)
        return lax.dot_general(
            stacked, keys, (((1,), (1,)), ((), ())), preferred_element_type=jnp.float32
        )

    def finished(head, heads, scores, values):
        scores = scores.reshape(heads, quota, -1) * unit + bias[...][None]
        weights = jnp.exp2(scores - jnp.max(scores, axis=2, keepdims=True))
        weights = weights.astype(jnp.bfloat16).reshape(heads * quota, -1)
        mixed = jnp.dot(weights, values, preferred_element_type=jnp.float32)
        totals = mixed[:, HEAD_SIZE:]
        inverse = pl.reciprocal(totals, approx=True)
        inverse = inverse * (2.0 - totals * inverse)
        mixed = (mixed[:, :HEAD_SIZE] * inverse).astype(jnp.bfloat16)
        for h in range(heads):
            result[:, head_columns(head - first + h)] = mixed[h * quota : (h + 1) * quota]

    keys, values = key_head(steps[0][0] // GROUP)
    scores = scored(*steps[0], keys)
    for i, (head, heads) in enumerate(steps):
        own_values, later = values, None
        if i + 1 < len(steps):
            if steps[i + 1][0] // GROUP != head // GROUP:
                keys, values = key_head(steps[i + 1][0] // GROUP)
            later = scored(*steps[i + 1], keys)
        finished(head, heads, scores, own_values)
        scores = later


def early_kernel(blocks, ahead_count, rank_ref, *refs):
    kv_refs, far_ref, mate_ref = refs[: blocks - 1], refs[blocks - 1], refs[blocks]
    placed_ref, q_hbm, in_hbm, out_hbm, local = refs[blocks + 1 : blocks + 6]
    bias, rest, queries, result, sems = refs[blocks + 6 :]
    count = ahead_count + placed_ref.shape[1] // HEAD_SIZE
    own, others = head_columns(0, count), head_columns(count, QUERY_HEADS - count)
    fetch = pltpu.make_async_copy(in_hbm.at[0, :, head_columns(0, ahead_count)], queries, sems.at[0])
    fetch.start()
    rank = rank_ref[0]
    make_bias(kv_refs, far_ref, mate_ref, bias, rank)
    choose_rest(0, count, lax.rem(rank, 2), far_ref, mate_ref, rest)
    fetch.wait()
    edge = queries.shape[1]

    def take(cols):
        if cols.stop <= edge:
            return queries[:, cols]
        if cols.start >= edge:
            return placed_ref[:, cols.start - edge : cols.stop - edge]
        halves = queries[:, cols.start : edge], placed_ref[:, 0 : cols.stop - edge]
        return jnp.concatenate(halves, axis=1)

    attend_heads(0, pieces(0, count), [*kv_refs, rest], bias, take, result)
    store = pltpu.make_async_copy(result, out_hbm.at[0, :, own], sems.at[1])
    store.start()
    ahead = pltpu.make_async_copy(q_hbm.at[0, 0 : bias.shape[0], others], local, sems.at[2])
    ahead.start()
    store.wait()
    ahead.wait()


def late_kernel(blocks, first, rank_ref, *refs):
    kv_refs, far_ref, mate_ref = refs[: blocks - 1], refs[blocks - 1], refs[blocks]
    hot_ref, arrived_hbm, local_ref, _, out_hbm = refs[blocks + 1 : blocks + 6]
    bias, rest, arrived, result, sems = refs[blocks + 6 :]
    count = QUERY_HEADS - first
    fetch = pltpu.make_async_copy(arrived_hbm, arrived, sems.at[0])
    fetch.start()
    rank = rank_ref[0]
    make_bias(kv_refs, far_ref, mate_ref, bias, rank)
    choose_rest(first, count, lax.rem(rank, 2), far_ref, mate_ref, rest)
    fetch.wait()

    def take(cols):
        return place_rows(hot_ref[...], arrived[:, cols], local_ref[:, cols])

    steps = sorted(pieces(first, count), key=lambda piece: -piece[1])
    attend_heads(first, steps, [*kv_refs, rest], bias, take, result)
    store = pltpu.make_async_copy(result, out_hbm.at[0, :, head_columns(first, count)], sems.at[1])
    store.start()
    store.wait()


def attend(rank, hot, placed, arrived, q_rows, kv_blocks, out):
    quota, width = arrived.shape
    blocks = len(kv_blocks) - 1
    first = QUERY_HEADS - width // HEAD_SIZE
    bias = pltpu.VMEM((quota, blocks * quota), jnp.float32)
    rest = pltpu.VMEM((quota, NOTE), jnp.bfloat16)
    own = pltpu.VMEM(arrived.shape, jnp.bfloat16)
    others = pltpu.VMEM((quota, first * HEAD_SIZE), jnp.bfloat16)
    ahead = pltpu.VMEM((quota, first * HEAD_SIZE - placed.shape[1]), jnp.bfloat16)
    out, local = in_place(
        functools.partial(early_kernel, blocks, first - placed.shape[1] // HEAD_SIZE),
        [rank, *kv_blocks, placed, q_rows],
        out,
        more_out=[jax.ShapeDtypeStruct(arrived.shape, jnp.bfloat16)],
        more_specs=[WHOLE],
        in_specs=[SCALARS] + [WHOLE] * (len(kv_blocks) + 1) + [ANYWHERE],
        scratch_shapes=[bias, rest, ahead, others, pltpu.SemaphoreType.DMA((3,))],
        name="attend_early",
    )
    return in_place(
        functools.partial(late_kernel, blocks, first),
        [rank, *kv_blocks, hot, arrived, local],
        out,
        in_specs=[SCALARS] + [WHOLE] * (len(kv_blocks) + 1) + [ANYWHERE, WHOLE],
        scratch_shapes=[bias, rest, own, own, pltpu.SemaphoreType.DMA((2,))],
        name="attend_late",
    )[0]


def circular_tail(rows, later):
    quota = later.shape[0]
    return jnp.where(later[:, None], rows[quota:], rows[:quota])


def body(q_rows, k_rows, value_slot_rows, counts, doc_ids):
    quota = doc_ids.shape[1]
    rounds = lax.axis_size("ctx") // 4
    rank = lax.axis_index("ctx")
    own_count = counts[0, 0]

    later = quota + jnp.arange(quota, dtype=jnp.int32) < own_count
    kv_tail = jnp.concatenate(
        [circular_tail(k_rows[0], later), circular_tail(value_slot_rows[0], later)], axis=1
    )
    local_kv = jnp.concatenate([k_rows[0, :quota], value_slot_rows[0, :quota]], axis=1)
    kv_tail, later = lax.optimization_barrier((kv_tail, later))
    local_kv, later = lax.optimization_barrier((local_kv, later))
    arrived_kv = shifted(kv_tail, "dp", 1)
    q_tails = []
    first = 0
    for size in CHUNKS:
        q_tails.append(circular_tail(q_rows[0, :, head_columns(first, size)], later))
        first += size
    q_tails = lax.optimization_barrier(q_tails)
    arrived_q = [shifted(tail, "dp", 1) for tail in q_tails]

    shift = shifts_in(own_count, quota)
    own, hot = settle_kv(shift, doc_ids, arrived_kv, local_kv)

    swapped = [across_cores(own, (0,))]
    same_core = []
    carried, out = own, None
    for back in range(1, rounds + 1):
        carried = shifted(carried, "ctx", 2)
        same_core.append(carried)
        if back < len(CHUNKS):
            first, arrived = sum(CHUNKS[: back - 1]), arrived_q[back - 1]
            if back < min(rounds, len(CHUNKS) - 1):
                out = place_queries(hot, arrived, q_rows, first, out)
                carried, out = lax.optimization_barrier((carried, out))
            else:
                placed = place_soon(hot, arrived, q_rows, first)
                carried, placed = lax.optimization_barrier((carried, placed))
        swapped.append(across_cores(carried))
    mate, *others = swapped
    kv_blocks = [own]
    for same, other in zip(same_core, others):
        kv_blocks += [same, other]
    kv_blocks.append(mate)
    return attend(rank[None], hot, placed, arrived_q[-1], q_rows, kv_blocks, out)


def solution(mesh):
    return jax.shard_map(
        body,
        mesh=mesh,
        in_specs=(
            P("dp", "ctx", None),
            P("dp", "ctx", None),
            P("dp", "ctx", None),
            P("dp", "ctx"),
            P("dp", "ctx"),
        ),
        out_specs=P("dp", "ctx", None),
        check_vma=False,
    )
```

```python
import functools
import math

import jax
import jax.numpy as jnp
from jax import lax
from jax.experimental import pallas as pl
from jax.experimental.pallas import tpu as pltpu
from jax.sharding import PartitionSpec as P

QUERY_HEADS = 64
KEY_VALUE_HEADS = 8
HEAD_SIZE = 128
GROUP = QUERY_HEADS // KEY_VALUE_HEADS
KV_WIDTH = KEY_VALUE_HEADS * HEAD_SIZE
NOTE = 2 * KV_WIDTH
MASKED = -1e30
HALF = GROUP // 2
CHUNKS = (20, 26, 18)
VMEM_GRANT = 48 * 1024 * 1024

WHOLE = pl.BlockSpec(memory_space=pltpu.VMEM)
ANYWHERE = pl.BlockSpec(memory_space=pl.ANY)
SCALARS = pl.BlockSpec(memory_space=pltpu.SMEM)


def shifted(x, axis, steps):
    n = lax.axis_size(axis)
    return lax.ppermute(x, axis, [(i, i + steps) for i in range(n - steps)])


def across_cores(x, sources=(0, 1)):
    n = lax.axis_size("ctx")
    return lax.ppermute(x, "ctx", [(i, i ^ 1) for i in range(n) if i % 2 in sources])


def everyones(x, axis):
    n = lax.axis_size(axis)
    spread = jnp.broadcast_to(x[None], (n,) + x.shape)
    return lax.all_to_all(spread, axis, split_axis=0, concat_axis=0)


def shifts_in(own_count, quota):
    n = lax.axis_size("dp")
    replica = lax.axis_index("dp")
    if n > 4:
        all_counts = everyones(own_count[None], "dp")[:, 0]
        places = jnp.arange(n, dtype=jnp.int32)
        before = jnp.sum(jnp.where(places < replica, all_counts, 0))
        before_last = jnp.sum(jnp.where(places < replica - 1, all_counts, 0))
        return jnp.stack([before - replica * quota, before_last - (replica - 1) * quota])
    return jnp.stack([jnp.maximum(quota - own_count, 0), jnp.int32(0)])


def place_rows(hot, arrived, local):
    both = jnp.concatenate([arrived, local], axis=0)
    return jnp.dot(hot, both, preferred_element_type=jnp.float32).astype(jnp.bfloat16)


def settle_kernel(shift_ref, docs_ref, arrived_ref, local_ref, out_ref, hot_ref):
    quota = out_ref.shape[0]
    shift, shift_before = shift_ref[0], shift_ref[1]
    row = lax.broadcasted_iota(jnp.int32, (quota, quota), 0)
    col = lax.broadcasted_iota(jnp.int32, (quota, quota), 1)
    turned = row - shift_before
    turned = jnp.where(turned < 0, turned + quota, turned)
    hot_arrived = jnp.where((row < shift) & (col == turned), 1.0, 0.0)
    hot_local = jnp.where(col == row - shift, 1.0, 0.0)
    hot = jnp.concatenate([hot_arrived, hot_local], axis=1).astype(jnp.bfloat16)
    hot_ref[...] = hot
    out_ref[:, :NOTE] = place_rows(hot, arrived_ref[...], local_ref[...])
    docs = jnp.broadcast_to(docs_ref[...].astype(jnp.float32), (quota, quota))
    out_ref[:, NOTE:] = docs.astype(jnp.bfloat16)


def settle_kv(shift, docs, arrived, local):
    quota = arrived.shape[0]
    return pl.pallas_call(
        settle_kernel,
        in_specs=[SCALARS, WHOLE, WHOLE, WHOLE],
        out_specs=[WHOLE, WHOLE],
        out_shape=[
            jax.ShapeDtypeStruct((quota, NOTE + quota), jnp.bfloat16),
            jax.ShapeDtypeStruct((quota, 2 * quota), jnp.bfloat16),
        ],
        compiler_params=pltpu.CompilerParams(vmem_limit_bytes=VMEM_GRANT),
        name="settle_kv",
    )(shift, docs, arrived, local)


def block_ranks(rank, core, rounds):
    ranks = [rank]
    for back in range(1, rounds + 1):
        ranks.append(rank - 2 * back)
        if back < rounds:
            ranks.append(rank - 2 * back + jnp.where(core == 0, 1, -1))
    ranks.append(jnp.where(core == 0, rank - 2 * rounds + 1, rank - 1))
    return ranks


def head_columns(head, heads=1):
    return slice(head * HEAD_SIZE, (head + heads) * HEAD_SIZE)


def pieces(first, count):
    at, found = first, []
    while at < first + count:
        end = min(first + count, (at // GROUP + 1) * GROUP)
        heads = end - at
        if heads > HALF:
            heads = min(HALF, -(-heads // 2))
        found.append((at, heads))
        at += heads
    return found


def in_place(kernel, operands, out, more_out=(), more_specs=(), **arguments):
    specs = arguments.pop("in_specs") + [ANYWHERE]
    return pl.pallas_call(
        kernel,
        in_specs=specs,
        out_specs=[ANYWHERE, *more_specs],
        out_shape=[jax.ShapeDtypeStruct(out.shape, out.dtype), *more_out],
        input_output_aliases={len(operands): 0},
        cost_estimate=pl.CostEstimate(flops=0, bytes_accessed=0, transcendentals=0),
        compiler_params=pltpu.CompilerParams(vmem_limit_bytes=VMEM_GRANT),
        **arguments,
    )(*operands, out)


def place_kernel(first, hot_ref, arrived_ref, q_hbm, *refs):
    out_hbm, local, placed, in_sem, out_sem = refs[-5:]
    quota, width = arrived_ref.shape
    cols = head_columns(first, width // HEAD_SIZE)
    fetch = pltpu.make_async_copy(q_hbm.at[0, 0:quota, cols], local, in_sem)
    fetch.start()
    fetch.wait()
    for head, heads in pieces(first, width // HEAD_SIZE):
        own = head_columns(head - first, heads)
        placed[:, own] = place_rows(hot_ref[...], arrived_ref[:, own], local[:, own])
    store = pltpu.make_async_copy(placed, out_hbm.at[0, :, cols], out_sem)
    store.start()
    store.wait()


def place_queries(hot, arrived, q_rows, first, out):
    quota = arrived.shape[0]
    arguments = dict(
        in_specs=[WHOLE, WHOLE, ANYWHERE],
        scratch_shapes=[
            pltpu.VMEM(arrived.shape, jnp.bfloat16),
            pltpu.VMEM(arrived.shape, jnp.bfloat16),
            pltpu.SemaphoreType.DMA,
            pltpu.SemaphoreType.DMA,
        ],
        name="place_queries",
    )
    kernel = functools.partial(place_kernel, first)
    if out is not None:
        return in_place(kernel, [hot, arrived, q_rows], out, **arguments)[0]
    return pl.pallas_call(
        kernel,
        out_specs=ANYWHERE,
        out_shape=jax.ShapeDtypeStruct((1, quota, QUERY_HEADS * HEAD_SIZE), jnp.bfloat16),
        compiler_params=pltpu.CompilerParams(vmem_limit_bytes=VMEM_GRANT),
        **arguments,
    )(hot, arrived, q_rows)


def place_soon_kernel(first, hot_ref, arrived_ref, q_hbm, placed_ref, local, sem):
    quota, width = arrived_ref.shape
    fetch = pltpu.make_async_copy(
        q_hbm.at[0, 0:quota, head_columns(first, width // HEAD_SIZE)], local, sem
    )
    fetch.start()
    fetch.wait()
    for head, heads in pieces(first, width // HEAD_SIZE):
        own = head_columns(head - first, heads)
        placed_ref[:, own] = place_rows(hot_ref[...], arrived_ref[:, own], local[:, own])


def place_soon(hot, arrived, q_rows, first):
    return pl.pallas_call(
        functools.partial(place_soon_kernel, first),
        in_specs=[WHOLE, WHOLE, ANYWHERE],
        out_specs=WHOLE,
        out_shape=jax.ShapeDtypeStruct(arrived.shape, jnp.bfloat16),
        scratch_shapes=[pltpu.VMEM(arrived.shape, jnp.bfloat16), pltpu.SemaphoreType.DMA],
        compiler_params=pltpu.CompilerParams(vmem_limit_bytes=VMEM_GRANT),
        name="place_soon",
    )(hot, arrived, q_rows)


def make_bias(kv_refs, far_ref, mate_ref, bias, rank):
    quota = bias.shape[0]
    core = lax.rem(rank, 2)
    row = lax.broadcasted_iota(jnp.int32, (quota, quota), 0)
    col = lax.broadcasted_iota(jnp.int32, (quota, quota), 1)
    note = slice(NOTE, NOTE + quota)
    q_docs = jnp.where(row == col, kv_refs[0][:, note].astype(jnp.float32), 0.0)
    q_docs = jnp.sum(q_docs, axis=1, keepdims=True)
    blocks = len(kv_refs) + 1
    for b, block_rank in enumerate(block_ranks(rank, core, (blocks - 1) // 2)):
        if b < blocks - 1:
            docs = kv_refs[b][:, note].astype(jnp.float32)
        else:
            far = far_ref[:, note].astype(jnp.float32)
            docs = jnp.where(core == 0, far, mate_ref[:, note].astype(jnp.float32))
        allowed = docs == q_docs
        allowed &= (col <= row) if b == 0 else (block_rank >= 0)
        bias[:, b * quota : (b + 1) * quota] = jnp.where(allowed, 0.0, MASKED)


def choose_rest(first, count, core, far_ref, mate_ref, rest):
    first_head, last_head = first // GROUP, (first + count - 1) // GROUP
    keys = head_columns(first_head, last_head - first_head + 1)
    values = slice(KV_WIDTH + keys.start, KV_WIDTH + keys.stop)

    @pl.when(core == 0)
    def _():
        rest[:, keys] = far_ref[:, keys]
        rest[:, values] = far_ref[:, values]

    @pl.when(core == 1)
    def _():
        rest[:, keys] = mate_ref[:, keys]
        rest[:, values] = mate_ref[:, values]


def attend_heads(first, steps, kv_refs, bias, take, result):
    quota = bias.shape[0]
    unit = math.log2(math.e) / math.sqrt(HEAD_SIZE)

    def key_head(head):
        cols = head_columns(head)
        keys = jnp.concatenate([r[:, cols] for r in kv_refs], axis=0)
        cols = head_columns(KEY_VALUE_HEADS + head)
        values = jnp.concatenate([r[:, cols] for r in kv_refs], axis=0)
        return keys, jnp.concatenate([values, jnp.ones_like(values)], axis=1)

    def scored(head, heads, keys):
        q = take(head_columns(head - first, heads))
        stacked = jnp.concatenate([q[:, head_columns(h)] for h in range(heads)], axis=0)
        return lax.dot_general(
            stacked, keys, (((1,), (1,)), ((), ())), preferred_element_type=jnp.float32
        )

    def finished(head, heads, scores, values):
        scores = scores.reshape(heads, quota, -1) * unit + bias[...][None]
        weights = jnp.exp2(scores - jnp.max(scores, axis=2, keepdims=True))
        weights = weights.astype(jnp.bfloat16).reshape(heads * quota, -1)
        mixed = jnp.dot(weights, values, preferred_element_type=jnp.float32)
        totals = mixed[:, HEAD_SIZE:]
        inverse = pl.reciprocal(totals, approx=True)
        inverse = inverse * (2.0 - totals * inverse)
        mixed = (mixed[:, :HEAD_SIZE] * inverse).astype(jnp.bfloat16)
        for h in range(heads):
            result[:, head_columns(head - first + h)] = mixed[h * quota : (h + 1) * quota]

    keys, values = key_head(steps[0][0] // GROUP)
    scores = scored(*steps[0], keys)
    for i, (head, heads) in enumerate(steps):
        own_values, later = values, None
        if i + 1 < len(steps):
            if steps[i + 1][0] // GROUP != head // GROUP:
                keys, values = key_head(steps[i + 1][0] // GROUP)
            later = scored(*steps[i + 1], keys)
        finished(head, heads, scores, own_values)
        scores = later


def early_kernel(blocks, ahead_count, rank_ref, *refs):
    kv_refs, far_ref, mate_ref = refs[: blocks - 1], refs[blocks - 1], refs[blocks]
    placed_ref, q_hbm, in_hbm, out_hbm, local = refs[blocks + 1 : blocks + 6]
    bias, rest, queries, result, sems = refs[blocks + 6 :]
    count = ahead_count + placed_ref.shape[1] // HEAD_SIZE
    own, others = head_columns(0, count), head_columns(count, QUERY_HEADS - count)
    fetch = pltpu.make_async_copy(in_hbm.at[0, :, head_columns(0, ahead_count)], queries, sems.at[0])
    fetch.start()
    rank = rank_ref[0]
    make_bias(kv_refs, far_ref, mate_ref, bias, rank)
    choose_rest(0, count, lax.rem(rank, 2), far_ref, mate_ref, rest)
    fetch.wait()
    edge = queries.shape[1]

    def take(cols):
        if cols.stop <= edge:
            return queries[:, cols]
        if cols.start >= edge:
            return placed_ref[:, cols.start - edge : cols.stop - edge]
        halves = queries[:, cols.start : edge], placed_ref[:, 0 : cols.stop - edge]
        return jnp.concatenate(halves, axis=1)

    attend_heads(0, pieces(0, count), [*kv_refs, rest], bias, take, result)
    store = pltpu.make_async_copy(result, out_hbm.at[0, :, own], sems.at[1])
    store.start()
    ahead = pltpu.make_async_copy(q_hbm.at[0, 0 : bias.shape[0], others], local, sems.at[2])
    ahead.start()
    store.wait()
    ahead.wait()


def late_kernel(blocks, first, rank_ref, *refs):
    kv_refs, far_ref, mate_ref = refs[: blocks - 1], refs[blocks - 1], refs[blocks]
    hot_ref, arrived_hbm, local_ref, _, out_hbm = refs[blocks + 1 : blocks + 6]
    bias, rest, arrived, result, sems = refs[blocks + 6 :]
    count = QUERY_HEADS - first
    fetch = pltpu.make_async_copy(arrived_hbm, arrived, sems.at[0])
    fetch.start()
    rank = rank_ref[0]
    make_bias(kv_refs, far_ref, mate_ref, bias, rank)
    choose_rest(first, count, lax.rem(rank, 2), far_ref, mate_ref, rest)
    fetch.wait()

    def take(cols):
        return place_rows(hot_ref[...], arrived[:, cols], local_ref[:, cols])

    steps = sorted(pieces(first, count), key=lambda piece: -piece[1])
    attend_heads(first, steps, [*kv_refs, rest], bias, take, result)
    store = pltpu.make_async_copy(result, out_hbm.at[0, :, head_columns(first, count)], sems.at[1])
    store.start()
    store.wait()


def attend(rank, hot, placed, arrived, q_rows, kv_blocks, out):
    quota, width = arrived.shape
    blocks = len(kv_blocks) - 1
    first = QUERY_HEADS - width // HEAD_SIZE
    bias = pltpu.VMEM((quota, blocks * quota), jnp.float32)
    rest = pltpu.VMEM((quota, NOTE), jnp.bfloat16)
    own = pltpu.VMEM(arrived.shape, jnp.bfloat16)
    others = pltpu.VMEM((quota, first * HEAD_SIZE), jnp.bfloat16)
    ahead = pltpu.VMEM((quota, first * HEAD_SIZE - placed.shape[1]), jnp.bfloat16)
    out, local = in_place(
        functools.partial(early_kernel, blocks, first - placed.shape[1] // HEAD_SIZE),
        [rank, *kv_blocks, placed, q_rows],
        out,
        more_out=[jax.ShapeDtypeStruct(arrived.shape, jnp.bfloat16)],
        more_specs=[WHOLE],
        in_specs=[SCALARS] + [WHOLE] * (len(kv_blocks) + 1) + [ANYWHERE],
        scratch_shapes=[bias, rest, ahead, others, pltpu.SemaphoreType.DMA((3,))],
        name="attend_early",
    )
    return in_place(
        functools.partial(late_kernel, blocks, first),
        [rank, *kv_blocks, hot, arrived, local],
        out,
        in_specs=[SCALARS] + [WHOLE] * (len(kv_blocks) + 1) + [ANYWHERE, WHOLE],
        scratch_shapes=[bias, rest, own, own, pltpu.SemaphoreType.DMA((2,))],
        name="attend_late",
    )[0]


def circular_tail(rows, later):
    quota = later.shape[0]
    return jnp.where(later[:, None], rows[quota:], rows[:quota])


def body(q_rows, k_rows, value_slot_rows, counts, doc_ids):
    quota = doc_ids.shape[1]
    rounds = lax.axis_size("ctx") // 4
    rank = lax.axis_index("ctx")
    own_count = counts[0, 0]

    later = quota + jnp.arange(quota, dtype=jnp.int32) < own_count
    kv_tail = jnp.concatenate(
        [circular_tail(k_rows[0], later), circular_tail(value_slot_rows[0], later)], axis=1
    )
    local_kv = jnp.concatenate([k_rows[0, :quota], value_slot_rows[0, :quota]], axis=1)
    kv_tail, later = lax.optimization_barrier((kv_tail, later))
    local_kv, later = lax.optimization_barrier((local_kv, later))
    arrived_kv = shifted(kv_tail, "dp", 1)
    q_tails = []
    first = 0
    for size in CHUNKS:
        q_tails.append(circular_tail(q_rows[0, :, head_columns(first, size)], later))
        first += size
    q_tails = lax.optimization_barrier(q_tails)
    arrived_q = [shifted(tail, "dp", 1) for tail in q_tails]

    shift = shifts_in(own_count, quota)
    own, hot = settle_kv(shift, doc_ids, arrived_kv, local_kv)

    swapped = [across_cores(own, (0,))]
    same_core = []
    carried, out = own, None
    for back in range(1, rounds + 1):
        carried = shifted(carried, "ctx", 2)
        same_core.append(carried)
        if back < len(CHUNKS):
            first, arrived = sum(CHUNKS[: back - 1]), arrived_q[back - 1]
            if back < min(rounds, len(CHUNKS) - 1):
                out = place_queries(hot, arrived, q_rows, first, out)
                carried, out = lax.optimization_barrier((carried, out))
            else:
                placed = place_soon(hot, arrived, q_rows, first)
                carried, placed, swapped = lax.optimization_barrier((carried, placed, swapped))
        swapped.append(across_cores(carried))
    mate, *others = swapped
    kv_blocks = [own]
    for same, other in zip(same_core, others):
        kv_blocks += [same, other]
    kv_blocks.append(mate)
    return attend(rank[None], hot, placed, arrived_q[-1], q_rows, kv_blocks, out)


def solution(mesh):
    return jax.shard_map(
        body,
        mesh=mesh,
        in_specs=(
            P("dp", "ctx", None),
            P("dp", "ctx", None),
            P("dp", "ctx", None),
            P("dp", "ctx"),
            P("dp", "ctx"),
        ),
        out_specs=P("dp", "ctx", None),
        check_vma=False,
    )
```

```python
import functools
import math

import jax
import jax.numpy as jnp
from jax import lax
from jax.experimental import pallas as pl
from jax.experimental.pallas import tpu as pltpu
from jax.sharding import PartitionSpec as P

QUERY_HEADS = 64
KEY_VALUE_HEADS = 8
HEAD_SIZE = 128
GROUP = QUERY_HEADS // KEY_VALUE_HEADS
KV_WIDTH = KEY_VALUE_HEADS * HEAD_SIZE
NOTE = 2 * KV_WIDTH
MASKED = -1e30
HALF = GROUP // 2
CHUNKS = (20, 24, 20)
VMEM_GRANT = 48 * 1024 * 1024

WHOLE = pl.BlockSpec(memory_space=pltpu.VMEM)
ANYWHERE = pl.BlockSpec(memory_space=pl.ANY)
SCALARS = pl.BlockSpec(memory_space=pltpu.SMEM)


def shifted(x, axis, steps):
    n = lax.axis_size(axis)
    return lax.ppermute(x, axis, [(i, i + steps) for i in range(n - steps)])


def across_cores(x, sources=(0, 1)):
    n = lax.axis_size("ctx")
    return lax.ppermute(x, "ctx", [(i, i ^ 1) for i in range(n) if i % 2 in sources])


def everyones(x, axis):
    n = lax.axis_size(axis)
    spread = jnp.broadcast_to(x[None], (n,) + x.shape)
    return lax.all_to_all(spread, axis, split_axis=0, concat_axis=0)


def shifts_in(own_count, quota):
    n = lax.axis_size("dp")
    replica = lax.axis_index("dp")
    if n > 4:
        all_counts = everyones(own_count[None], "dp")[:, 0]
        places = jnp.arange(n, dtype=jnp.int32)
        before = jnp.sum(jnp.where(places < replica, all_counts, 0))
        before_last = jnp.sum(jnp.where(places < replica - 1, all_counts, 0))
        return jnp.stack([before - replica * quota, before_last - (replica - 1) * quota])
    return jnp.stack([jnp.maximum(quota - own_count, 0), jnp.int32(0)])


def place_rows(hot, arrived, local):
    both = jnp.concatenate([arrived, local], axis=0)
    return jnp.dot(hot, both, preferred_element_type=jnp.float32).astype(jnp.bfloat16)


def settle_kernel(shift_ref, docs_ref, arrived_ref, local_ref, out_ref, hot_ref):
    quota = out_ref.shape[0]
    shift, shift_before = shift_ref[0], shift_ref[1]
    row = lax.broadcasted_iota(jnp.int32, (quota, quota), 0)
    col = lax.broadcasted_iota(jnp.int32, (quota, quota), 1)
    turned = row - shift_before
    turned = jnp.where(turned < 0, turned + quota, turned)
    hot_arrived = jnp.where((row < shift) & (col == turned), 1.0, 0.0)
    hot_local = jnp.where(col == row - shift, 1.0, 0.0)
    hot = jnp.concatenate([hot_arrived, hot_local], axis=1).astype(jnp.bfloat16)
    hot_ref[...] = hot
    out_ref[:, :NOTE] = place_rows(hot, arrived_ref[...], local_ref[...])
    docs = jnp.broadcast_to(docs_ref[...].astype(jnp.float32), (quota, quota))
    out_ref[:, NOTE:] = docs.astype(jnp.bfloat16)


def settle_kv(shift, docs, arrived, local):
    quota = arrived.shape[0]
    return pl.pallas_call(
        settle_kernel,
        in_specs=[SCALARS, WHOLE, WHOLE, WHOLE],
        out_specs=[WHOLE, WHOLE],
        out_shape=[
            jax.ShapeDtypeStruct((quota, NOTE + quota), jnp.bfloat16),
            jax.ShapeDtypeStruct((quota, 2 * quota), jnp.bfloat16),
        ],
        compiler_params=pltpu.CompilerParams(vmem_limit_bytes=VMEM_GRANT),
        name="settle_kv",
    )(shift, docs, arrived, local)


def block_ranks(rank, core, rounds):
    ranks = [rank]
    for back in range(1, rounds + 1):
        ranks.append(rank - 2 * back)
        if back < rounds:
            ranks.append(rank - 2 * back + jnp.where(core == 0, 1, -1))
    ranks.append(jnp.where(core == 0, rank - 2 * rounds + 1, rank - 1))
    return ranks


def head_columns(head, heads=1):
    return slice(head * HEAD_SIZE, (head + heads) * HEAD_SIZE)


def pieces(first, count):
    at, found = first, []
    while at < first + count:
        end = min(first + count, (at // GROUP + 1) * GROUP)
        heads = end - at
        if heads > HALF:
            heads = min(HALF, -(-heads // 2))
        found.append((at, heads))
        at += heads
    return found


def in_place(kernel, operands, out, more_out=(), more_specs=(), **arguments):
    specs = arguments.pop("in_specs") + [ANYWHERE]
    return pl.pallas_call(
        kernel,
        in_specs=specs,
        out_specs=[ANYWHERE, *more_specs],
        out_shape=[jax.ShapeDtypeStruct(out.shape, out.dtype), *more_out],
        input_output_aliases={len(operands): 0},
        cost_estimate=pl.CostEstimate(flops=0, bytes_accessed=0, transcendentals=0),
        compiler_params=pltpu.CompilerParams(vmem_limit_bytes=VMEM_GRANT),
        **arguments,
    )(*operands, out)


def place_kernel(first, hot_ref, arrived_ref, q_hbm, *refs):
    out_hbm, local, placed, in_sem, out_sem = refs[-5:]
    quota, width = arrived_ref.shape
    cols = head_columns(first, width // HEAD_SIZE)
    fetch = pltpu.make_async_copy(q_hbm.at[0, 0:quota, cols], local, in_sem)
    fetch.start()
    fetch.wait()
    for head, heads in pieces(first, width // HEAD_SIZE):
        own = head_columns(head - first, heads)
        placed[:, own] = place_rows(hot_ref[...], arrived_ref[:, own], local[:, own])
    store = pltpu.make_async_copy(placed, out_hbm.at[0, :, cols], out_sem)
    store.start()
    store.wait()


def place_queries(hot, arrived, q_rows, first, out):
    quota = arrived.shape[0]
    arguments = dict(
        in_specs=[WHOLE, WHOLE, ANYWHERE],
        scratch_shapes=[
            pltpu.VMEM(arrived.shape, jnp.bfloat16),
            pltpu.VMEM(arrived.shape, jnp.bfloat16),
            pltpu.SemaphoreType.DMA,
            pltpu.SemaphoreType.DMA,
        ],
        name="place_queries",
    )
    kernel = functools.partial(place_kernel, first)
    if out is not None:
        return in_place(kernel, [hot, arrived, q_rows], out, **arguments)[0]
    return pl.pallas_call(
        kernel,
        out_specs=ANYWHERE,
        out_shape=jax.ShapeDtypeStruct((1, quota, QUERY_HEADS * HEAD_SIZE), jnp.bfloat16),
        compiler_params=pltpu.CompilerParams(vmem_limit_bytes=VMEM_GRANT),
        **arguments,
    )(hot, arrived, q_rows)


def make_bias(kv_refs, far_ref, mate_ref, bias, rank):
    quota = bias.shape[0]
    core = lax.rem(rank, 2)
    row = lax.broadcasted_iota(jnp.int32, (quota, quota), 0)
    col = lax.broadcasted_iota(jnp.int32, (quota, quota), 1)
    note = slice(NOTE, NOTE + quota)
    q_docs = jnp.where(row == col, kv_refs[0][:, note].astype(jnp.float32), 0.0)
    q_docs = jnp.sum(q_docs, axis=1, keepdims=True)
    blocks = len(kv_refs) + 1
    for b, block_rank in enumerate(block_ranks(rank, core, (blocks - 1) // 2)):
        if b < blocks - 1:
            docs = kv_refs[b][:, note].astype(jnp.float32)
        else:
            far = far_ref[:, note].astype(jnp.float32)
            docs = jnp.where(core == 0, far, mate_ref[:, note].astype(jnp.float32))
        allowed = docs == q_docs
        allowed &= (col <= row) if b == 0 else (block_rank >= 0)
        bias[:, b * quota : (b + 1) * quota] = jnp.where(allowed, 0.0, MASKED)


def choose_rest(first, count, core, far_ref, mate_ref, rest):
    first_head, last_head = first // GROUP, (first + count - 1) // GROUP
    keys = head_columns(first_head, last_head - first_head + 1)
    values = slice(KV_WIDTH + keys.start, KV_WIDTH + keys.stop)

    @pl.when(core == 0)
    def _():
        rest[:, keys] = far_ref[:, keys]
        rest[:, values] = far_ref[:, values]

    @pl.when(core == 1)
    def _():
        rest[:, keys] = mate_ref[:, keys]
        rest[:, values] = mate_ref[:, values]


def attend_heads(first, steps, kv_refs, bias, take, result):
    quota = bias.shape[0]
    unit = math.log2(math.e) / math.sqrt(HEAD_SIZE)

    def key_head(head):
        cols = head_columns(head)
        keys = jnp.concatenate([r[:, cols] for r in kv_refs], axis=0)
        cols = head_columns(KEY_VALUE_HEADS + head)
        values = jnp.concatenate([r[:, cols] for r in kv_refs], axis=0)
        return keys, jnp.concatenate([values, jnp.ones_like(values)], axis=1)

    def scored(head, heads, keys):
        q = take(head_columns(head - first, heads))
        stacked = jnp.concatenate([q[:, head_columns(h)] for h in range(heads)], axis=0)
        return lax.dot_general(
            stacked, keys, (((1,), (1,)), ((), ())), preferred_element_type=jnp.float32
        )

    def finished(head, heads, scores, values):
        scores = scores.reshape(heads, quota, -1) * unit + bias[...][None]
        weights = jnp.exp2(scores - jnp.max(scores, axis=2, keepdims=True))
        weights = weights.astype(jnp.bfloat16).reshape(heads * quota, -1)
        mixed = jnp.dot(weights, values, preferred_element_type=jnp.float32)
        totals = mixed[:, HEAD_SIZE:]
        inverse = pl.reciprocal(totals, approx=True)
        inverse = inverse * (2.0 - totals * inverse)
        mixed = (mixed[:, :HEAD_SIZE] * inverse).astype(jnp.bfloat16)
        for h in range(heads):
            result[:, head_columns(head - first + h)] = mixed[h * quota : (h + 1) * quota]

    keys, values = key_head(steps[0][0] // GROUP)
    scores = scored(*steps[0], keys)
    for i, (head, heads) in enumerate(steps):
        own_values, later = values, None
        if i + 1 < len(steps):
            if steps[i + 1][0] // GROUP != head // GROUP:
                keys, values = key_head(steps[i + 1][0] // GROUP)
            later = scored(*steps[i + 1], keys)
        finished(head, heads, scores, own_values)
        scores = later


def early_kernel(blocks, count, rank_ref, *refs):
    kv_refs, far_ref, mate_ref = refs[: blocks - 1], refs[blocks - 1], refs[blocks]
    q_hbm, in_hbm, out_hbm, local, bias, rest, queries, result, sems = refs[blocks + 1 :]
    own, others = head_columns(0, count), head_columns(count, QUERY_HEADS - count)
    fetch = pltpu.make_async_copy(in_hbm.at[0, :, own], queries, sems.at[0])
    fetch.start()
    rank = rank_ref[0]
    make_bias(kv_refs, far_ref, mate_ref, bias, rank)
    choose_rest(0, count, lax.rem(rank, 2), far_ref, mate_ref, rest)
    fetch.wait()
    attend_heads(0, pieces(0, count), [*kv_refs, rest], bias, lambda cols: queries[:, cols], result)
    store = pltpu.make_async_copy(result, out_hbm.at[0, :, own], sems.at[1])
    store.start()
    ahead = pltpu.make_async_copy(q_hbm.at[0, 0 : bias.shape[0], others], local, sems.at[2])
    ahead.start()
    store.wait()
    ahead.wait()


def late_kernel(blocks, first, rank_ref, *refs):
    kv_refs, far_ref, mate_ref = refs[: blocks - 1], refs[blocks - 1], refs[blocks]
    hot_ref, arrived_hbm, local_ref, _, out_hbm = refs[blocks + 1 : blocks + 6]
    bias, rest, arrived, result, sems = refs[blocks + 6 :]
    count = QUERY_HEADS - first
    fetch = pltpu.make_async_copy(arrived_hbm, arrived, sems.at[0])
    fetch.start()
    rank = rank_ref[0]
    make_bias(kv_refs, far_ref, mate_ref, bias, rank)
    choose_rest(first, count, lax.rem(rank, 2), far_ref, mate_ref, rest)
    fetch.wait()

    def take(cols):
        return place_rows(hot_ref[...], arrived[:, cols], local_ref[:, cols])

    steps = sorted(pieces(first, count), key=lambda piece: -piece[1])
    head, heads = steps.pop()
    if heads == HALF:
        steps += [(head, heads // 2), (head + heads // 2, heads // 2)]
    else:
        steps.append((head, heads))
    attend_heads(first, steps, [*kv_refs, rest], bias, take, result)
    store = pltpu.make_async_copy(result, out_hbm.at[0, :, head_columns(first, count)], sems.at[1])
    store.start()
    store.wait()


def attend(rank, hot, arrived, q_rows, kv_blocks, out):
    quota, width = arrived.shape
    blocks = len(kv_blocks) - 1
    first = QUERY_HEADS - width // HEAD_SIZE
    bias = pltpu.VMEM((quota, blocks * quota), jnp.float32)
    rest = pltpu.VMEM((quota, NOTE), jnp.bfloat16)
    own = pltpu.VMEM(arrived.shape, jnp.bfloat16)
    others = pltpu.VMEM((quota, first * HEAD_SIZE), jnp.bfloat16)
    out, local = in_place(
        functools.partial(early_kernel, blocks, first),
        [rank, *kv_blocks, q_rows],
        out,
        more_out=[jax.ShapeDtypeStruct(arrived.shape, jnp.bfloat16)],
        more_specs=[WHOLE],
        in_specs=[SCALARS] + [WHOLE] * len(kv_blocks) + [ANYWHERE],
        scratch_shapes=[bias, rest, others, others, pltpu.SemaphoreType.DMA((3,))],
        name="attend_early",
    )
    return in_place(
        functools.partial(late_kernel, blocks, first),
        [rank, *kv_blocks, hot, arrived, local],
        out,
        in_specs=[SCALARS] + [WHOLE] * (len(kv_blocks) + 1) + [ANYWHERE, WHOLE],
        scratch_shapes=[bias, rest, own, own, pltpu.SemaphoreType.DMA((2,))],
        name="attend_late",
    )[0]


def circular_tail(rows, later):
    quota = later.shape[0]
    return jnp.where(later[:, None], rows[quota:], rows[:quota])


def sent(rows, later):
    if lax.axis_size("dp") > 4:
        return circular_tail(rows, later)
    return rows[later.shape[0] :]


def body(q_rows, k_rows, value_slot_rows, counts, doc_ids):
    quota = doc_ids.shape[1]
    rounds = lax.axis_size("ctx") // 4
    rank = lax.axis_index("ctx")
    own_count = counts[0, 0]

    later = quota + jnp.arange(quota, dtype=jnp.int32) < own_count
    k_local, v_local = k_rows[0], value_slot_rows[0]
    kv_tail = jnp.concatenate([sent(k_local, later), sent(v_local, later)], axis=1)
    arrived_kv = shifted(kv_tail, "dp", 1)
    zero = (kv_tail[:1, :1] + kv_tail[:1, -1:]) * 0
    local_kv = jnp.concatenate([k_local[:quota] + zero, v_local[:quota] + zero], axis=1)
    local_kv, zero = lax.optimization_barrier((local_kv, zero))
    q_tails = []
    first = 0
    for size in CHUNKS:
        q_tails.append(sent(q_rows[0, :, head_columns(first, size)], later) + zero)
        first += size
    q_tails = lax.optimization_barrier(q_tails)
    arrived_q = [shifted(tail, "dp", 1) for tail in q_tails]

    shift = shifts_in(own_count, quota)
    own, hot = settle_kv(shift, doc_ids, arrived_kv, local_kv)

    kv_blocks = [own]
    carried, out = own, None
    for back in range(1, rounds + 1):
        carried = shifted(carried, "ctx", 2)
        kv_blocks.append(carried)
        if back < len(CHUNKS):
            first = sum(CHUNKS[: back - 1])
            out = place_queries(hot, arrived_q[back - 1], q_rows, first, out)
            carried, out = lax.optimization_barrier((carried, out))
        if back < rounds:
            kv_blocks.append(across_cores(carried))
    kv_blocks += [across_cores(carried), across_cores(own, (0,))]
    return attend(rank[None], hot, arrived_q[-1], q_rows, kv_blocks, out)


def solution(mesh):
    return jax.shard_map(
        body,
        mesh=mesh,
        in_specs=(
            P("dp", "ctx", None),
            P("dp", "ctx", None),
            P("dp", "ctx", None),
            P("dp", "ctx"),
            P("dp", "ctx"),
        ),
        out_specs=P("dp", "ctx", None),
        check_vma=False,
    )
```

```python
import functools
import math

import jax
import jax.numpy as jnp
from jax import lax
from jax.experimental import pallas as pl
from jax.experimental.pallas import tpu as pltpu
from jax.sharding import PartitionSpec as P

QUERY_HEADS = 64
KEY_VALUE_HEADS = 8
HEAD_SIZE = 128
GROUP = QUERY_HEADS // KEY_VALUE_HEADS
KV_WIDTH = KEY_VALUE_HEADS * HEAD_SIZE
NOTE = 2 * KV_WIDTH
MASKED = -1e30
HALF = GROUP // 2
CHUNKS = (20, 26, 18)
VMEM_GRANT = 48 * 1024 * 1024

WHOLE = pl.BlockSpec(memory_space=pltpu.VMEM)
ANYWHERE = pl.BlockSpec(memory_space=pl.ANY)
SCALARS = pl.BlockSpec(memory_space=pltpu.SMEM)


def shifted(x, axis, steps):
    n = lax.axis_size(axis)
    return lax.ppermute(x, axis, [(i, i + steps) for i in range(n - steps)])


def across_cores(x, sources=(0, 1)):
    n = lax.axis_size("ctx")
    return lax.ppermute(x, "ctx", [(i, i ^ 1) for i in range(n) if i % 2 in sources])


def everyones(x, axis):
    n = lax.axis_size(axis)
    spread = jnp.broadcast_to(x[None], (n,) + x.shape)
    return lax.all_to_all(spread, axis, split_axis=0, concat_axis=0)


def shifts_in(own_count, quota):
    n = lax.axis_size("dp")
    replica = lax.axis_index("dp")
    if n > 4:
        all_counts = everyones(own_count[None], "dp")[:, 0]
        places = jnp.arange(n, dtype=jnp.int32)
        before = jnp.sum(jnp.where(places < replica, all_counts, 0))
        before_last = jnp.sum(jnp.where(places < replica - 1, all_counts, 0))
        return jnp.stack([before - replica * quota, before_last - (replica - 1) * quota])
    return jnp.stack([jnp.maximum(quota - own_count, 0), jnp.int32(0)])


def place_rows(hot, arrived, local):
    both = jnp.concatenate([arrived, local], axis=0)
    return jnp.dot(hot, both, preferred_element_type=jnp.float32).astype(jnp.bfloat16)


def settle_kernel(shift_ref, docs_ref, arrived_ref, local_ref, out_ref, hot_ref):
    quota = out_ref.shape[0]
    shift, shift_before = shift_ref[0], shift_ref[1]
    row = lax.broadcasted_iota(jnp.int32, (quota, quota), 0)
    col = lax.broadcasted_iota(jnp.int32, (quota, quota), 1)
    turned = row - shift_before
    turned = jnp.where(turned < 0, turned + quota, turned)
    hot_arrived = jnp.where((row < shift) & (col == turned), 1.0, 0.0)
    hot_local = jnp.where(col == row - shift, 1.0, 0.0)
    hot = jnp.concatenate([hot_arrived, hot_local], axis=1).astype(jnp.bfloat16)
    hot_ref[...] = hot
    out_ref[:, :NOTE] = place_rows(hot, arrived_ref[...], local_ref[...])
    docs = jnp.broadcast_to(docs_ref[...].astype(jnp.float32), (quota, quota))
    out_ref[:, NOTE:] = docs.astype(jnp.bfloat16)


def settle_kv(shift, docs, arrived, local):
    quota = arrived.shape[0]
    return pl.pallas_call(
        settle_kernel,
        in_specs=[SCALARS, WHOLE, WHOLE, WHOLE],
        out_specs=[WHOLE, WHOLE],
        out_shape=[
            jax.ShapeDtypeStruct((quota, NOTE + quota), jnp.bfloat16),
            jax.ShapeDtypeStruct((quota, 2 * quota), jnp.bfloat16),
        ],
        compiler_params=pltpu.CompilerParams(vmem_limit_bytes=VMEM_GRANT),
        name="settle_kv",
    )(shift, docs, arrived, local)


def block_ranks(rank, core, rounds):
    ranks = [rank]
    for back in range(1, rounds + 1):
        ranks.append(rank - 2 * back)
        if back < rounds:
            ranks.append(rank - 2 * back + jnp.where(core == 0, 1, -1))
    ranks.append(jnp.where(core == 0, rank - 2 * rounds + 1, rank - 1))
    return ranks


def head_columns(head, heads=1):
    return slice(head * HEAD_SIZE, (head + heads) * HEAD_SIZE)


def pieces(first, count):
    at, found = first, []
    while at < first + count:
        end = min(first + count, (at // GROUP + 1) * GROUP)
        heads = end - at
        if heads > HALF:
            heads = min(HALF, -(-heads // 2))
        found.append((at, heads))
        at += heads
    return found


def in_place(kernel, operands, out, more_out=(), more_specs=(), **arguments):
    specs = arguments.pop("in_specs") + [ANYWHERE]
    return pl.pallas_call(
        kernel,
        in_specs=specs,
        out_specs=[ANYWHERE, *more_specs],
        out_shape=[jax.ShapeDtypeStruct(out.shape, out.dtype), *more_out],
        input_output_aliases={len(operands): 0},
        cost_estimate=pl.CostEstimate(flops=0, bytes_accessed=0, transcendentals=0),
        compiler_params=pltpu.CompilerParams(vmem_limit_bytes=VMEM_GRANT),
        **arguments,
    )(*operands, out)


def place_kernel(first, hot_ref, arrived_ref, q_hbm, *refs):
    out_hbm, local, placed, in_sem, out_sem = refs[-5:]
    quota, width = arrived_ref.shape
    cols = head_columns(first, width // HEAD_SIZE)
    fetch = pltpu.make_async_copy(q_hbm.at[0, 0:quota, cols], local, in_sem)
    fetch.start()
    fetch.wait()
    for head, heads in pieces(first, width // HEAD_SIZE):
        own = head_columns(head - first, heads)
        placed[:, own] = place_rows(hot_ref[...], arrived_ref[:, own], local[:, own])
    store = pltpu.make_async_copy(placed, out_hbm.at[0, :, cols], out_sem)
    store.start()
    store.wait()


def place_queries(hot, arrived, q_rows, first, out):
    quota = arrived.shape[0]
    arguments = dict(
        in_specs=[WHOLE, WHOLE, ANYWHERE],
        scratch_shapes=[
            pltpu.VMEM(arrived.shape, jnp.bfloat16),
            pltpu.VMEM(arrived.shape, jnp.bfloat16),
            pltpu.SemaphoreType.DMA,
            pltpu.SemaphoreType.DMA,
        ],
        name="place_queries",
    )
    kernel = functools.partial(place_kernel, first)
    if out is not None:
        return in_place(kernel, [hot, arrived, q_rows], out, **arguments)[0]
    return pl.pallas_call(
        kernel,
        out_specs=ANYWHERE,
        out_shape=jax.ShapeDtypeStruct((1, quota, QUERY_HEADS * HEAD_SIZE), jnp.bfloat16),
        compiler_params=pltpu.CompilerParams(vmem_limit_bytes=VMEM_GRANT),
        **arguments,
    )(hot, arrived, q_rows)


def make_bias(kv_refs, far_ref, mate_ref, bias, rank):
    quota = bias.shape[0]
    core = lax.rem(rank, 2)
    row = lax.broadcasted_iota(jnp.int32, (quota, quota), 0)
    col = lax.broadcasted_iota(jnp.int32, (quota, quota), 1)
    note = slice(NOTE, NOTE + quota)
    q_docs = jnp.where(row == col, kv_refs[0][:, note].astype(jnp.float32), 0.0)
    q_docs = jnp.sum(q_docs, axis=1, keepdims=True)
    blocks = len(kv_refs) + 1
    for b, block_rank in enumerate(block_ranks(rank, core, (blocks - 1) // 2)):
        if b < blocks - 1:
            docs = kv_refs[b][:, note].astype(jnp.float32)
        else:
            far = far_ref[:, note].astype(jnp.float32)
            docs = jnp.where(core == 0, far, mate_ref[:, note].astype(jnp.float32))
        allowed = docs == q_docs
        allowed &= (col <= row) if b == 0 else (block_rank >= 0)
        bias[:, b * quota : (b + 1) * quota] = jnp.where(allowed, 0.0, MASKED)


def choose_rest(first, count, core, far_ref, mate_ref, rest):
    first_head, last_head = first // GROUP, (first + count - 1) // GROUP
    keys = head_columns(first_head, last_head - first_head + 1)
    values = slice(KV_WIDTH + keys.start, KV_WIDTH + keys.stop)

    @pl.when(core == 0)
    def _():
        rest[:, keys] = far_ref[:, keys]
        rest[:, values] = far_ref[:, values]

    @pl.when(core == 1)
    def _():
        rest[:, keys] = mate_ref[:, keys]
        rest[:, values] = mate_ref[:, values]


def attend_heads(first, steps, kv_refs, bias, take, result, after_first, before_last):
    quota = bias.shape[0]
    unit = math.log2(math.e) / math.sqrt(HEAD_SIZE)

    def key_head(head):
        cols = head_columns(head)
        keys = jnp.concatenate([r[:, cols] for r in kv_refs], axis=0)
        cols = head_columns(KEY_VALUE_HEADS + head)
        values = jnp.concatenate([r[:, cols] for r in kv_refs], axis=0)
        return keys, jnp.concatenate([values, jnp.ones_like(values)], axis=1)

    def scored(head, heads, keys):
        q = take(head_columns(head - first, heads))
        stacked = jnp.concatenate([q[:, head_columns(h)] for h in range(heads)], axis=0)
        return lax.dot_general(
            stacked, keys, (((1,), (1,)), ((), ())), preferred_element_type=jnp.float32
        )

    def finished(head, heads, scores, values):
        scores = scores.reshape(heads, quota, -1) * unit + bias[...][None]
        weights = jnp.exp2(scores - jnp.max(scores, axis=2, keepdims=True))
        weights = weights.astype(jnp.bfloat16).reshape(heads * quota, -1)
        mixed = jnp.dot(weights, values, preferred_element_type=jnp.float32)
        totals = mixed[:, HEAD_SIZE:]
        inverse = pl.reciprocal(totals, approx=True)
        inverse = inverse * (2.0 - totals * inverse)
        mixed = (mixed[:, :HEAD_SIZE] * inverse).astype(jnp.bfloat16)
        for h in range(heads):
            result[:, head_columns(head - first + h)] = mixed[h * quota : (h + 1) * quota]

    keys, values = key_head(steps[0][0] // GROUP)
    scores = scored(*steps[0], keys)
    after_first()
    for i, (head, heads) in enumerate(steps):
        own_values, later = values, None
        if i + 1 < len(steps):
            if steps[i + 1][0] // GROUP != head // GROUP:
                keys, values = key_head(steps[i + 1][0] // GROUP)
            later = scored(*steps[i + 1], keys)
        if i + 1 == len(steps):
            before_last()
        finished(head, heads, scores, own_values)
        scores = later


def early_kernel(blocks, count, rank_ref, *refs):
    kv_refs, far_ref, mate_ref = refs[: blocks - 1], refs[blocks - 1], refs[blocks]
    q_hbm, in_hbm, out_hbm, local, bias, rest, queries, result, sems = refs[blocks + 1 :]
    steps = pieces(0, count)
    edge, end = steps[0][1], steps[-1][0]

    def fetching(cols, sem):
        return pltpu.make_async_copy(in_hbm.at[0, :, cols], queries.at[:, cols], sem)

    def storing(cols, sem):
        return pltpu.make_async_copy(result.at[:, cols], out_hbm.at[0, :, cols], sem)

    fetch = fetching(head_columns(0, edge), sems.at[0])
    fetch_rest = fetching(head_columns(edge, count - edge), sems.at[1])
    store = storing(head_columns(0, end), sems.at[2])
    store_last = storing(head_columns(end, count - end), sems.at[3])
    others = head_columns(count, QUERY_HEADS - count)
    ahead = pltpu.make_async_copy(q_hbm.at[0, 0 : bias.shape[0], others], local, sems.at[4])
    fetch.start()
    fetch_rest.start()
    rank = rank_ref[0]
    make_bias(kv_refs, far_ref, mate_ref, bias, rank)
    choose_rest(0, count, lax.rem(rank, 2), far_ref, mate_ref, rest)
    fetch.wait()
    attend_heads(
        0,
        steps,
        [*kv_refs, rest],
        bias,
        lambda cols: queries[:, cols],
        result,
        fetch_rest.wait,
        store.start,
    )
    store_last.start()
    ahead.start()
    store.wait()
    store_last.wait()
    ahead.wait()


def late_kernel(blocks, first, rank_ref, *refs):
    kv_refs, far_ref, mate_ref = refs[: blocks - 1], refs[blocks - 1], refs[blocks]
    hot_ref, arrived_hbm, local_ref, _, out_hbm = refs[blocks + 1 : blocks + 6]
    bias, rest, arrived, result, sems = refs[blocks + 6 :]
    count = QUERY_HEADS - first
    steps = pieces(first, count)[::-1]
    edge, end = steps[0][0], sum(steps[-1])

    def fetching(cols, sem):
        return pltpu.make_async_copy(arrived_hbm.at[:, cols], arrived.at[:, cols], sem)

    def storing(at, heads, sem):
        own = head_columns(at - first, heads)
        return pltpu.make_async_copy(
            result.at[:, own], out_hbm.at[0, :, head_columns(at, heads)], sem
        )

    fetch = fetching(head_columns(edge - first, QUERY_HEADS - edge), sems.at[0])
    fetch_rest = fetching(head_columns(0, edge - first), sems.at[1])
    store = storing(end, QUERY_HEADS - end, sems.at[2])
    store_last = storing(first, end - first, sems.at[3])
    fetch.start()
    fetch_rest.start()
    rank = rank_ref[0]
    make_bias(kv_refs, far_ref, mate_ref, bias, rank)
    choose_rest(first, count, lax.rem(rank, 2), far_ref, mate_ref, rest)
    fetch.wait()

    def take(cols):
        return place_rows(hot_ref[...], arrived[:, cols], local_ref[:, cols])

    attend_heads(
        first, steps, [*kv_refs, rest], bias, take, result, fetch_rest.wait, store.start
    )
    store_last.start()
    store.wait()
    store_last.wait()


def attend(rank, hot, arrived, q_rows, kv_blocks, out):
    quota, width = arrived.shape
    blocks = len(kv_blocks) - 1
    first = QUERY_HEADS - width // HEAD_SIZE
    bias = pltpu.VMEM((quota, blocks * quota), jnp.float32)
    rest = pltpu.VMEM((quota, NOTE), jnp.bfloat16)
    own = pltpu.VMEM(arrived.shape, jnp.bfloat16)
    others = pltpu.VMEM((quota, first * HEAD_SIZE), jnp.bfloat16)
    out, local = in_place(
        functools.partial(early_kernel, blocks, first),
        [rank, *kv_blocks, q_rows],
        out,
        more_out=[jax.ShapeDtypeStruct(arrived.shape, jnp.bfloat16)],
        more_specs=[WHOLE],
        in_specs=[SCALARS] + [WHOLE] * len(kv_blocks) + [ANYWHERE],
        scratch_shapes=[bias, rest, others, others, pltpu.SemaphoreType.DMA((5,))],
        name="attend_early",
    )
    return in_place(
        functools.partial(late_kernel, blocks, first),
        [rank, *kv_blocks, hot, arrived, local],
        out,
        in_specs=[SCALARS] + [WHOLE] * (len(kv_blocks) + 1) + [ANYWHERE, WHOLE],
        scratch_shapes=[bias, rest, own, own, pltpu.SemaphoreType.DMA((4,))],
        name="attend_late",
    )[0]


def circular_tail(rows, later):
    quota = later.shape[0]
    return jnp.where(later[:, None], rows[quota:], rows[:quota])


def sent(rows, later):
    if lax.axis_size("dp") > 4:
        return circular_tail(rows, later)
    return rows[later.shape[0] :]


def body(q_rows, k_rows, value_slot_rows, counts, doc_ids):
    quota = doc_ids.shape[1]
    rounds = lax.axis_size("ctx") // 4
    rank = lax.axis_index("ctx")
    own_count = counts[0, 0]

    later = quota + jnp.arange(quota, dtype=jnp.int32) < own_count
    k_local, v_local = k_rows[0], value_slot_rows[0]
    kv_tail = jnp.concatenate([sent(k_local, later), sent(v_local, later)], axis=1)
    arrived_kv = shifted(kv_tail, "dp", 1)
    zero = (kv_tail[:1, :1] + kv_tail[:1, -1:]) * 0
    local_kv = jnp.concatenate([k_local[:quota] + zero, v_local[:quota] + zero], axis=1)
    local_kv, zero = lax.optimization_barrier((local_kv, zero))
    q_tails = []
    first = 0
    for size in CHUNKS:
        q_tails.append(sent(q_rows[0, :, head_columns(first, size)], later) + zero)
        first += size
    q_tails = lax.optimization_barrier(q_tails)
    arrived_q = [shifted(tail, "dp", 1) for tail in q_tails]

    shift = shifts_in(own_count, quota)
    own, hot = settle_kv(shift, doc_ids, arrived_kv, local_kv)

    kv_blocks = [own]
    carried, out = own, None
    for back in range(1, rounds + 1):
        carried = shifted(carried, "ctx", 2)
        kv_blocks.append(carried)
        if back < len(CHUNKS):
            first = sum(CHUNKS[: back - 1])
            out = place_queries(hot, arrived_q[back - 1], q_rows, first, out)
            carried, out = lax.optimization_barrier((carried, out))
        if back < rounds:
            kv_blocks.append(across_cores(carried))
    kv_blocks += [across_cores(carried), across_cores(own, (0,))]
    return attend(rank[None], hot, arrived_q[-1], q_rows, kv_blocks, out)


def solution(mesh):
    return jax.shard_map(
        body,
        mesh=mesh,
        in_specs=(
            P("dp", "ctx", None),
            P("dp", "ctx", None),
            P("dp", "ctx", None),
            P("dp", "ctx"),
            P("dp", "ctx"),
        ),
        out_specs=P("dp", "ctx", None),
        check_vma=False,
    )
```

```python
import functools
import math

import jax
import jax.numpy as jnp
from jax import lax
from jax.experimental import pallas as pl
from jax.experimental.pallas import tpu as pltpu
from jax.sharding import PartitionSpec as P

QUERY_HEADS = 64
KEY_VALUE_HEADS = 8
HEAD_SIZE = 128
GROUP = QUERY_HEADS // KEY_VALUE_HEADS
KV_WIDTH = KEY_VALUE_HEADS * HEAD_SIZE
NOTE = 2 * KV_WIDTH
MASKED = -1e30
HALF = GROUP // 2
CHUNKS = (20, 25, 19)
VMEM_GRANT = 48 * 1024 * 1024

WHOLE = pl.BlockSpec(memory_space=pltpu.VMEM)
ANYWHERE = pl.BlockSpec(memory_space=pl.ANY)
SCALARS = pl.BlockSpec(memory_space=pltpu.SMEM)


def shifted(x, axis, steps):
    n = lax.axis_size(axis)
    return lax.ppermute(x, axis, [(i, i + steps) for i in range(n - steps)])


def across_cores(x, sources=(0, 1)):
    n = lax.axis_size("ctx")
    return lax.ppermute(x, "ctx", [(i, i ^ 1) for i in range(n) if i % 2 in sources])


def everyones(x, axis):
    n = lax.axis_size(axis)
    spread = jnp.broadcast_to(x[None], (n,) + x.shape)
    return lax.all_to_all(spread, axis, split_axis=0, concat_axis=0)


def shifts_in(own_count, quota):
    n = lax.axis_size("dp")
    replica = lax.axis_index("dp")
    if n > 4:
        all_counts = everyones(own_count[None], "dp")[:, 0]
        places = jnp.arange(n, dtype=jnp.int32)
        before = jnp.sum(jnp.where(places < replica, all_counts, 0))
        before_last = jnp.sum(jnp.where(places < replica - 1, all_counts, 0))
        return jnp.stack([before - replica * quota, before_last - (replica - 1) * quota])
    return jnp.stack([jnp.maximum(quota - own_count, 0), jnp.int32(0)])


def place_rows(hot, arrived, local):
    both = jnp.concatenate([arrived, local], axis=0)
    return jnp.dot(hot, both, preferred_element_type=jnp.float32).astype(jnp.bfloat16)


def settle_kernel(shift_ref, docs_ref, arrived_ref, local_ref, out_ref, hot_ref):
    quota = out_ref.shape[0]
    shift, shift_before = shift_ref[0], shift_ref[1]
    row = lax.broadcasted_iota(jnp.int32, (quota, quota), 0)
    col = lax.broadcasted_iota(jnp.int32, (quota, quota), 1)
    turned = row - shift_before
    turned = jnp.where(turned < 0, turned + quota, turned)
    hot_arrived = jnp.where((row < shift) & (col == turned), 1.0, 0.0)
    hot_local = jnp.where(col == row - shift, 1.0, 0.0)
    hot = jnp.concatenate([hot_arrived, hot_local], axis=1).astype(jnp.bfloat16)
    hot_ref[...] = hot
    out_ref[:, :NOTE] = place_rows(hot, arrived_ref[...], local_ref[...])
    docs = jnp.broadcast_to(docs_ref[...].astype(jnp.float32), (quota, quota))
    out_ref[:, NOTE:] = docs.astype(jnp.bfloat16)


def settle_kv(shift, docs, arrived, local):
    quota = arrived.shape[0]
    return pl.pallas_call(
        settle_kernel,
        in_specs=[SCALARS, WHOLE, WHOLE, WHOLE],
        out_specs=[WHOLE, WHOLE],
        out_shape=[
            jax.ShapeDtypeStruct((quota, NOTE + quota), jnp.bfloat16),
            jax.ShapeDtypeStruct((quota, 2 * quota), jnp.bfloat16),
        ],
        compiler_params=pltpu.CompilerParams(vmem_limit_bytes=VMEM_GRANT),
        name="settle_kv",
    )(shift, docs, arrived, local)


def block_ranks(rank, core, rounds):
    ranks = [rank]
    for back in range(1, rounds + 1):
        ranks.append(rank - 2 * back)
        if back < rounds:
            ranks.append(rank - 2 * back + jnp.where(core == 0, 1, -1))
    ranks.append(jnp.where(core == 0, rank - 2 * rounds + 1, rank - 1))
    return ranks


def head_columns(head, heads=1):
    return slice(head * HEAD_SIZE, (head + heads) * HEAD_SIZE)


def pieces(first, count):
    at, found = first, []
    while at < first + count:
        end = min(first + count, (at // GROUP + 1) * GROUP)
        heads = end - at
        if heads > HALF:
            heads = min(HALF, -(-heads // 2))
        found.append((at, heads))
        at += heads
    return found


def in_place(kernel, operands, out, more_out=(), more_specs=(), **arguments):
    specs = arguments.pop("in_specs") + [ANYWHERE]
    return pl.pallas_call(
        kernel,
        in_specs=specs,
        out_specs=[ANYWHERE, *more_specs],
        out_shape=[jax.ShapeDtypeStruct(out.shape, out.dtype), *more_out],
        input_output_aliases={len(operands): 0},
        cost_estimate=pl.CostEstimate(flops=0, bytes_accessed=0, transcendentals=0),
        compiler_params=pltpu.CompilerParams(vmem_limit_bytes=VMEM_GRANT),
        **arguments,
    )(*operands, out)


def place_kernel(first, hot_ref, arrived_ref, q_hbm, *refs):
    out_hbm, local, placed, in_sem, out_sem = refs[-5:]
    quota, width = arrived_ref.shape
    cols = head_columns(first, width // HEAD_SIZE)
    fetch = pltpu.make_async_copy(q_hbm.at[0, 0:quota, cols], local, in_sem)
    fetch.start()
    fetch.wait()
    for head, heads in pieces(first, width // HEAD_SIZE):
        own = head_columns(head - first, heads)
        placed[:, own] = place_rows(hot_ref[...], arrived_ref[:, own], local[:, own])
    store = pltpu.make_async_copy(placed, out_hbm.at[0, :, cols], out_sem)
    store.start()
    store.wait()


def place_queries(hot, arrived, q_rows, first, out):
    quota = arrived.shape[0]
    arguments = dict(
        in_specs=[WHOLE, WHOLE, ANYWHERE],
        scratch_shapes=[
            pltpu.VMEM(arrived.shape, jnp.bfloat16),
            pltpu.VMEM(arrived.shape, jnp.bfloat16),
            pltpu.SemaphoreType.DMA,
            pltpu.SemaphoreType.DMA,
        ],
        name="place_queries",
    )
    kernel = functools.partial(place_kernel, first)
    if out is not None:
        return in_place(kernel, [hot, arrived, q_rows], out, **arguments)[0]
    return pl.pallas_call(
        kernel,
        out_specs=ANYWHERE,
        out_shape=jax.ShapeDtypeStruct((1, quota, QUERY_HEADS * HEAD_SIZE), jnp.bfloat16),
        compiler_params=pltpu.CompilerParams(vmem_limit_bytes=VMEM_GRANT),
        **arguments,
    )(hot, arrived, q_rows)


def make_bias(kv_refs, far_ref, mate_ref, bias, rank):
    quota = bias.shape[0]
    core = lax.rem(rank, 2)
    row = lax.broadcasted_iota(jnp.int32, (quota, quota), 0)
    col = lax.broadcasted_iota(jnp.int32, (quota, quota), 1)
    note = slice(NOTE, NOTE + quota)
    q_docs = jnp.where(row == col, kv_refs[0][:, note].astype(jnp.float32), 0.0)
    q_docs = jnp.sum(q_docs, axis=1, keepdims=True)
    blocks = len(kv_refs) + 1
    for b, block_rank in enumerate(block_ranks(rank, core, (blocks - 1) // 2)):
        if b < blocks - 1:
            docs = kv_refs[b][:, note].astype(jnp.float32)
        else:
            far = far_ref[:, note].astype(jnp.float32)
            docs = jnp.where(core == 0, far, mate_ref[:, note].astype(jnp.float32))
        allowed = docs == q_docs
        allowed &= (col <= row) if b == 0 else (block_rank >= 0)
        bias[:, b * quota : (b + 1) * quota] = jnp.where(allowed, 0.0, MASKED)


def choose_rest(first, count, core, far_ref, mate_ref, rest):
    first_head, last_head = first // GROUP, (first + count - 1) // GROUP
    keys = head_columns(first_head, last_head - first_head + 1)
    values = slice(KV_WIDTH + keys.start, KV_WIDTH + keys.stop)

    @pl.when(core == 0)
    def _():
        rest[:, keys] = far_ref[:, keys]
        rest[:, values] = far_ref[:, values]

    @pl.when(core == 1)
    def _():
        rest[:, keys] = mate_ref[:, keys]
        rest[:, values] = mate_ref[:, values]


def attend_heads(first, steps, kv_refs, bias, take, result, after_first, before_last):
    quota = bias.shape[0]
    unit = math.log2(math.e) / math.sqrt(HEAD_SIZE)

    def key_head(head):
        cols = head_columns(head)
        keys = jnp.concatenate([r[:, cols] for r in kv_refs], axis=0)
        cols = head_columns(KEY_VALUE_HEADS + head)
        values = jnp.concatenate([r[:, cols] for r in kv_refs], axis=0)
        return keys, jnp.concatenate([values, jnp.ones_like(values)], axis=1)

    def scored(head, heads, keys):
        q = take(head_columns(head - first, heads))
        stacked = jnp.concatenate([q[:, head_columns(h)] for h in range(heads)], axis=0)
        return lax.dot_general(
            stacked, keys, (((1,), (1,)), ((), ())), preferred_element_type=jnp.float32
        )

    def finished(head, heads, scores, values):
        scores = scores.reshape(heads, quota, -1) * unit + bias[...][None]
        weights = jnp.exp2(scores - jnp.max(scores, axis=2, keepdims=True))
        weights = weights.astype(jnp.bfloat16).reshape(heads * quota, -1)
        mixed = jnp.dot(weights, values, preferred_element_type=jnp.float32)
        totals = mixed[:, HEAD_SIZE:]
        inverse = pl.reciprocal(totals, approx=True)
        inverse = inverse * (2.0 - totals * inverse)
        mixed = (mixed[:, :HEAD_SIZE] * inverse).astype(jnp.bfloat16)
        for h in range(heads):
            result[:, head_columns(head - first + h)] = mixed[h * quota : (h + 1) * quota]

    keys, values = key_head(steps[0][0] // GROUP)
    scores = scored(*steps[0], keys)
    after_first()
    for i, (head, heads) in enumerate(steps):
        own_values, later = values, None
        if i + 1 < len(steps):
            if steps[i + 1][0] // GROUP != head // GROUP:
                keys, values = key_head(steps[i + 1][0] // GROUP)
            later = scored(*steps[i + 1], keys)
        if i + 1 == len(steps):
            before_last()
        finished(head, heads, scores, own_values)
        scores = later


def early_kernel(blocks, count, rank_ref, *refs):
    kv_refs, far_ref, mate_ref = refs[: blocks - 1], refs[blocks - 1], refs[blocks]
    q_hbm, in_hbm, out_hbm, local, bias, rest, queries, result, sems = refs[blocks + 1 :]
    steps = pieces(0, count)
    edge, end = steps[0][1], steps[-1][0]

    def fetching(cols, sem):
        return pltpu.make_async_copy(in_hbm.at[0, :, cols], queries.at[:, cols], sem)

    def storing(cols, sem):
        return pltpu.make_async_copy(result.at[:, cols], out_hbm.at[0, :, cols], sem)

    fetch = fetching(head_columns(0, edge), sems.at[0])
    fetch_rest = fetching(head_columns(edge, count - edge), sems.at[1])
    store = storing(head_columns(0, end), sems.at[2])
    store_last = storing(head_columns(end, count - end), sems.at[3])
    others = head_columns(count, QUERY_HEADS - count)
    ahead = pltpu.make_async_copy(q_hbm.at[0, 0 : bias.shape[0], others], local, sems.at[4])
    fetch.start()
    fetch_rest.start()
    rank = rank_ref[0]
    make_bias(kv_refs, far_ref, mate_ref, bias, rank)
    choose_rest(0, count, lax.rem(rank, 2), far_ref, mate_ref, rest)
    fetch.wait()

    def after_first():
        fetch_rest.wait()
        ahead.start()

    attend_heads(
        0,
        steps,
        [*kv_refs, rest],
        bias,
        lambda cols: queries[:, cols],
        result,
        after_first,
        store.start,
    )
    store_last.start()
    store.wait()
    store_last.wait()
    ahead.wait()


def late_kernel(blocks, first, rank_ref, *refs):
    kv_refs, far_ref, mate_ref = refs[: blocks - 1], refs[blocks - 1], refs[blocks]
    hot_ref, arrived_hbm, local_ref, _, out_hbm = refs[blocks + 1 : blocks + 6]
    bias, rest, arrived, result, sems = refs[blocks + 6 :]
    count = QUERY_HEADS - first
    steps = pieces(first, count)[::-1]
    edge, end = steps[0][0], sum(steps[-1])

    def fetching(cols, sem):
        return pltpu.make_async_copy(arrived_hbm.at[:, cols], arrived.at[:, cols], sem)

    def storing(at, heads, sem):
        own = head_columns(at - first, heads)
        return pltpu.make_async_copy(
            result.at[:, own], out_hbm.at[0, :, head_columns(at, heads)], sem
        )

    fetch = fetching(head_columns(edge - first, QUERY_HEADS - edge), sems.at[0])
    fetch_rest = fetching(head_columns(0, edge - first), sems.at[1])
    store = storing(end, QUERY_HEADS - end, sems.at[2])
    store_last = storing(first, end - first, sems.at[3])
    fetch.start()
    fetch_rest.start()
    rank = rank_ref[0]
    make_bias(kv_refs, far_ref, mate_ref, bias, rank)
    choose_rest(first, count, lax.rem(rank, 2), far_ref, mate_ref, rest)
    fetch.wait()

    def take(cols):
        return place_rows(hot_ref[...], arrived[:, cols], local_ref[:, cols])

    attend_heads(
        first, steps, [*kv_refs, rest], bias, take, result, fetch_rest.wait, store.start
    )
    store_last.start()
    store.wait()
    store_last.wait()


def attend(rank, hot, arrived, q_rows, kv_blocks, out):
    quota, width = arrived.shape
    blocks = len(kv_blocks) - 1
    first = QUERY_HEADS - width // HEAD_SIZE
    bias = pltpu.VMEM((quota, blocks * quota), jnp.float32)
    rest = pltpu.VMEM((quota, NOTE), jnp.bfloat16)
    own = pltpu.VMEM(arrived.shape, jnp.bfloat16)
    others = pltpu.VMEM((quota, first * HEAD_SIZE), jnp.bfloat16)
    out, local = in_place(
        functools.partial(early_kernel, blocks, first),
        [rank, *kv_blocks, q_rows],
        out,
        more_out=[jax.ShapeDtypeStruct(arrived.shape, jnp.bfloat16)],
        more_specs=[WHOLE],
        in_specs=[SCALARS] + [WHOLE] * len(kv_blocks) + [ANYWHERE],
        scratch_shapes=[bias, rest, others, others, pltpu.SemaphoreType.DMA((5,))],
        name="attend_early",
    )
    return in_place(
        functools.partial(late_kernel, blocks, first),
        [rank, *kv_blocks, hot, arrived, local],
        out,
        in_specs=[SCALARS] + [WHOLE] * (len(kv_blocks) + 1) + [ANYWHERE, WHOLE],
        scratch_shapes=[bias, rest, own, own, pltpu.SemaphoreType.DMA((4,))],
        name="attend_late",
    )[0]


def circular_tail(rows, later):
    quota = later.shape[0]
    return jnp.where(later[:, None], rows[quota:], rows[:quota])


def sent(rows, later):
    if lax.axis_size("dp") > 4:
        return circular_tail(rows, later)
    return rows[later.shape[0] :]


def body(q_rows, k_rows, value_slot_rows, counts, doc_ids):
    quota = doc_ids.shape[1]
    rounds = lax.axis_size("ctx") // 4
    rank = lax.axis_index("ctx")
    own_count = counts[0, 0]

    later = quota + jnp.arange(quota, dtype=jnp.int32) < own_count
    k_local, v_local = k_rows[0], value_slot_rows[0]
    kv_tail = jnp.concatenate([sent(k_local, later), sent(v_local, later)], axis=1)
    arrived_kv = shifted(kv_tail, "dp", 1)
    zero = (kv_tail[:1, :1] + kv_tail[:1, -1:]) * 0
    local_kv = jnp.concatenate([k_local[:quota] + zero, v_local[:quota] + zero], axis=1)
    local_kv, zero = lax.optimization_barrier((local_kv, zero))
    q_tails = []
    first = 0
    for size in CHUNKS:
        q_tails.append(sent(q_rows[0, :, head_columns(first, size)], later) + zero)
        first += size
    q_tails = lax.optimization_barrier(q_tails)
    arrived_q = [shifted(tail, "dp", 1) for tail in q_tails]

    shift = shifts_in(own_count, quota)
    own, hot = settle_kv(shift, doc_ids, arrived_kv, local_kv)

    kv_blocks = [own]
    carried, out = own, None
    for back in range(1, rounds + 1):
        carried = shifted(carried, "ctx", 2)
        kv_blocks.append(carried)
        if back < len(CHUNKS):
            first = sum(CHUNKS[: back - 1])
            out = place_queries(hot, arrived_q[back - 1], q_rows, first, out)
            carried, out = lax.optimization_barrier((carried, out))
        if back < rounds:
            kv_blocks.append(across_cores(carried))
    kv_blocks += [across_cores(carried), across_cores(own, (0,))]
    return attend(rank[None], hot, arrived_q[-1], q_rows, kv_blocks, out)


def solution(mesh):
    return jax.shard_map(
        body,
        mesh=mesh,
        in_specs=(
            P("dp", "ctx", None),
            P("dp", "ctx", None),
            P("dp", "ctx", None),
            P("dp", "ctx"),
            P("dp", "ctx"),
        ),
        out_specs=P("dp", "ctx", None),
        check_vma=False,
    )
```

```python
import functools
import math

import jax
import jax.numpy as jnp
from jax import lax
from jax.experimental import pallas as pl
from jax.experimental.pallas import tpu as pltpu
from jax.sharding import PartitionSpec as P

QUERY_HEADS = 64
KEY_VALUE_HEADS = 8
HEAD_SIZE = 128
GROUP = QUERY_HEADS // KEY_VALUE_HEADS
KV_WIDTH = KEY_VALUE_HEADS * HEAD_SIZE
NOTE = 2 * KV_WIDTH
MASKED = -1e30
HALF = GROUP // 2
CHUNKS = (24, 22, 18)
VMEM_GRANT = 48 * 1024 * 1024

WHOLE = pl.BlockSpec(memory_space=pltpu.VMEM)
ANYWHERE = pl.BlockSpec(memory_space=pl.ANY)
SCALARS = pl.BlockSpec(memory_space=pltpu.SMEM)


def shifted(x, axis, steps):
    n = lax.axis_size(axis)
    return lax.ppermute(x, axis, [(i, i + steps) for i in range(n - steps)])


def across_cores(x, sources=(0, 1)):
    n = lax.axis_size("ctx")
    return lax.ppermute(x, "ctx", [(i, i ^ 1) for i in range(n) if i % 2 in sources])


def everyones(x, axis):
    n = lax.axis_size(axis)
    spread = jnp.broadcast_to(x[None], (n,) + x.shape)
    return lax.all_to_all(spread, axis, split_axis=0, concat_axis=0)


def shifts_in(own_count, quota):
    n = lax.axis_size("dp")
    replica = lax.axis_index("dp")
    if n > 4:
        all_counts = everyones(own_count[None], "dp")[:, 0]
        places = jnp.arange(n, dtype=jnp.int32)
        before = jnp.sum(jnp.where(places < replica, all_counts, 0))
        before_last = jnp.sum(jnp.where(places < replica - 1, all_counts, 0))
        return jnp.stack([before - replica * quota, before_last - (replica - 1) * quota])
    return jnp.stack([jnp.maximum(quota - own_count, 0), jnp.int32(0)])


def place_rows(hot, arrived, local):
    both = jnp.concatenate([arrived, local], axis=0)
    return jnp.dot(hot, both, preferred_element_type=jnp.float32).astype(jnp.bfloat16)


def settle_kernel(shift_ref, docs_ref, arrived_ref, local_ref, out_ref, hot_ref):
    quota = out_ref.shape[0]
    shift, shift_before = shift_ref[0], shift_ref[1]
    row = lax.broadcasted_iota(jnp.int32, (quota, quota), 0)
    col = lax.broadcasted_iota(jnp.int32, (quota, quota), 1)
    turned = row - shift_before
    turned = jnp.where(turned < 0, turned + quota, turned)
    hot_arrived = jnp.where((row < shift) & (col == turned), 1.0, 0.0)
    hot_local = jnp.where(col == row - shift, 1.0, 0.0)
    hot = jnp.concatenate([hot_arrived, hot_local], axis=1).astype(jnp.bfloat16)
    hot_ref[...] = hot
    out_ref[:, :NOTE] = place_rows(hot, arrived_ref[...], local_ref[...])
    docs = jnp.broadcast_to(docs_ref[...].astype(jnp.float32), (quota, quota))
    out_ref[:, NOTE:] = docs.astype(jnp.bfloat16)


def settle_kv(shift, docs, arrived, local):
    quota = arrived.shape[0]
    return pl.pallas_call(
        settle_kernel,
        in_specs=[SCALARS, WHOLE, WHOLE, WHOLE],
        out_specs=[WHOLE, WHOLE],
        out_shape=[
            jax.ShapeDtypeStruct((quota, NOTE + quota), jnp.bfloat16),
            jax.ShapeDtypeStruct((quota, 2 * quota), jnp.bfloat16),
        ],
        compiler_params=pltpu.CompilerParams(vmem_limit_bytes=VMEM_GRANT),
        name="settle_kv",
    )(shift, docs, arrived, local)


def block_ranks(rank, core, rounds):
    ranks = [rank]
    for back in range(1, rounds + 1):
        ranks.append(rank - 2 * back)
        if back < rounds:
            ranks.append(rank - 2 * back + jnp.where(core == 0, 1, -1))
    ranks.append(jnp.where(core == 0, rank - 2 * rounds + 1, rank - 1))
    return ranks


def head_columns(head, heads=1):
    return slice(head * HEAD_SIZE, (head + heads) * HEAD_SIZE)


def pieces(first, count):
    at, found = first, []
    while at < first + count:
        end = min(first + count, (at // GROUP + 1) * GROUP)
        heads = end - at
        if heads > HALF:
            heads = min(HALF, -(-heads // 2))
        found.append((at, heads))
        at += heads
    return found


def in_place(kernel, operands, out, more_out=(), more_specs=(), **arguments):
    specs = arguments.pop("in_specs") + [ANYWHERE]
    return pl.pallas_call(
        kernel,
        in_specs=specs,
        out_specs=[ANYWHERE, *more_specs],
        out_shape=[jax.ShapeDtypeStruct(out.shape, out.dtype), *more_out],
        input_output_aliases={len(operands): 0},
        cost_estimate=pl.CostEstimate(flops=0, bytes_accessed=0, transcendentals=0),
        compiler_params=pltpu.CompilerParams(vmem_limit_bytes=VMEM_GRANT),
        **arguments,
    )(*operands, out)


def place_kernel(first, hot_ref, arrived_ref, q_hbm, *refs):
    out_hbm, local, placed, in_sem, out_sem = refs[-5:]
    quota, width = arrived_ref.shape
    cols = head_columns(first, width // HEAD_SIZE)
    fetch = pltpu.make_async_copy(q_hbm.at[0, 0:quota, cols], local, in_sem)
    fetch.start()
    fetch.wait()
    for head, heads in pieces(first, width // HEAD_SIZE):
        own = head_columns(head - first, heads)
        placed[:, own] = place_rows(hot_ref[...], arrived_ref[:, own], local[:, own])
    store = pltpu.make_async_copy(placed, out_hbm.at[0, :, cols], out_sem)
    store.start()
    store.wait()


def place_queries(hot, arrived, q_rows, first, out):
    quota = arrived.shape[0]
    arguments = dict(
        in_specs=[WHOLE, WHOLE, ANYWHERE],
        scratch_shapes=[
            pltpu.VMEM(arrived.shape, jnp.bfloat16),
            pltpu.VMEM(arrived.shape, jnp.bfloat16),
            pltpu.SemaphoreType.DMA,
            pltpu.SemaphoreType.DMA,
        ],
        name="place_queries",
    )
    kernel = functools.partial(place_kernel, first)
    if out is not None:
        return in_place(kernel, [hot, arrived, q_rows], out, **arguments)[0]
    return pl.pallas_call(
        kernel,
        out_specs=ANYWHERE,
        out_shape=jax.ShapeDtypeStruct((1, quota, QUERY_HEADS * HEAD_SIZE), jnp.bfloat16),
        compiler_params=pltpu.CompilerParams(vmem_limit_bytes=VMEM_GRANT),
        **arguments,
    )(hot, arrived, q_rows)


def make_bias(kv_refs, far_ref, mate_ref, bias, rank):
    quota = bias.shape[0]
    core = lax.rem(rank, 2)
    row = lax.broadcasted_iota(jnp.int32, (quota, quota), 0)
    col = lax.broadcasted_iota(jnp.int32, (quota, quota), 1)
    note = slice(NOTE, NOTE + quota)
    q_docs = jnp.where(row == col, kv_refs[0][:, note].astype(jnp.float32), 0.0)
    q_docs = jnp.sum(q_docs, axis=1, keepdims=True)
    blocks = len(kv_refs) + 1
    for b, block_rank in enumerate(block_ranks(rank, core, (blocks - 1) // 2)):
        if b < blocks - 1:
            docs = kv_refs[b][:, note].astype(jnp.float32)
        else:
            far = far_ref[:, note].astype(jnp.float32)
            docs = jnp.where(core == 0, far, mate_ref[:, note].astype(jnp.float32))
        allowed = docs == q_docs
        allowed &= (col <= row) if b == 0 else (block_rank >= 0)
        bias[:, b * quota : (b + 1) * quota] = jnp.where(allowed, 0.0, MASKED)


def choose_rest(first, count, core, far_ref, mate_ref, rest):
    first_head, last_head = first // GROUP, (first + count - 1) // GROUP
    keys = head_columns(first_head, last_head - first_head + 1)
    values = slice(KV_WIDTH + keys.start, KV_WIDTH + keys.stop)

    @pl.when(core == 0)
    def _():
        rest[:, keys] = far_ref[:, keys]
        rest[:, values] = far_ref[:, values]

    @pl.when(core == 1)
    def _():
        rest[:, keys] = mate_ref[:, keys]
        rest[:, values] = mate_ref[:, values]


def attend_heads(first, steps, kv_refs, bias, take, result, after_first, before_last):
    quota = bias.shape[0]
    unit = math.log2(math.e) / math.sqrt(HEAD_SIZE)

    def key_head(head):
        cols = head_columns(head)
        keys = jnp.concatenate([r[:, cols] for r in kv_refs], axis=0)
        cols = head_columns(KEY_VALUE_HEADS + head)
        values = jnp.concatenate([r[:, cols] for r in kv_refs], axis=0)
        return keys, jnp.concatenate([values, jnp.ones_like(values)], axis=1)

    def scored(head, heads, keys):
        q = take(head_columns(head - first, heads))
        stacked = jnp.concatenate([q[:, head_columns(h)] for h in range(heads)], axis=0)
        return lax.dot_general(
            stacked, keys, (((1,), (1,)), ((), ())), preferred_element_type=jnp.float32
        )

    def finished(head, heads, scores, values):
        scores = scores.reshape(heads, quota, -1) * unit + bias[...][None]
        weights = jnp.exp2(scores - jnp.max(scores, axis=2, keepdims=True))
        weights = weights.astype(jnp.bfloat16).reshape(heads * quota, -1)
        mixed = jnp.dot(weights, values, preferred_element_type=jnp.float32)
        totals = mixed[:, HEAD_SIZE:]
        inverse = pl.reciprocal(totals, approx=True)
        inverse = inverse * (2.0 - totals * inverse)
        mixed = (mixed[:, :HEAD_SIZE] * inverse).astype(jnp.bfloat16)
        for h in range(heads):
            result[:, head_columns(head - first + h)] = mixed[h * quota : (h + 1) * quota]

    keys, values = key_head(steps[0][0] // GROUP)
    scores = scored(*steps[0], keys)
    after_first()
    for i, (head, heads) in enumerate(steps):
        own_values, later = values, None
        if i + 1 < len(steps):
            if steps[i + 1][0] // GROUP != head // GROUP:
                keys, values = key_head(steps[i + 1][0] // GROUP)
            later = scored(*steps[i + 1], keys)
        if i + 1 == len(steps):
            before_last()
        finished(head, heads, scores, own_values)
        scores = later


def early_kernel(blocks, count, rank_ref, *refs):
    kv_refs, far_ref, mate_ref = refs[: blocks - 1], refs[blocks - 1], refs[blocks]
    q_hbm, in_hbm, out_hbm, local, bias, rest, queries, result, sems = refs[blocks + 1 :]
    steps = pieces(0, count)
    edge, end = steps[0][1], steps[-1][0]

    def fetching(cols, sem):
        return pltpu.make_async_copy(in_hbm.at[0, :, cols], queries.at[:, cols], sem)

    def storing(cols, sem):
        return pltpu.make_async_copy(result.at[:, cols], out_hbm.at[0, :, cols], sem)

    fetch = fetching(head_columns(0, edge), sems.at[0])
    fetch_rest = fetching(head_columns(edge, count - edge), sems.at[1])
    store = storing(head_columns(0, end), sems.at[2])
    store_last = storing(head_columns(end, count - end), sems.at[3])
    others = head_columns(count, QUERY_HEADS - count)
    ahead = pltpu.make_async_copy(q_hbm.at[0, 0 : bias.shape[0], others], local, sems.at[4])
    fetch.start()
    fetch_rest.start()
    rank = rank_ref[0]
    make_bias(kv_refs, far_ref, mate_ref, bias, rank)
    choose_rest(0, count, lax.rem(rank, 2), far_ref, mate_ref, rest)
    fetch.wait()

    def after_first():
        fetch_rest.wait()
        ahead.start()

    attend_heads(
        0,
        steps,
        [*kv_refs, rest],
        bias,
        lambda cols: queries[:, cols],
        result,
        after_first,
        store.start,
    )
    store_last.start()
    store.wait()
    store_last.wait()
    ahead.wait()


def late_kernel(blocks, first, rank_ref, *refs):
    kv_refs, far_ref, mate_ref = refs[: blocks - 1], refs[blocks - 1], refs[blocks]
    hot_ref, arrived_hbm, local_ref, _, out_hbm = refs[blocks + 1 : blocks + 6]
    bias, rest, arrived, result, sems = refs[blocks + 6 :]
    count = QUERY_HEADS - first
    steps = pieces(first, count)[::-1]
    edge, end = steps[0][0], sum(steps[-1])

    def fetching(cols, sem):
        return pltpu.make_async_copy(arrived_hbm.at[:, cols], arrived.at[:, cols], sem)

    def storing(at, heads, sem):
        own = head_columns(at - first, heads)
        return pltpu.make_async_copy(
            result.at[:, own], out_hbm.at[0, :, head_columns(at, heads)], sem
        )

    fetch = fetching(head_columns(edge - first, QUERY_HEADS - edge), sems.at[0])
    fetch_rest = fetching(head_columns(0, edge - first), sems.at[1])
    store = storing(end, QUERY_HEADS - end, sems.at[2])
    store_last = storing(first, end - first, sems.at[3])
    fetch.start()
    fetch_rest.start()
    rank = rank_ref[0]
    make_bias(kv_refs, far_ref, mate_ref, bias, rank)
    choose_rest(first, count, lax.rem(rank, 2), far_ref, mate_ref, rest)
    fetch.wait()

    def take(cols):
        return place_rows(hot_ref[...], arrived[:, cols], local_ref[:, cols])

    attend_heads(
        first, steps, [*kv_refs, rest], bias, take, result, fetch_rest.wait, store.start
    )
    store_last.start()
    store.wait()
    store_last.wait()


def attend(rank, hot, arrived, q_rows, kv_blocks, out):
    quota, width = arrived.shape
    blocks = len(kv_blocks) - 1
    first = QUERY_HEADS - width // HEAD_SIZE
    bias = pltpu.VMEM((quota, blocks * quota), jnp.float32)
    rest = pltpu.VMEM((quota, NOTE), jnp.bfloat16)
    own = pltpu.VMEM(arrived.shape, jnp.bfloat16)
    others = pltpu.VMEM((quota, first * HEAD_SIZE), jnp.bfloat16)
    out, local = in_place(
        functools.partial(early_kernel, blocks, first),
        [rank, *kv_blocks, q_rows],
        out,
        more_out=[jax.ShapeDtypeStruct(arrived.shape, jnp.bfloat16)],
        more_specs=[WHOLE],
        in_specs=[SCALARS] + [WHOLE] * len(kv_blocks) + [ANYWHERE],
        scratch_shapes=[bias, rest, others, others, pltpu.SemaphoreType.DMA((5,))],
        name="attend_early",
    )
    return in_place(
        functools.partial(late_kernel, blocks, first),
        [rank, *kv_blocks, hot, arrived, local],
        out,
        in_specs=[SCALARS] + [WHOLE] * (len(kv_blocks) + 1) + [ANYWHERE, WHOLE],
        scratch_shapes=[bias, rest, own, own, pltpu.SemaphoreType.DMA((4,))],
        name="attend_late",
    )[0]


def circular_tail(rows, later):
    quota = later.shape[0]
    return jnp.where(later[:, None], rows[quota:], rows[:quota])


def sent(rows, later):
    if lax.axis_size("dp") > 4:
        return circular_tail(rows, later)
    return rows[later.shape[0] :]


def body(q_rows, k_rows, value_slot_rows, counts, doc_ids):
    quota = doc_ids.shape[1]
    rounds = lax.axis_size("ctx") // 4
    rank = lax.axis_index("ctx")
    own_count = counts[0, 0]

    later = quota + jnp.arange(quota, dtype=jnp.int32) < own_count
    k_local, v_local = k_rows[0], value_slot_rows[0]
    kv_tail = jnp.concatenate([sent(k_local, later), sent(v_local, later)], axis=1)
    arrived_kv = shifted(kv_tail, "dp", 1)
    zero = (kv_tail[:1, :1] + kv_tail[:1, -1:]) * 0
    local_kv = jnp.concatenate([k_local[:quota] + zero, v_local[:quota] + zero], axis=1)
    local_kv, zero = lax.optimization_barrier((local_kv, zero))
    q_tails = []
    first = 0
    for size in CHUNKS:
        q_tails.append(sent(q_rows[0, :, head_columns(first, size)], later) + zero)
        first += size
    q_tails = lax.optimization_barrier(q_tails)
    arrived_q = [shifted(tail, "dp", 1) for tail in q_tails]

    shift = shifts_in(own_count, quota)
    own, hot = settle_kv(shift, doc_ids, arrived_kv, local_kv)

    kv_blocks = [own]
    carried, out = own, None
    for back in range(1, rounds + 1):
        carried = shifted(carried, "ctx", 2)
        kv_blocks.append(carried)
        if back < len(CHUNKS):
            first = sum(CHUNKS[: back - 1])
            out = place_queries(hot, arrived_q[back - 1], q_rows, first, out)
            carried, out = lax.optimization_barrier((carried, out))
        if back < rounds:
            kv_blocks.append(across_cores(carried))
    kv_blocks += [across_cores(carried), across_cores(own, (0,))]
    return attend(rank[None], hot, arrived_q[-1], q_rows, kv_blocks, out)


def solution(mesh):
    return jax.shard_map(
        body,
        mesh=mesh,
        in_specs=(
            P("dp", "ctx", None),
            P("dp", "ctx", None),
            P("dp", "ctx", None),
            P("dp", "ctx"),
            P("dp", "ctx"),
        ),
        out_specs=P("dp", "ctx", None),
        check_vma=False,
    )
```

```python
import functools
import math

import jax
import jax.numpy as jnp
from jax import lax
from jax.experimental import pallas as pl
from jax.experimental.pallas import tpu as pltpu
from jax.sharding import PartitionSpec as P

QUERY_HEADS = 64
KEY_VALUE_HEADS = 8
HEAD_SIZE = 128
GROUP = QUERY_HEADS // KEY_VALUE_HEADS
KV_WIDTH = KEY_VALUE_HEADS * HEAD_SIZE
NOTE = 2 * KV_WIDTH
MASKED = -1e30
HALF = GROUP // 2
CHUNKS = (20, 25, 19)
VMEM_GRANT = 30 * 1024 * 1024

WHOLE = pl.BlockSpec(memory_space=pltpu.VMEM)
ANYWHERE = pl.BlockSpec(memory_space=pl.ANY)
SCALARS = pl.BlockSpec(memory_space=pltpu.SMEM)


def shifted(x, axis, steps):
    n = lax.axis_size(axis)
    return lax.ppermute(x, axis, [(i, i + steps) for i in range(n - steps)])


def across_cores(x, sources=(0, 1)):
    n = lax.axis_size("ctx")
    return lax.ppermute(x, "ctx", [(i, i ^ 1) for i in range(n) if i % 2 in sources])


def everyones(x, axis):
    n = lax.axis_size(axis)
    spread = jnp.broadcast_to(x[None], (n,) + x.shape)
    return lax.all_to_all(spread, axis, split_axis=0, concat_axis=0)


def shifts_in(own_count, quota):
    n = lax.axis_size("dp")
    replica = lax.axis_index("dp")
    if n > 4:
        all_counts = everyones(own_count[None], "dp")[:, 0]
        places = jnp.arange(n, dtype=jnp.int32)
        before = jnp.sum(jnp.where(places < replica, all_counts, 0))
        before_last = jnp.sum(jnp.where(places < replica - 1, all_counts, 0))
        return jnp.stack([before - replica * quota, before_last - (replica - 1) * quota])
    return jnp.stack([jnp.maximum(quota - own_count, 0), jnp.int32(0)])


def place_rows(hot, arrived, local):
    both = jnp.concatenate([arrived, local], axis=0)
    return jnp.dot(hot, both, preferred_element_type=jnp.float32).astype(jnp.bfloat16)


def settle_kernel(shift_ref, docs_ref, arrived_ref, local_ref, out_ref, hot_ref):
    quota = out_ref.shape[0]
    shift, shift_before = shift_ref[0], shift_ref[1]
    row = lax.broadcasted_iota(jnp.int32, (quota, quota), 0)
    col = lax.broadcasted_iota(jnp.int32, (quota, quota), 1)
    turned = row - shift_before
    turned = jnp.where(turned < 0, turned + quota, turned)
    hot_arrived = jnp.where((row < shift) & (col == turned), 1.0, 0.0)
    hot_local = jnp.where(col == row - shift, 1.0, 0.0)
    hot = jnp.concatenate([hot_arrived, hot_local], axis=1).astype(jnp.bfloat16)
    hot_ref[...] = hot
    out_ref[:, :NOTE] = place_rows(hot, arrived_ref[...], local_ref[...])
    docs = jnp.broadcast_to(docs_ref[...].astype(jnp.float32), (quota, quota))
    out_ref[:, NOTE:] = docs.astype(jnp.bfloat16)


def settle_kv(shift, docs, arrived, local):
    quota = arrived.shape[0]
    return pl.pallas_call(
        settle_kernel,
        in_specs=[SCALARS, WHOLE, WHOLE, WHOLE],
        out_specs=[WHOLE, WHOLE],
        out_shape=[
            jax.ShapeDtypeStruct((quota, NOTE + quota), jnp.bfloat16),
            jax.ShapeDtypeStruct((quota, 2 * quota), jnp.bfloat16),
        ],
        compiler_params=pltpu.CompilerParams(vmem_limit_bytes=VMEM_GRANT),
        name="settle_kv",
    )(shift, docs, arrived, local)


def block_ranks(rank, core, rounds):
    ranks = [rank]
    for back in range(1, rounds + 1):
        ranks.append(rank - 2 * back)
        if back < rounds:
            ranks.append(rank - 2 * back + jnp.where(core == 0, 1, -1))
    ranks.append(jnp.where(core == 0, rank - 2 * rounds + 1, rank - 1))
    return ranks


def head_columns(head, heads=1):
    return slice(head * HEAD_SIZE, (head + heads) * HEAD_SIZE)


def pieces(first, count):
    at, found = first, []
    while at < first + count:
        end = min(first + count, (at // GROUP + 1) * GROUP)
        heads = end - at
        if heads > HALF:
            heads = min(HALF, -(-heads // 2))
        found.append((at, heads))
        at += heads
    return found


def in_place(kernel, operands, out, more_out=(), more_specs=(), **arguments):
    specs = arguments.pop("in_specs") + [ANYWHERE]
    return pl.pallas_call(
        kernel,
        in_specs=specs,
        out_specs=[ANYWHERE, *more_specs],
        out_shape=[jax.ShapeDtypeStruct(out.shape, out.dtype), *more_out],
        input_output_aliases={len(operands): 0},
        cost_estimate=pl.CostEstimate(flops=0, bytes_accessed=0, transcendentals=0),
        compiler_params=pltpu.CompilerParams(vmem_limit_bytes=VMEM_GRANT),
        **arguments,
    )(*operands, out)


def place_kernel(first, hot_ref, arrived_ref, q_hbm, *refs):
    out_hbm, local, placed, in_sem, out_sem = refs[-5:]
    quota, width = arrived_ref.shape
    cols = head_columns(first, width // HEAD_SIZE)
    fetch = pltpu.make_async_copy(q_hbm.at[0, 0:quota, cols], local, in_sem)
    fetch.start()
    fetch.wait()
    for head, heads in pieces(first, width // HEAD_SIZE):
        own = head_columns(head - first, heads)
        placed[:, own] = place_rows(hot_ref[...], arrived_ref[:, own], local[:, own])
    store = pltpu.make_async_copy(placed, out_hbm.at[0, :, cols], out_sem)
    store.start()
    store.wait()


def place_queries(hot, arrived, q_rows, first, out):
    quota = arrived.shape[0]
    arguments = dict(
        in_specs=[WHOLE, WHOLE, ANYWHERE],
        scratch_shapes=[
            pltpu.VMEM(arrived.shape, jnp.bfloat16),
            pltpu.VMEM(arrived.shape, jnp.bfloat16),
            pltpu.SemaphoreType.DMA,
            pltpu.SemaphoreType.DMA,
        ],
        name="place_queries",
    )
    kernel = functools.partial(place_kernel, first)
    if out is not None:
        return in_place(kernel, [hot, arrived, q_rows], out, **arguments)[0]
    return pl.pallas_call(
        kernel,
        out_specs=ANYWHERE,
        out_shape=jax.ShapeDtypeStruct((1, quota, QUERY_HEADS * HEAD_SIZE), jnp.bfloat16),
        compiler_params=pltpu.CompilerParams(vmem_limit_bytes=VMEM_GRANT),
        **arguments,
    )(hot, arrived, q_rows)


def make_bias(kv_refs, far_ref, mate_ref, bias, rank):
    quota = bias.shape[0]
    core = lax.rem(rank, 2)
    row = lax.broadcasted_iota(jnp.int32, (quota, quota), 0)
    col = lax.broadcasted_iota(jnp.int32, (quota, quota), 1)
    note = slice(NOTE, NOTE + quota)
    q_docs = jnp.where(row == col, kv_refs[0][:, note].astype(jnp.float32), 0.0)
    q_docs = jnp.sum(q_docs, axis=1, keepdims=True)
    blocks = len(kv_refs) + 1
    for b, block_rank in enumerate(block_ranks(rank, core, (blocks - 1) // 2)):
        if b < blocks - 1:
            docs = kv_refs[b][:, note].astype(jnp.float32)
        else:
            far = far_ref[:, note].astype(jnp.float32)
            docs = jnp.where(core == 0, far, mate_ref[:, note].astype(jnp.float32))
        allowed = docs == q_docs
        allowed &= (col <= row) if b == 0 else (block_rank >= 0)
        bias[:, b * quota : (b + 1) * quota] = jnp.where(allowed, 0.0, MASKED)


def choose_rest(first, count, core, far_ref, mate_ref, rest):
    first_head, last_head = first // GROUP, (first + count - 1) // GROUP
    keys = head_columns(first_head, last_head - first_head + 1)
    values = slice(KV_WIDTH + keys.start, KV_WIDTH + keys.stop)

    @pl.when(core == 0)
    def _():
        rest[:, keys] = far_ref[:, keys]
        rest[:, values] = far_ref[:, values]

    @pl.when(core == 1)
    def _():
        rest[:, keys] = mate_ref[:, keys]
        rest[:, values] = mate_ref[:, values]


def attend_heads(first, steps, kv_refs, bias, take, result, after_first, before_last):
    quota = bias.shape[0]
    unit = math.log2(math.e) / math.sqrt(HEAD_SIZE)

    def key_head(head):
        cols = head_columns(head)
        keys = jnp.concatenate([r[:, cols] for r in kv_refs], axis=0)
        cols = head_columns(KEY_VALUE_HEADS + head)
        values = jnp.concatenate([r[:, cols] for r in kv_refs], axis=0)
        return keys, jnp.concatenate([values, jnp.ones_like(values)], axis=1)

    def scored(head, heads, keys):
        q = take(head_columns(head - first, heads))
        stacked = jnp.concatenate([q[:, head_columns(h)] for h in range(heads)], axis=0)
        return lax.dot_general(
            stacked, keys, (((1,), (1,)), ((), ())), preferred_element_type=jnp.float32
        )

    def finished(head, heads, scores, values):
        scores = scores.reshape(heads, quota, -1) * unit + bias[...][None]
        weights = jnp.exp2(scores - jnp.max(scores, axis=2, keepdims=True))
        weights = weights.astype(jnp.bfloat16).reshape(heads * quota, -1)
        mixed = jnp.dot(weights, values, preferred_element_type=jnp.float32)
        totals = mixed[:, HEAD_SIZE:]
        inverse = pl.reciprocal(totals, approx=True)
        inverse = inverse * (2.0 - totals * inverse)
        mixed = (mixed[:, :HEAD_SIZE] * inverse).astype(jnp.bfloat16)
        for h in range(heads):
            result[:, head_columns(head - first + h)] = mixed[h * quota : (h + 1) * quota]

    keys, values = key_head(steps[0][0] // GROUP)
    scores = scored(*steps[0], keys)
    after_first()
    for i, (head, heads) in enumerate(steps):
        own_values, later = values, None
        if i + 1 < len(steps):
            if steps[i + 1][0] // GROUP != head // GROUP:
                keys, values = key_head(steps[i + 1][0] // GROUP)
            later = scored(*steps[i + 1], keys)
        if i + 1 == len(steps):
            before_last()
        finished(head, heads, scores, own_values)
        scores = later


def early_kernel(blocks, count, rank_ref, *refs):
    kv_refs, far_ref, mate_ref = refs[: blocks - 1], refs[blocks - 1], refs[blocks]
    q_hbm, in_hbm, out_hbm, local, bias, rest, queries, result, sems = refs[blocks + 1 :]
    steps = pieces(0, count)
    edge, end = steps[0][1], steps[-1][0]

    def fetching(cols, sem):
        return pltpu.make_async_copy(in_hbm.at[0, :, cols], queries.at[:, cols], sem)

    def storing(cols, sem):
        return pltpu.make_async_copy(result.at[:, cols], out_hbm.at[0, :, cols], sem)

    fetch = fetching(head_columns(0, edge), sems.at[0])
    fetch_rest = fetching(head_columns(edge, count - edge), sems.at[1])
    store = storing(head_columns(0, end), sems.at[2])
    store_last = storing(head_columns(end, count - end), sems.at[3])
    others = head_columns(count, QUERY_HEADS - count)
    ahead = pltpu.make_async_copy(q_hbm.at[0, 0 : bias.shape[0], others], local, sems.at[4])
    fetch.start()
    fetch_rest.start()
    rank = rank_ref[0]
    make_bias(kv_refs, far_ref, mate_ref, bias, rank)
    choose_rest(0, count, lax.rem(rank, 2), far_ref, mate_ref, rest)
    fetch.wait()

    def after_first():
        fetch_rest.wait()
        ahead.start()

    attend_heads(
        0,
        steps,
        [*kv_refs, rest],
        bias,
        lambda cols: queries[:, cols],
        result,
        after_first,
        store.start,
    )
    store_last.start()
    store.wait()
    store_last.wait()
    ahead.wait()


def late_kernel(blocks, first, rank_ref, *refs):
    kv_refs, far_ref, mate_ref = refs[: blocks - 1], refs[blocks - 1], refs[blocks]
    hot_ref, arrived_hbm, local_ref, _, out_hbm = refs[blocks + 1 : blocks + 6]
    bias, rest, arrived, result, sems = refs[blocks + 6 :]
    count = QUERY_HEADS - first
    steps = pieces(first, count)[::-1]
    edge, end = steps[0][0], sum(steps[-1])

    def fetching(cols, sem):
        return pltpu.make_async_copy(arrived_hbm.at[:, cols], arrived.at[:, cols], sem)

    def storing(at, heads, sem):
        own = head_columns(at - first, heads)
        return pltpu.make_async_copy(
            result.at[:, own], out_hbm.at[0, :, head_columns(at, heads)], sem
        )

    fetch = fetching(head_columns(edge - first, QUERY_HEADS - edge), sems.at[0])
    fetch_rest = fetching(head_columns(0, edge - first), sems.at[1])
    store = storing(end, QUERY_HEADS - end, sems.at[2])
    store_last = storing(first, end - first, sems.at[3])
    fetch.start()
    fetch_rest.start()
    rank = rank_ref[0]
    make_bias(kv_refs, far_ref, mate_ref, bias, rank)
    choose_rest(first, count, lax.rem(rank, 2), far_ref, mate_ref, rest)
    fetch.wait()

    def take(cols):
        return place_rows(hot_ref[...], arrived[:, cols], local_ref[:, cols])

    attend_heads(
        first, steps, [*kv_refs, rest], bias, take, result, fetch_rest.wait, store.start
    )
    store_last.start()
    store.wait()
    store_last.wait()


def attend(rank, hot, arrived, q_rows, kv_blocks, out):
    quota, width = arrived.shape
    blocks = len(kv_blocks) - 1
    first = QUERY_HEADS - width // HEAD_SIZE
    bias = pltpu.VMEM((quota, blocks * quota), jnp.float32)
    rest = pltpu.VMEM((quota, NOTE), jnp.bfloat16)
    own = pltpu.VMEM(arrived.shape, jnp.bfloat16)
    others = pltpu.VMEM((quota, first * HEAD_SIZE), jnp.bfloat16)
    out, local = in_place(
        functools.partial(early_kernel, blocks, first),
        [rank, *kv_blocks, q_rows],
        out,
        more_out=[jax.ShapeDtypeStruct(arrived.shape, jnp.bfloat16)],
        more_specs=[WHOLE],
        in_specs=[SCALARS] + [WHOLE] * len(kv_blocks) + [ANYWHERE],
        scratch_shapes=[bias, rest, others, others, pltpu.SemaphoreType.DMA((5,))],
        name="attend_early",
    )
    return in_place(
        functools.partial(late_kernel, blocks, first),
        [rank, *kv_blocks, hot, arrived, local],
        out,
        in_specs=[SCALARS] + [WHOLE] * (len(kv_blocks) + 1) + [ANYWHERE, WHOLE],
        scratch_shapes=[bias, rest, own, own, pltpu.SemaphoreType.DMA((4,))],
        name="attend_late",
    )[0]


def circular_tail(rows, later):
    quota = later.shape[0]
    return jnp.where(later[:, None], rows[quota:], rows[:quota])


def sent(rows, later):
    if lax.axis_size("dp") > 4:
        return circular_tail(rows, later)
    return rows[later.shape[0] :]


def body(q_rows, k_rows, value_slot_rows, counts, doc_ids):
    quota = doc_ids.shape[1]
    rounds = lax.axis_size("ctx") // 4
    rank = lax.axis_index("ctx")
    own_count = counts[0, 0]

    later = quota + jnp.arange(quota, dtype=jnp.int32) < own_count
    k_local, v_local = k_rows[0], value_slot_rows[0]
    kv_tail = jnp.concatenate([sent(k_local, later), sent(v_local, later)], axis=1)
    arrived_kv = shifted(kv_tail, "dp", 1)
    zero = (kv_tail[:1, :1] + kv_tail[:1, -1:]) * 0
    local_kv = jnp.concatenate([k_local[:quota] + zero, v_local[:quota] + zero], axis=1)
    local_kv, zero = lax.optimization_barrier((local_kv, zero))
    q_tails = []
    first = 0
    for size in CHUNKS:
        q_tails.append(sent(q_rows[0, :, head_columns(first, size)], later) + zero)
        first += size
    q_tails = lax.optimization_barrier(q_tails)
    arrived_q = [shifted(tail, "dp", 1) for tail in q_tails]

    shift = shifts_in(own_count, quota)
    own, hot = settle_kv(shift, doc_ids, arrived_kv, local_kv)

    kv_blocks = [own]
    carried, out = own, None
    for back in range(1, rounds + 1):
        carried = shifted(carried, "ctx", 2)
        kv_blocks.append(carried)
        if back < len(CHUNKS):
            first = sum(CHUNKS[: back - 1])
            out = place_queries(hot, arrived_q[back - 1], q_rows, first, out)
            carried, out = lax.optimization_barrier((carried, out))
        if back < rounds:
            kv_blocks.append(across_cores(carried))
    kv_blocks += [across_cores(carried), across_cores(own, (0,))]
    return attend(rank[None], hot, arrived_q[-1], q_rows, kv_blocks, out)


def solution(mesh):
    return jax.shard_map(
        body,
        mesh=mesh,
        in_specs=(
            P("dp", "ctx", None),
            P("dp", "ctx", None),
            P("dp", "ctx", None),
            P("dp", "ctx"),
            P("dp", "ctx"),
        ),
        out_specs=P("dp", "ctx", None),
        check_vma=False,
    )
```

```python
import functools
import math

import jax
import jax.numpy as jnp
from jax import lax
from jax.experimental import pallas as pl
from jax.experimental.pallas import tpu as pltpu
from jax.sharding import PartitionSpec as P

QUERY_HEADS = 64
KEY_VALUE_HEADS = 8
HEAD_SIZE = 128
GROUP = QUERY_HEADS // KEY_VALUE_HEADS
KV_WIDTH = KEY_VALUE_HEADS * HEAD_SIZE
NOTE = 2 * KV_WIDTH
MASKED = -1e30
HALF = GROUP // 2
CHUNKS = (20, 26, 18)
VMEM_GRANT = 48 * 1024 * 1024

WHOLE = pl.BlockSpec(memory_space=pltpu.VMEM)
ANYWHERE = pl.BlockSpec(memory_space=pl.ANY)
SCALARS = pl.BlockSpec(memory_space=pltpu.SMEM)


def shifted(x, axis, steps):
    n = lax.axis_size(axis)
    return lax.ppermute(x, axis, [(i, i + steps) for i in range(n - steps)])


def across_cores(x, sources=(0, 1)):
    n = lax.axis_size("ctx")
    return lax.ppermute(x, "ctx", [(i, i ^ 1) for i in range(n) if i % 2 in sources])


def everyones(x, axis):
    n = lax.axis_size(axis)
    spread = jnp.broadcast_to(x[None], (n,) + x.shape)
    return lax.all_to_all(spread, axis, split_axis=0, concat_axis=0)


def shifts_in(own_count, quota):
    n = lax.axis_size("dp")
    replica = lax.axis_index("dp")
    if n > 4:
        all_counts = everyones(own_count[None], "dp")[:, 0]
        places = jnp.arange(n, dtype=jnp.int32)
        before = jnp.sum(jnp.where(places < replica, all_counts, 0))
        before_last = jnp.sum(jnp.where(places < replica - 1, all_counts, 0))
        return jnp.stack([before - replica * quota, before_last - (replica - 1) * quota])
    return jnp.stack([jnp.maximum(quota - own_count, 0), jnp.int32(0)])


def place_rows(hot, arrived, local):
    both = jnp.concatenate([arrived, local], axis=0)
    return jnp.dot(hot, both, preferred_element_type=jnp.float32).astype(jnp.bfloat16)


def settle_kernel(shift_ref, docs_ref, arrived_ref, local_ref, out_ref, hot_ref):
    quota = out_ref.shape[0]
    shift, shift_before = shift_ref[0], shift_ref[1]
    row = lax.broadcasted_iota(jnp.int32, (quota, quota), 0)
    col = lax.broadcasted_iota(jnp.int32, (quota, quota), 1)
    turned = row - shift_before
    turned = jnp.where(turned < 0, turned + quota, turned)
    hot_arrived = jnp.where((row < shift) & (col == turned), 1.0, 0.0)
    hot_local = jnp.where(col == row - shift, 1.0, 0.0)
    hot = jnp.concatenate([hot_arrived, hot_local], axis=1).astype(jnp.bfloat16)
    hot_ref[...] = hot
    out_ref[:, :NOTE] = place_rows(hot, arrived_ref[...], local_ref[...])
    docs = jnp.broadcast_to(docs_ref[...].astype(jnp.float32), (quota, quota))
    out_ref[:, NOTE:] = docs.astype(jnp.bfloat16)


def settle_kv(shift, docs, arrived, local):
    quota = arrived.shape[0]
    return pl.pallas_call(
        settle_kernel,
        in_specs=[SCALARS, WHOLE, WHOLE, WHOLE],
        out_specs=[WHOLE, WHOLE],
        out_shape=[
            jax.ShapeDtypeStruct((quota, NOTE + quota), jnp.bfloat16),
            jax.ShapeDtypeStruct((quota, 2 * quota), jnp.bfloat16),
        ],
        compiler_params=pltpu.CompilerParams(vmem_limit_bytes=VMEM_GRANT),
        name="settle_kv",
    )(shift, docs, arrived, local)


def block_ranks(rank, core, rounds):
    ranks = [rank]
    for back in range(1, rounds + 1):
        ranks.append(rank - 2 * back)
        if back < rounds:
            ranks.append(rank - 2 * back + jnp.where(core == 0, 1, -1))
    ranks.append(jnp.where(core == 0, rank - 2 * rounds + 1, rank - 1))
    return ranks


def head_columns(head, heads=1):
    return slice(head * HEAD_SIZE, (head + heads) * HEAD_SIZE)


def pieces(first, count):
    at, found = first, []
    while at < first + count:
        end = min(first + count, (at // GROUP + 1) * GROUP)
        heads = end - at
        if heads > HALF:
            heads = min(HALF, -(-heads // 2))
        found.append((at, heads))
        at += heads
    return found


def in_place(kernel, operands, out, more_out=(), more_specs=(), **arguments):
    specs = arguments.pop("in_specs") + [ANYWHERE]
    return pl.pallas_call(
        kernel,
        in_specs=specs,
        out_specs=[ANYWHERE, *more_specs],
        out_shape=[jax.ShapeDtypeStruct(out.shape, out.dtype), *more_out],
        input_output_aliases={len(operands): 0},
        cost_estimate=pl.CostEstimate(flops=0, bytes_accessed=0, transcendentals=0),
        compiler_params=pltpu.CompilerParams(vmem_limit_bytes=VMEM_GRANT),
        **arguments,
    )(*operands, out)


def place_kernel(first, hot_ref, arrived_ref, q_hbm, *refs):
    out_hbm, local, placed, in_sem, out_sem = refs[-5:]
    quota, width = arrived_ref.shape
    cols = head_columns(first, width // HEAD_SIZE)
    fetch = pltpu.make_async_copy(q_hbm.at[0, 0:quota, cols], local, in_sem)
    fetch.start()
    fetch.wait()
    for head, heads in pieces(first, width // HEAD_SIZE):
        own = head_columns(head - first, heads)
        placed[:, own] = place_rows(hot_ref[...], arrived_ref[:, own], local[:, own])
    store = pltpu.make_async_copy(placed, out_hbm.at[0, :, cols], out_sem)
    store.start()
    store.wait()


def place_queries(hot, arrived, q_rows, first, out):
    quota = arrived.shape[0]
    arguments = dict(
        in_specs=[WHOLE, WHOLE, ANYWHERE],
        scratch_shapes=[
            pltpu.VMEM(arrived.shape, jnp.bfloat16),
            pltpu.VMEM(arrived.shape, jnp.bfloat16),
            pltpu.SemaphoreType.DMA,
            pltpu.SemaphoreType.DMA,
        ],
        name="place_queries",
    )
    kernel = functools.partial(place_kernel, first)
    if out is not None:
        return in_place(kernel, [hot, arrived, q_rows], out, **arguments)[0]
    return pl.pallas_call(
        kernel,
        out_specs=ANYWHERE,
        out_shape=jax.ShapeDtypeStruct((1, quota, QUERY_HEADS * HEAD_SIZE), jnp.bfloat16),
        compiler_params=pltpu.CompilerParams(vmem_limit_bytes=VMEM_GRANT),
        **arguments,
    )(hot, arrived, q_rows)


def make_bias(kv_refs, far_ref, mate_ref, bias, rank):
    quota = bias.shape[0]
    core = lax.rem(rank, 2)
    row = lax.broadcasted_iota(jnp.int32, (quota, quota), 0)
    col = lax.broadcasted_iota(jnp.int32, (quota, quota), 1)
    note = slice(NOTE, NOTE + quota)
    q_docs = jnp.where(row == col, kv_refs[0][:, note].astype(jnp.float32), 0.0)
    q_docs = jnp.sum(q_docs, axis=1, keepdims=True)
    blocks = len(kv_refs) + 1
    for b, block_rank in enumerate(block_ranks(rank, core, (blocks - 1) // 2)):
        if b < blocks - 1:
            docs = kv_refs[b][:, note].astype(jnp.float32)
        else:
            far = far_ref[:, note].astype(jnp.float32)
            docs = jnp.where(core == 0, far, mate_ref[:, note].astype(jnp.float32))
        allowed = docs == q_docs
        allowed &= (col <= row) if b == 0 else (block_rank >= 0)
        bias[:, b * quota : (b + 1) * quota] = jnp.where(allowed, 0.0, MASKED)


def choose_rest(first, count, core, far_ref, mate_ref, rest):
    first_head, last_head = first // GROUP, (first + count - 1) // GROUP
    keys = head_columns(first_head, last_head - first_head + 1)
    values = slice(KV_WIDTH + keys.start, KV_WIDTH + keys.stop)

    @pl.when(core == 0)
    def _():
        rest[:, keys] = far_ref[:, keys]
        rest[:, values] = far_ref[:, values]

    @pl.when(core == 1)
    def _():
        rest[:, keys] = mate_ref[:, keys]
        rest[:, values] = mate_ref[:, values]


def attend_heads(first, steps, kv_refs, bias, take, result, after_first, before_last):
    quota = bias.shape[0]
    unit = math.log2(math.e) / math.sqrt(HEAD_SIZE)

    def key_head(head):
        cols = head_columns(head)
        keys = jnp.concatenate([r[:, cols] for r in kv_refs], axis=0)
        cols = head_columns(KEY_VALUE_HEADS + head)
        values = jnp.concatenate([r[:, cols] for r in kv_refs], axis=0)
        return keys, jnp.concatenate([values, jnp.ones_like(values)], axis=1)

    def scored(head, heads, keys):
        q = take(head_columns(head - first, heads))
        stacked = jnp.concatenate([q[:, head_columns(h)] for h in range(heads)], axis=0)
        return lax.dot_general(
            stacked, keys, (((1,), (1,)), ((), ())), preferred_element_type=jnp.float32
        )

    def finished(head, heads, scores, values):
        scores = scores.reshape(heads, quota, -1) * unit + bias[...][None]
        weights = jnp.exp2(scores - jnp.max(scores, axis=2, keepdims=True))
        weights = weights.astype(jnp.bfloat16).reshape(heads * quota, -1)
        mixed = jnp.dot(weights, values, preferred_element_type=jnp.float32)
        totals = mixed[:, HEAD_SIZE:]
        inverse = pl.reciprocal(totals, approx=True)
        inverse = inverse * (2.0 - totals * inverse)
        mixed = (mixed[:, :HEAD_SIZE] * inverse).astype(jnp.bfloat16)
        for h in range(heads):
            result[:, head_columns(head - first + h)] = mixed[h * quota : (h + 1) * quota]

    keys, values = key_head(steps[0][0] // GROUP)
    scores = scored(*steps[0], keys)
    after_first()
    for i, (head, heads) in enumerate(steps):
        own_values, later = values, None
        if i + 1 < len(steps):
            if steps[i + 1][0] // GROUP != head // GROUP:
                keys, values = key_head(steps[i + 1][0] // GROUP)
            later = scored(*steps[i + 1], keys)
        if i + 1 == len(steps):
            before_last()
        finished(head, heads, scores, own_values)
        scores = later


def early_kernel(blocks, count, rank_ref, *refs):
    kv_refs, far_ref, mate_ref = refs[: blocks - 1], refs[blocks - 1], refs[blocks]
    q_hbm, in_hbm, out_hbm, local, bias, rest, queries, result, sems = refs[blocks + 1 :]
    steps = pieces(0, count)
    edge, end = steps[0][1], steps[-1][0]

    def fetching(cols, sem):
        return pltpu.make_async_copy(in_hbm.at[0, :, cols], queries.at[:, cols], sem)

    def storing(cols, sem):
        return pltpu.make_async_copy(result.at[:, cols], out_hbm.at[0, :, cols], sem)

    fetch = fetching(head_columns(0, edge), sems.at[0])
    fetch_rest = fetching(head_columns(edge, count - edge), sems.at[1])
    store = storing(head_columns(0, end), sems.at[2])
    store_last = storing(head_columns(end, count - end), sems.at[3])
    others = head_columns(count, QUERY_HEADS - count)
    ahead = pltpu.make_async_copy(q_hbm.at[0, 0 : bias.shape[0], others], local, sems.at[4])
    fetch.start()
    fetch_rest.start()
    rank = rank_ref[0]
    make_bias(kv_refs, far_ref, mate_ref, bias, rank)
    choose_rest(0, count, lax.rem(rank, 2), far_ref, mate_ref, rest)
    fetch.wait()

    def after_first():
        fetch_rest.wait()
        ahead.start()

    attend_heads(
        0,
        steps,
        [*kv_refs, rest],
        bias,
        lambda cols: queries[:, cols],
        result,
        after_first,
        store.start,
    )
    store_last.start()
    store.wait()
    store_last.wait()
    ahead.wait()


def late_kernel(blocks, first, rank_ref, *refs):
    kv_refs, far_ref, mate_ref = refs[: blocks - 1], refs[blocks - 1], refs[blocks]
    hot_ref, arrived_hbm, local_ref, _, out_hbm = refs[blocks + 1 : blocks + 6]
    bias, rest, arrived, result, sems = refs[blocks + 6 :]
    count = QUERY_HEADS - first
    steps = pieces(first, count)[::-1]
    edge, end = steps[0][0], sum(steps[-1])

    def fetching(cols, sem):
        return pltpu.make_async_copy(arrived_hbm.at[:, cols], arrived.at[:, cols], sem)

    def storing(at, heads, sem):
        own = head_columns(at - first, heads)
        return pltpu.make_async_copy(
            result.at[:, own], out_hbm.at[0, :, head_columns(at, heads)], sem
        )

    fetch = fetching(head_columns(edge - first, QUERY_HEADS - edge), sems.at[0])
    fetch_rest = fetching(head_columns(0, edge - first), sems.at[1])
    store = storing(end, QUERY_HEADS - end, sems.at[2])
    store_last = storing(first, end - first, sems.at[3])
    fetch.start()
    fetch_rest.start()
    rank = rank_ref[0]
    make_bias(kv_refs, far_ref, mate_ref, bias, rank)
    choose_rest(first, count, lax.rem(rank, 2), far_ref, mate_ref, rest)
    fetch.wait()

    def take(cols):
        return place_rows(hot_ref[...], arrived[:, cols], local_ref[:, cols])

    attend_heads(
        first, steps, [*kv_refs, rest], bias, take, result, fetch_rest.wait, store.start
    )
    store_last.start()
    store.wait()
    store_last.wait()


def attend(rank, hot, arrived, q_rows, kv_blocks, out):
    quota, width = arrived.shape
    blocks = len(kv_blocks) - 1
    first = QUERY_HEADS - width // HEAD_SIZE
    bias = pltpu.VMEM((quota, blocks * quota), jnp.float32)
    rest = pltpu.VMEM((quota, NOTE), jnp.bfloat16)
    own = pltpu.VMEM(arrived.shape, jnp.bfloat16)
    others = pltpu.VMEM((quota, first * HEAD_SIZE), jnp.bfloat16)
    out, local = in_place(
        functools.partial(early_kernel, blocks, first),
        [rank, *kv_blocks, q_rows],
        out,
        more_out=[jax.ShapeDtypeStruct(arrived.shape, jnp.bfloat16)],
        more_specs=[WHOLE],
        in_specs=[SCALARS] + [WHOLE] * len(kv_blocks) + [ANYWHERE],
        scratch_shapes=[bias, rest, others, others, pltpu.SemaphoreType.DMA((5,))],
        name="attend_early",
    )
    return in_place(
        functools.partial(late_kernel, blocks, first),
        [rank, *kv_blocks, hot, arrived, local],
        out,
        in_specs=[SCALARS] + [WHOLE] * (len(kv_blocks) + 1) + [ANYWHERE, WHOLE],
        scratch_shapes=[bias, rest, own, own, pltpu.SemaphoreType.DMA((4,))],
        name="attend_late",
    )[0]


def circular_tail(rows, later):
    quota = later.shape[0]
    return jnp.where(later[:, None], rows[quota:], rows[:quota])


def sent(rows, later):
    if lax.axis_size("dp") > 4:
        return circular_tail(rows, later)
    return rows[later.shape[0] :]


def body(q_rows, k_rows, value_slot_rows, counts, doc_ids):
    quota = doc_ids.shape[1]
    rounds = lax.axis_size("ctx") // 4
    rank = lax.axis_index("ctx")
    own_count = counts[0, 0]

    later = quota + jnp.arange(quota, dtype=jnp.int32) < own_count
    k_local, v_local = k_rows[0], value_slot_rows[0]
    kv_tail = jnp.concatenate([sent(k_local, later), sent(v_local, later)], axis=1)
    arrived_kv = shifted(kv_tail, "dp", 1)
    zero = (kv_tail[:1, :1] + kv_tail[:1, -1:]) * 0
    local_kv = jnp.concatenate([k_local[:quota] + zero, v_local[:quota] + zero], axis=1)
    local_kv, zero = lax.optimization_barrier((local_kv, zero))
    q_tails = []
    first = 0
    for size in CHUNKS:
        q_tails.append(sent(q_rows[0, :, head_columns(first, size)], later) + zero)
        first += size
    q_tails = lax.optimization_barrier(q_tails)
    arrived_q = [shifted(tail, "dp", 1) for tail in q_tails]

    shift = shifts_in(own_count, quota)
    own, hot = settle_kv(shift, doc_ids, arrived_kv, local_kv)

    kv_blocks = [own]
    carried, out = own, None
    for back in range(1, rounds + 1):
        carried = shifted(carried, "ctx", 2)
        kv_blocks.append(carried)
        if back < len(CHUNKS):
            first = sum(CHUNKS[: back - 1])
            out = place_queries(hot, arrived_q[back - 1], q_rows, first, out)
            carried, out = lax.optimization_barrier((carried, out))
        if back < rounds:
            kv_blocks.append(across_cores(carried))
    kv_blocks += [across_cores(carried), across_cores(own, (0,))]
    return attend(rank[None], hot, arrived_q[-1], q_rows, kv_blocks, out)


def solution(mesh):
    return jax.shard_map(
        body,
        mesh=mesh,
        in_specs=(
            P("dp", "ctx", None),
            P("dp", "ctx", None),
            P("dp", "ctx", None),
            P("dp", "ctx"),
            P("dp", "ctx"),
        ),
        out_specs=P("dp", "ctx", None),
        check_vma=False,
    )
```
